32 devices in a mesh: dp: 2 (over core), ctx: 16 (over z, y, x).
Axes of the slice: x: 2, y: 2, z: 4, core: 2. Of those that a mesh axis runs over, the one named last changes fastest.
Arguments:
- state_x: bfloat16 [2, 4096, 512], P('dp', 'ctx'), may hold values from -6 to 6
- state_y: bfloat16 [2, 4096, 512], P('dp', 'ctx'), may hold values from -6 to 6
- teacher: bfloat16 [2, 4096, 512], P('dp', 'ctx'), may hold values from -6 to 6
- segment_ids: int32 [2, 4096], P('dp'), may hold values from 0 to 7, never falling along the last dimension, each value on 1 to 2048 neighbouring positions
- valid_mask: int32 [2, 4096], P('dp', 'ctx'), may hold values from 0 to 1, as said below
- w_query: bfloat16 [512, 512], P('dp'), may hold values from -0.25 to 0.25
- w_key: bfloat16 [512, 512], P('dp'), may hold values from -0.25 to 0.25
- w_value: bfloat16 [512, 512], P('dp'), may hold values from -0.25 to 0.25
- w_out: bfloat16 [512, 512], P('dp'), may hold values from -1 to 1
- w_up: bfloat16 [512, 2048], P('dp'), may hold values from -0.25 to 0.25
- w_down: bfloat16 [2048, 512], P('dp'), may hold values from -0.1875 to 0.1875
- gain_attn: bfloat16 [512], P('dp'), may hold values from 0.099609375 to 1.8984375
- gain_ffn: bfloat16 [512], P('dp'), may hold values from 0.099609375 to 1.8984375
- gain_final: bfloat16 [512], P('dp'), may hold values from 0.099609375 to 1.8984375
Outputs:
- loss: float32 [], replicated
- output: bfloat16 [2, 4096, 512], P('dp', 'ctx')
- grad_x: float32 [2, 4096, 512], P('dp', 'ctx')
- grad_y: float32 [2, 4096, 512], P('dp', 'ctx')
- grad_w_query: float32 [512, 512], P(('dp', 'ctx'))
- grad_w_key: float32 [512, 512], P(('dp', 'ctx'))
- grad_w_value: float32 [512, 512], P(('dp', 'ctx'))
- grad_w_out: float32 [512, 512], P(('dp', 'ctx'))
- grad_w_up: float32 [512, 2048], P(('dp', 'ctx'))
- grad_w_down: float32 [2048, 512], P(('dp', 'ctx'))
- grad_gain_attn: float32 [512], P(('dp', 'ctx'))
- grad_gain_ffn: float32 [512], P(('dp', 'ctx'))
- grad_gain_final: float32 [512], P(('dp', 'ctx'))
The draws below stay inside these ranges and needn't reach their ends.
Inputs may be any that keep to these rules, and one draw needn't show every extreme that they name: `segment_ids`: segment numbers never fall along a sequence; each document has 1 to 2048 tokens and every sequence has one of exactly 2048. `valid_mask`: the last token of every sequence is valid.
All inputs are finite; a program needn't handle non-finite values.
Results may differ from the reference program's by a relative error of at most 0.014.
The reference program's roundings to bfloat16 on the way count: a program that leaves them out, or rounds other values in their place, can miss the bound.
Values may be sent and summed in bfloat16 or wider, within the bound.
No kernel may reach another device: no remote copies, remote signals or barrier semaphores. Data moves between devices by JAX's collectives and lax.ppermute only.
A program may use at most 128 MiB of HBM per device.

```python
import math
import jax
import jax.numpy as jnp
import numpy as np
from jax import lax

D = 512
HEADS = 8
FF = 2048
LEN = 4096
NSEQ = 2
DOCS = 8
DOC_MAX = 2048


def draw_valid_mask(key, part):
    ranks = jax.random.randint(key, (NSEQ, LEN), 0, 9 * LEN * (NSEQ - 1))
    positions = jnp.arange(LEN)[None, :]
    sequence = jnp.arange(NSEQ)[:, None]
    limits = (LEN + 2 * positions) * (NSEQ - 1 + 2 * sequence)
    chosen = (ranks < limits) | (positions == LEN - 1)
    return chosen.astype(jnp.int32)


def raised(values, stream_key, source, target, parts, factor):
    owner, partner = [(jnp.arange(values.shape[axis_at]) // (values.shape[axis_at] // parts)).reshape([-1 if axis == axis_at else 1 for axis in range(values.ndim)]) for axis_at in (source, target)]
    chosen = jax.random.permutation(stream_key, parts)[partner]
    strong = (owner == chosen) | (owner == (partner + parts // 2) % parts)
    return jnp.where(strong, factor * values, values)


def block_levels(key, dims, shards, low, largest):
    def one(position, shards_of):
        steps = jax.random.uniform(jax.random.fold_in(jax.random.fold_in(key, 6), position), (shards_of,), jnp.float32, low / len(shards), largest / len(shards))
        return jnp.repeat(jnp.exp(steps), dims[position] // shards_of).reshape((-1,) + (1,) * (len(dims) - position - 1))

    level = one(*shards[0])
    for cut in shards[1:]:
        level = level * one(*cut)
    return level


def profile(amount, total, reach, slope):
    portions = [(1 << 20) // math.isqrt(grade ** slope) + 1 for grade in range(2, amount + 1)]
    surplus, given = total - reach - (amount - 1), [1] * (amount - 1)
    while surplus > 0:
        movable = [i for i in range(amount - 1) if given[i] < reach]
        whole, remaining = sum([portions[i] for i in movable]), surplus
        for i in movable:
            addition = min(reach - given[i], max(1, remaining * portions[i] // whole), surplus)
            given[i] = given[i] + addition
            surplus = surplus - addition
    return np.array([reach] + given)


def uneven(stream_key, number_of, total, reach, skew):
    if number_of == 2:
        one = jax.random.randint(stream_key, (), max(1, total - reach), min(reach, total - 1) + 1)
        return jnp.stack([one, total - one])
    lengths = jnp.asarray(profile(number_of, total, reach, skew), jnp.int32)
    couples = (number_of - 1) // 2
    source_of, taker = lengths[1:1 + 2 * couples:2], lengths[2:2 + 2 * couples:2]
    room = jnp.minimum(source_of - 1, reach - taker)
    moved = jax.random.randint(jax.random.fold_in(stream_key, 1), (couples,), 0, 1 << 20) % (room + 1)
    lengths = lengths.at[1:1 + 2 * couples:2].set(source_of - moved).at[2:2 + 2 * couples:2].set(taker + moved)
    return lengths[jax.random.permutation(jax.random.fold_in(stream_key, 2), number_of)]


def normal_values(stream_key, extent, scale, reach, shards=(), held_as=jnp.bfloat16):
    values = scale * jax.random.normal(stream_key, extent, jnp.float32)
    if shards:
        values = values * block_levels(stream_key, extent, shards, -0.22, 0.18)
    return jnp.clip(values, -reach, reach).astype(held_as)


def noise_with(own_key, dims, scale, reach, cuts, heavy, dtype=jnp.bfloat16):
    drawn = scale * jax.random.normal(own_key, dims, jnp.float32)
    if cuts:
        drawn = drawn * block_levels(own_key, dims, cuts, -0.22, 0.18)
    return jnp.clip(raised(drawn, jax.random.fold_in(own_key, 3), *heavy), -reach, reach).astype(dtype)


def setup_inputs(seed: int = 0) -> dict:
    arg_keys = jax.random.split(jax.random.key(seed), 15)
    state_x = noise_with(arg_keys[0], (NSEQ, LEN, D), 1.0, 6.0, ((0, 2), (1, 16)), (1, 2, 16, 2.0))
    state_y = normal_values(arg_keys[1], (NSEQ, LEN, D), 1.0, 6.0, ((0, 2), (1, 16)))
    teacher = normal_values(arg_keys[2], (NSEQ, LEN, D), 1.0, 6.0, ((0, 2), (1, 16)))
    segment_ids = jax.vmap(lambda own: jnp.searchsorted(jnp.cumsum(uneven(own, DOCS, LEN, DOC_MAX, 2)), jnp.arange(LEN), side="right"))(jax.random.split(arg_keys[3], NSEQ)).reshape((NSEQ, LEN)).astype(jnp.int32)
    valid_mask = draw_valid_mask(jax.random.fold_in(arg_keys[14], 71), 0)
    w_query = normal_values(arg_keys[5], (D, D), D ** -0.5, 0.25, ((0, 2),))
    w_key = normal_values(arg_keys[6], (D, D), D ** -0.5, 0.25, ((0, 2),))
    w_value = normal_values(arg_keys[7], (D, D), D ** -0.5, 0.25, ((0, 2),))
    w_out = normal_values(arg_keys[8], (D, D), (D // 16) ** -0.5, 1.0, ((0, 2),))
    w_up = normal_values(arg_keys[9], (D, FF), D ** -0.5, 0.25, ((0, 2),))
    w_down = normal_values(arg_keys[10], (FF, D), (FF // 2) ** -0.5, 0.1875, ((0, 2),))
    gain_attn = jnp.clip(1.0 + 0.18 * jax.random.normal(arg_keys[11], (D,), jnp.float32), 0.099609375, 1.8984375).astype(jnp.bfloat16)
    gain_ffn = jnp.clip(1.0 + 0.18 * jax.random.normal(arg_keys[12], (D,), jnp.float32), 0.099609375, 1.8984375).astype(jnp.bfloat16)
    gain_final = jnp.clip(1.0 + 0.18 * jax.random.normal(arg_keys[13], (D,), jnp.float32), 0.099609375, 1.8984375).astype(jnp.bfloat16)
    return {"state_x": state_x, "state_y": state_y, "teacher": teacher, "segment_ids": segment_ids, "valid_mask": valid_mask, "w_query": w_query, "w_key": w_key, "w_value": w_value, "w_out": w_out, "w_up": w_up, "w_down": w_down, "gain_attn": gain_attn, "gain_ffn": gain_ffn, "gain_final": gain_final}


@jax.custom_vjp
def low(v):
    return lax.optimization_barrier(v.astype(jnp.bfloat16)).astype(jnp.float32)

@jax.custom_vjp
def low_back(v):
    return v

def low_keep(v):
    return (low(v), None)

def low_pass(kept, grad):
    return (grad,)

def back_keep(v):
    return (v, None)

def back_low(kept, grad):
    return (low(grad),)
low.defvjp(low_keep, low_pass)
low_back.defvjp(back_keep, back_low)
EPSILON = 1e-05
NEGATIVE = -1e+30
HIGH = lax.Precision.HIGHEST

def layer_norm(inputs, gain_row):
    centre = lax.optimization_barrier(jnp.mean(inputs, axis=-1, keepdims=True))
    centred = inputs - centre
    spread = lax.optimization_barrier(jnp.mean(centred * centred, axis=-1, keepdims=True))
    return centred * lax.rsqrt(spread + EPSILON) * gain_row

def product(left, right):
    return jnp.dot(left, right, precision=HIGH, preferred_element_type=jnp.float32)

def attend_sequence(packed):
    queries, keys_all, values_all, segments = packed
    length = queries.shape[0]
    block_rows = math.gcd(length, 512)
    block_count = length // block_rows
    head_size = D // HEADS
    scaling = head_size ** (-0.5)
    key_heads = keys_all.reshape(length, HEADS, head_size)
    value_heads = values_all.reshape(length, HEADS, head_size)

    @jax.checkpoint
    def one_block(block_item):
        query_block, first_row = block_item
        query_heads = query_block.reshape(block_rows, HEADS, head_size)
        scores = jnp.einsum('qhd,khd->hqk', query_heads, key_heads, precision=HIGH) * scaling
        scores = low_back(scores)
        query_seg = lax.dynamic_slice_in_dim(segments, first_row, block_rows)
        allowed = query_seg[:, None] == segments[None, :]
        scores = jnp.where(allowed[None], scores, NEGATIVE)
        highest = lax.optimization_barrier(jnp.max(scores, axis=-1, keepdims=True))
        weights = jnp.where(allowed[None], jnp.exp(scores - highest), 0.0)
        weights = low(weights / lax.optimization_barrier(jnp.sum(weights, axis=-1, keepdims=True)))
        mixed_part = jnp.einsum('hqk,khd->qhd', weights, value_heads, precision=HIGH)
        return mixed_part.reshape(block_rows, D)
    starts = (jnp.arange(block_count) * block_rows).astype(jnp.int32)
    outputs = lax.map(one_block, (queries.reshape(block_count, block_rows, D), starts))
    return outputs.reshape(length, D)

def forward(inputs_x, inputs_y, query_w, key_w, value_w, out_w, up_w, down_w, gain_one, gain_two, gain_three, segment_ids, target, mask_rows):
    queries = low_back(low(product(inputs_x, query_w)))
    keys_all = low_back(low(product(inputs_x, key_w)))
    values_all = low_back(low(product(inputs_x, value_w)))
    attended = lax.map(attend_sequence, (queries, keys_all, values_all, segment_ids))
    attended = low_back(low(attended))
    branch_a = low_back(product(attended, out_w))
    normed_one = layer_norm(inputs_x + branch_a, gain_one)
    hidden_pre = low_back(product(low(normed_one), up_w))
    hidden = low(jax.nn.gelu(hidden_pre, approximate=True))
    branch_f = low_back(product(hidden, down_w))
    normed_two = layer_norm(normed_one + branch_f, gain_two)
    carried = inputs_y + branch_a + branch_f
    result = normed_two + layer_norm(carried, gain_three)
    differ = result - target
    loss_value = jnp.sum(mask_rows * lax.optimization_barrier(jnp.sum(differ * differ, axis=-1))) / jnp.sum(mask_rows)
    return (loss_value, result)

def reference(state_x, state_y, teacher, segment_ids, valid_mask, w_query, w_key, w_value, w_out, w_up, w_down, gain_attn, gain_ffn, gain_final):
    floats = [array.astype(jnp.float32) for array in (state_x, state_y, w_query, w_key, w_value, w_out, w_up, w_down, gain_attn, gain_ffn, gain_final)]
    target = teacher.astype(jnp.float32)
    mask_rows = valid_mask.astype(jnp.float32)

    def loss_of(inputs_x, inputs_y, query_w, key_w, value_w, out_w, up_w, down_w, gain_one, gain_two, gain_three):
        return forward(inputs_x, inputs_y, query_w, key_w, value_w, out_w, up_w, down_w, gain_one, gain_two, gain_three, segment_ids, target, mask_rows)
    loss_value, pullback, result = jax.vjp(loss_of, *floats, has_aux=True)
    grads = pullback(jnp.ones((), jnp.float32))
    return (loss_value, result.astype(jnp.bfloat16), grads[0], grads[1], grads[2], grads[3], grads[4], grads[5], grads[6], grads[7], grads[8], grads[9], grads[10])
```

```python
import functools

import jax
import jax.numpy as jnp
from jax import lax
from jax.experimental import pallas as pl
from jax.experimental.pallas import tpu as pltpu
from jax.sharding import PartitionSpec as P

HEADS = 8
EPS = 1e-05
SLOTS = 32
FAR = -(2.0**100)
CORE = 0.7978845608028654
CUBE = 0.044715
MIB = 1024 * 1024

BF16 = jnp.bfloat16
F32 = jnp.float32


def dot(left, right):
    return jnp.dot(left, right, preferred_element_type=F32)


def dot_t(left, right):
    return lax.dot_general(left, right, (((1,), (1,)), ((), ())), preferred_element_type=F32)


def vmem(count):
    return [pl.BlockSpec(memory_space=pltpu.VMEM) for _ in range(count)]


def smem():
    return pl.BlockSpec(memory_space=pltpu.SMEM)


def shaped(shape, dtype):
    return jax.ShapeDtypeStruct(shape, dtype)


def swap(block, axis, bit):
    size = lax.axis_size(axis)
    return lax.ppermute(block, axis, [(i, i ^ bit) for i in range(size)])


def project_kernel(x_ref, wq_ref, wk_ref, wv_ref, q_ref, kv_ref):
    x = x_ref[...]
    size = q_ref.shape[1]
    for w_ref, out_ref, base, scale in (
        (wk_ref, kv_ref, 0, 1.0),
        (wv_ref, kv_ref, size, 1.0),
        (wq_ref, q_ref, 0, size**-0.5),
    ):
        flat = dot(x, w_ref[...]) * scale
        turned = flat.astype(BF16).T
        for h in range(HEADS):
            out_ref[h, base : base + size, :] = turned[h * size : (h + 1) * size, :]


def project(x, wq, wk, wv):
    tok, feat = x.shape
    size = feat // HEADS
    return pl.pallas_call(
        project_kernel,
        out_shape=(
            shaped((HEADS, size, tok), BF16),
            shaped((HEADS, 2 * size, tok), BF16),
        ),
        in_specs=vmem(4),
        out_specs=tuple(vmem(2)),
        compiler_params=pltpu.CompilerParams(vmem_limit_bytes=24 * MIB),
        name="project",
    )(x, wq, wk, wv)


def onehot(row, hit, miss):
    number = lax.broadcasted_iota(jnp.int32, (SLOTS, row.shape[1]), 0)
    return jnp.where(number == row, hit, miss).astype(BF16)


def key_range(seg_s, chunk, count, tok):
    first = seg_s[chunk * tok]
    last = seg_s[chunk * tok + tok - 1]
    low = jnp.int32(0)
    high = jnp.int32(0)
    for c in range(count):
        low += (seg_s[c * tok + tok - 1] < first).astype(jnp.int32)
        high += (seg_s[c * tok] <= last).astype(jnp.int32)
    return low // 2, (high + 1) // 2


def place(h, slot, ways, rank, tok):
    chunk = h * ways + lax.rem(rank - slot + ways, ways)
    return chunk, chunk // 2, pl.multiple_of(lax.rem(chunk, 2) * tok, tok)


def forward_kernel(ways, ids_ref, seg_s, seg_ref, q_ref, *refs):
    kv_refs = refs[:ways]
    o_ref, of_ref, lse_ref, kx, vt = refs[ways:]
    count, tok = seg_ref.shape
    size = q_ref.shape[1]
    rank = lax.rem(ids_ref[1], ways)
    for slot in range(ways):

        @pl.loop(0, HEADS)
        def fill(h):
            chunk, pair, start = place(h, slot, ways, rank, tok)
            row = seg_ref[pl.ds(chunk, 1), :]
            wide = jnp.concatenate(
                [kv_refs[slot][h, 0:size, :], onehot(row, 1.0, 0.0)], axis=0
            )
            kx[pair, pl.ds(start, tok), :] = wide.T
            vt[pair, :, pl.ds(start, tok)] = kv_refs[slot][h, size : 2 * size, :]

    @pl.loop(0, HEADS)
    def one(i):
        chunk = i * ways + rank
        low, high = key_range(seg_s, chunk, count, tok)
        row = seg_ref[pl.ds(chunk, 1), :]
        qx = jnp.concatenate([q_ref[i], onehot(row, 0.0, FAR)], axis=0)

        def step(p, carry):
            top, total, acc = carry
            s = dot(kx[p], qx)
            new = jnp.maximum(top, jnp.max(s, axis=0, keepdims=True))
            fade = jnp.exp(top - new)
            w = jnp.exp(s - new)
            total = total * fade + jnp.sum(w, axis=0, keepdims=True)
            acc = acc * fade + dot(vt[p], w.astype(BF16))
            return new, total, acc

        top, total, acc = lax.fori_loop(
            low,
            high,
            step,
            (
                jnp.full((1, tok), -3e38, F32),
                jnp.zeros((1, tok), F32),
                jnp.zeros((size, tok), F32),
            ),
        )
        out = acc / total
        of_ref[i] = out
        o_ref[i] = out.astype(BF16)
        lse_ref[pl.ds(i, 1), :] = top + jnp.log(total)


def attend(ids, seg, seg2, q, kvs):
    ways = len(kvs)
    _, size, tok = q.shape
    count = seg2.shape[0]
    return pl.pallas_call(
        functools.partial(forward_kernel, ways),
        out_shape=(
            shaped((HEADS, size, tok), BF16),
            shaped((HEADS, size, tok), F32),
            shaped((HEADS, tok), F32),
        ),
        in_specs=[smem(), smem()] + vmem(2 + ways),
        out_specs=tuple(vmem(3)),
        scratch_shapes=[
            pltpu.VMEM((count // 2, 2 * tok, size + SLOTS), BF16),
            pltpu.VMEM((count // 2, size, 2 * tok), BF16),
        ],
        compiler_params=pltpu.CompilerParams(vmem_limit_bytes=32 * MIB),
        name="attend",
    )(ids, seg, seg2, q, *kvs)


def backward_kernel(ways, ids_ref, seg_s, seg_ref, q_ref, do_ref, of_ref, lse_ref, *refs):
    kv_refs = refs[:ways]
    dq_ref = refs[ways]
    dkv_refs = refs[ways + 1 : 2 * ways + 1]
    kx, vx, kt, dk, dv = refs[2 * ways + 1 :]
    count, tok = seg_ref.shape
    size = q_ref.shape[1]
    rank = lax.rem(ids_ref[1], ways)
    for slot in range(ways):

        @pl.loop(0, HEADS)
        def fill(h):
            chunk, pair, start = place(h, slot, ways, rank, tok)
            row = seg_ref[pl.ds(chunk, 1), :]
            keys = kv_refs[slot][h, 0:size, :]
            kx[pair, pl.ds(start, tok), :] = jnp.concatenate(
                [keys, onehot(row, 1.0, 0.0)], axis=0
            ).T
            kt[pair, :, pl.ds(start, tok)] = keys
            vx[pair, pl.ds(start, tok), :] = kv_refs[slot][h, size : 2 * size, :].T

    dk[...] = jnp.zeros_like(dk)
    dv[...] = jnp.zeros_like(dv)

    @pl.loop(0, HEADS)
    def one(i):
        chunk = i * ways + rank
        low, high = key_range(seg_s, chunk, count, tok)
        row = seg_ref[pl.ds(chunk, 1), :]
        q = q_ref[i]
        qx = jnp.concatenate([q, onehot(row, 0.0, FAR)], axis=0)
        do = do_ref[i]
        delta = jnp.sum(do.astype(F32) * of_ref[i], axis=0, keepdims=True)
        lse = lse_ref[pl.ds(i, 1), :]

        def step(p, dq):
            w = jnp.exp(dot(kx[p], qx) - lse)
            dp = dot(vx[p], do)
            ds = (w * (dp - delta)).astype(BF16)
            dv[p] += dot_t(do, w.astype(BF16))
            dk[p] += dot_t(q, ds)
            return dq + dot(kt[p], ds)

        dq = lax.fori_loop(low, high, step, jnp.zeros((size, tok), F32))
        dq_ref[i] = (dq * size**-0.5).astype(BF16)

    for slot in range(ways):

        @pl.loop(0, HEADS)
        def drain(h):
            _, pair, start = place(h, slot, ways, rank, tok)
            out = dkv_refs[slot]
            out[h, 0:size, :] = dk[pair, :, pl.ds(start, tok)].astype(out.dtype)
            out[h, size : 2 * size, :] = dv[pair, :, pl.ds(start, tok)].astype(out.dtype)


def attend_back(ids, seg, seg2, q, do, of, lse, kvs):
    ways = len(kvs)
    _, size, tok = q.shape
    count = seg2.shape[0]
    return pl.pallas_call(
        functools.partial(backward_kernel, ways),
        out_shape=(shaped((HEADS, size, tok), BF16), shaped((HEADS, 2 * size, tok), F32))
        + (shaped((HEADS, 2 * size, tok), BF16),) * (ways - 1),
        in_specs=[smem(), smem()] + vmem(5 + ways),
        out_specs=tuple(vmem(1 + ways)),
        scratch_shapes=[
            pltpu.VMEM((count // 2, 2 * tok, size + SLOTS), BF16),
            pltpu.VMEM((count // 2, 2 * tok, size), BF16),
            pltpu.VMEM((count // 2, size, 2 * tok), BF16),
            pltpu.VMEM((count // 2, size, 2 * tok), F32),
            pltpu.VMEM((count // 2, size, 2 * tok), F32),
        ],
        compiler_params=pltpu.CompilerParams(vmem_limit_bytes=40 * MIB),
        name="attend_back",
    )(ids, seg, seg2, q, do, of, lse, *kvs)


def normed(rows):
    centred = rows - jnp.mean(rows, axis=-1, keepdims=True)
    spread = jnp.mean(centred * centred, axis=-1, keepdims=True)
    inverse = lax.rsqrt(spread + EPS)
    return centred * inverse, inverse


def norm_back(n, inverse, gain, up):
    scaled = up * gain
    mean_one = jnp.mean(scaled, axis=-1, keepdims=True)
    mean_two = jnp.mean(scaled * n, axis=-1, keepdims=True)
    grad = inverse * (scaled - mean_one - n * mean_two)
    return grad, jnp.sum(up * n, axis=0, keepdims=True)


def middle_kernel(
    tile,
    ot_ref,
    x_ref,
    y_ref,
    t_ref,
    mask_ref,
    gains_ref,
    wo_ref,
    wu_ref,
    wd_ref,
    out_ref,
    gy_ref,
    gr_ref,
    dot_ref,
    x1_ref,
    h_ref,
    df_ref,
    dz_ref,
    da_ref,
    small_ref,
    slope,
    acc,
):
    rows, feat = x_ref.shape
    steps = wu_ref.shape[1] // tile
    gains = gains_ref[...].astype(F32)
    g1, g2, g3 = gains[0:1], gains[1:2], gains[2:3]
    branch = dot(ot_ref[...].T, wo_ref[...])
    n1, r1 = normed(x_ref[...].astype(F32) + branch)
    x1 = n1 * g1
    x1_ref[...] = x1.astype(BF16)
    acc[...] = jnp.zeros_like(acc)

    @pl.loop(0, steps)
    def up(t):
        cols = pl.ds(pl.multiple_of(t * tile, tile), tile)
        z = dot(x1_ref[...], wu_ref[:, cols])
        z2 = z * z
        th = jnp.tanh(CORE * z * (1.0 + CUBE * z2))
        half = 0.5 * (1.0 + th)
        h = (z * half).astype(BF16)
        slope[:, cols] = half + 0.5 * z * (1.0 - th * th) * (CORE * (1.0 + 3.0 * CUBE * z2))
        h_ref[:, cols] = h
        acc[...] += dot(h, wd_ref[cols, :])

    ffn = acc[...]
    n2, r2 = normed(x1 + ffn)
    n3, r3 = normed(y_ref[...].astype(F32) + branch + ffn)
    result = n2 * g2 + n3 * g3
    out_ref[...] = result.astype(BF16)
    mask_row = mask_ref[...].astype(F32)
    mask = jnp.broadcast_to(mask_row, (8, rows)).T[:, 0:1]
    differ = result - t_ref[...].astype(F32)
    error = jnp.sum(mask * differ * differ)
    valid = jnp.sum(mask_row)
    upstream = 2.0 * mask * differ
    gy, dg3 = norm_back(n3, r3, g3, upstream)
    du, dg2 = norm_back(n2, r2, g2, upstream)
    gy_ref[...] = gy
    df_ref[...] = (du + gy).astype(BF16)
    acc[...] = du

    @pl.loop(0, steps)
    def down(t):
        cols = pl.ds(pl.multiple_of(t * tile, tile), tile)
        dz = (dot_t(df_ref[...], wd_ref[cols, :]) * slope[:, cols]).astype(BF16)
        dz_ref[:, cols] = dz
        acc[...] += dot_t(dz, wu_ref[:, cols])

    gr, dg1 = norm_back(n1, r1, g1, acc[...])
    gr_ref[...] = gr
    da = (gr + gy).astype(BF16)
    da_ref[...] = da
    dot_ref[...] = dot_t(wo_ref[...], da).astype(BF16)
    lane = lax.broadcasted_iota(jnp.int32, (1, feat), 1)
    scalars = jnp.where(lane == 0, error, jnp.where(lane == 1, valid, 0.0))
    small_ref[...] = jnp.concatenate(
        [dg1, dg2, dg3, scalars, jnp.zeros((4, feat), F32)], axis=0
    )


def middle(ot, x, y, teacher, mask, gains, wo, wu, wd):
    tok, feat = x.shape
    wide = wu.shape[1]
    return pl.pallas_call(
        functools.partial(middle_kernel, min(512, wide)),
        out_shape=(
            shaped((tok, feat), BF16),
            shaped((tok, feat), F32),
            shaped((tok, feat), F32),
            shaped((feat, tok), BF16),
            shaped((tok, feat), BF16),
            shaped((tok, wide), BF16),
            shaped((tok, feat), BF16),
            shaped((tok, wide), BF16),
            shaped((tok, feat), BF16),
            shaped((8, feat), F32),
        ),
        in_specs=vmem(9),
        out_specs=tuple(vmem(10)),
        scratch_shapes=[pltpu.VMEM((tok, wide), F32), pltpu.VMEM((tok, feat), F32)],
        compiler_params=pltpu.CompilerParams(vmem_limit_bytes=40 * MIB),
        name="middle",
    )(ot, x, y, teacher, mask, gains, wo, wu, wd)


def split_sum(values):
    high = values.astype(BF16)
    low = (values - high.astype(F32)).astype(BF16)
    return jnp.concatenate([high.astype(F32), low.astype(F32)], axis=0).astype(BF16)


def ffn_grad_kernel(
    tile, ids_ref, x1_ref, h_ref, df_ref, dz_ref, ot_ref, da_ref, small_ref, keep_ref, send_ref, xt
):
    feat = x1_ref.shape[1]
    wide = h_ref.shape[1]
    blocks = keep_ref.shape[0]
    half, wide_half = feat // 2, wide // 2
    step = half // blocks
    wide_step = wide_half // blocks
    parts = wide // feat
    xt[...] = x1_ref[...].T
    small = split_sum(small_ref[...])
    for flip, ref in ((1, send_ref), (0, keep_ref)):
        side = ids_ref[0] if flip == 0 else 1 - ids_ref[0]
        rows = pl.ds(pl.multiple_of(side * half, half), half)
        for j in range(parts):
            g = dot(xt[rows, :], dz_ref[:, j * feat : (j + 1) * feat])
            ref[:, j * step : (j + 1) * step, :] = g.astype(BF16).reshape(blocks, step, feat)
        base = parts * step
        each = tile // wide_step
        for j in range(wide_half // tile):
            cols = pl.ds(pl.multiple_of(side * wide_half + j * tile, tile), tile)
            g = dot(h_ref[:, cols].T, df_ref[...])
            ref[j * each : (j + 1) * each, base : base + wide_step, :] = g.astype(
                BF16
            ).reshape(each, wide_step, feat)
        base += wide_step
        g = dot(ot_ref[rows, :], da_ref[...])
        ref[:, base : base + step, :] = g.astype(BF16).reshape(blocks, step, feat)
        base += step
        ref[:, base : base + 16, :] = jnp.broadcast_to(small[None], (blocks, 16, feat))


def ffn_grads(ids, blocks, x1, h, df, dz, ot, da, small):
    tok, feat = x1.shape
    wide = h.shape[1]
    step = feat // (2 * blocks)
    depth = (wide // feat) * step + wide // (2 * blocks) + step + 16
    return pl.pallas_call(
        functools.partial(ffn_grad_kernel, min(512, wide // 2)),
        out_shape=(shaped((blocks, depth, feat), BF16),) * 2,
        in_specs=[smem()] + vmem(7),
        out_specs=tuple(vmem(2)),
        scratch_shapes=[pltpu.VMEM((feat, tok), BF16)],
        compiler_params=pltpu.CompilerParams(vmem_limit_bytes=32 * MIB),
        name="ffn_grads",
    )(ids, x1, h, df, dz, ot, da, small)


def added(one, two):
    depth = one.shape[0]
    main = one[: depth - 16].astype(F32) + two[: depth - 16].astype(F32)
    tail = one[depth - 16 :].astype(F32) + two[depth - 16 :].astype(F32)
    return main, tail[0:8] + tail[8:16]


def halve_kernel(bit, ids_ref, keep_ref, got_ref, next_ref, send_ref):
    mine = lax.rem(ids_ref[1] // bit, 2)
    depth = keep_ref.shape[1]

    @pl.loop(0, next_ref.shape[0])
    def one(b):
        for ref, which in ((send_ref, 1 - mine), (next_ref, mine)):
            at = 2 * b + which
            main, tail = added(keep_ref[at], got_ref[at])
            ref[b, 0 : depth - 16, :] = main.astype(BF16)
            ref[b, depth - 16 : depth, :] = split_sum(tail)


def halve(ids, bit, keep, got):
    blocks, depth, feat = keep.shape
    return pl.pallas_call(
        functools.partial(halve_kernel, bit),
        out_shape=(shaped((blocks // 2, depth, feat), BF16),) * 2,
        in_specs=[smem()] + vmem(2),
        out_specs=tuple(vmem(2)),
        compiler_params=pltpu.CompilerParams(vmem_limit_bytes=24 * MIB),
        name="halve",
    )(ids, keep, got)


def last_kernel(
    ids_ref, back_ref, x_ref, gr_ref, wq_ref, wk_ref, wv_ref, gx_ref, keep_ref, send_ref, xt
):
    feat = x_ref.shape[1]
    blocks = keep_ref.shape[0]
    half = feat // 2
    step = half // blocks
    size = back_ref.shape[1] // 3
    xt[...] = x_ref[...].T
    total = gr_ref[...]
    for j, w_ref in enumerate((wq_ref, wk_ref, wv_ref)):
        grad_t = jnp.concatenate(
            [back_ref[h, j * size : (j + 1) * size, :] for h in range(HEADS)], axis=0
        )
        total = total + dot_t(grad_t.T, w_ref[...])
        for flip, ref in ((1, send_ref), (0, keep_ref)):
            side = ids_ref[0] if flip == 0 else 1 - ids_ref[0]
            rows = pl.ds(pl.multiple_of(side * half, half), half)
            g = dot_t(xt[rows, :], grad_t)
            ref[:, j * step : (j + 1) * step, :] = g.astype(BF16).reshape(blocks, step, feat)
    gx_ref[...] = total


def last(ids, blocks, back, x, gr, wq, wk, wv):
    tok, feat = x.shape
    step = feat // (2 * blocks)
    return pl.pallas_call(
        last_kernel,
        out_shape=(shaped((tok, feat), F32),) + (shaped((blocks, 3 * step, feat), BF16),) * 2,
        in_specs=[smem()] + vmem(6),
        out_specs=tuple(vmem(3)),
        scratch_shapes=[pltpu.VMEM((feat, tok), BF16)],
        compiler_params=pltpu.CompilerParams(vmem_limit_bytes=24 * MIB),
        name="last",
    )(ids, back, x, gr, wq, wk, wv)


def finish_kernel(
    ids_ref,
    keep_ref,
    got_ref,
    pieces_ref,
    gx_in,
    gy_in,
    loss_ref,
    gx_ref,
    gy_ref,
    gq_ref,
    gk_ref,
    gv_ref,
    go_ref,
    gu_ref,
    gd_ref,
    g1_ref,
    g2_ref,
    g3_ref,
):
    step, feat = gq_ref.shape
    wide_step = gd_ref.shape[0]
    parts = gu_ref.shape[1] // feat
    main, small = added(keep_ref[0], got_ref[0])
    inverse = 1.0 / small[3:4, 1:2]
    loss_ref[...] = small[3:4, 0:1] * inverse
    gx_ref[...] = gx_in[...] * inverse
    gy_ref[...] = gy_in[...] * inverse
    main = main * inverse
    for j in range(parts):
        gu_ref[:, j * feat : (j + 1) * feat] = main[j * step : (j + 1) * step]
    base = parts * step
    gd_ref[...] = main[base : base + wide_step]
    base += wide_step
    go_ref[...] = main[base : base + step]
    summed = jnp.sum(pieces_ref[...].astype(F32), axis=0) * inverse
    gq_ref[...] = summed[0:step]
    gk_ref[...] = summed[step : 2 * step]
    gv_ref[...] = summed[2 * step : 3 * step]
    number = ids_ref[0] * pieces_ref.shape[0] + ids_ref[1]
    turned = pltpu.roll(small * inverse, lax.rem(feat - number * step, feat), 1)
    g1_ref[...] = turned[0:1, 0:step]
    g2_ref[...] = turned[1:2, 0:step]
    g3_ref[...] = turned[2:3, 0:step]


def finish(ids, keep, got, pieces, gx, gy, wide):
    tok, feat = gx.shape
    blocks = pieces.shape[0]
    step = feat // (2 * blocks)
    return pl.pallas_call(
        finish_kernel,
        out_shape=(
            shaped((1, 1), F32),
            shaped((tok, feat), F32),
            shaped((tok, feat), F32),
            shaped((step, feat), F32),
            shaped((step, feat), F32),
            shaped((step, feat), F32),
            shaped((step, feat), F32),
            shaped((step, wide), F32),
            shaped((wide // (2 * blocks), feat), F32),
            shaped((1, step), F32),
            shaped((1, step), F32),
            shaped((1, step), F32),
        ),
        in_specs=[smem()] + vmem(5),
        out_specs=tuple(vmem(12)),
        compiler_params=pltpu.CompilerParams(vmem_limit_bytes=24 * MIB),
        name="finish",
    )(ids, keep, got, pieces, gx, gy)


def body(
    state_x,
    state_y,
    teacher,
    segment_ids,
    valid_mask,
    w_query,
    w_key,
    w_value,
    w_out,
    w_up,
    w_down,
    gain_attn,
    gain_ffn,
    gain_final,
):
    _, tok, feat = state_x.shape
    size = feat // HEADS
    ctx = lax.axis_size("ctx")
    sides = lax.axis_size("dp")
    ways = ctx // HEADS
    groups = [[h * ways + r for h in range(HEADS)] for r in range(ways)]
    ids = jnp.stack([lax.axis_index("dp"), lax.axis_index("ctx")]).astype(jnp.int32)
    seg = segment_ids.reshape(-1)
    seg2 = segment_ids.reshape(ctx, tok)
    x = state_x[0]

    def gathered(block):
        return lax.all_gather(block, "dp", axis=0, tiled=True)

    def exchange(block):
        return lax.all_to_all(block, "ctx", 0, 0, axis_index_groups=groups, tiled=True)

    def around(block, distance):
        route = []
        for g in range(HEADS):
            for r in range(ways):
                route.append((g * ways + r, g * ways + (r + distance) % ways))
        return lax.ppermute(block, "ctx", route)

    wq, wk, wv = gathered(w_query), gathered(w_key), gathered(w_value)
    q, kv = project(x, wq, wk, wv)
    kv = exchange(kv)
    kvs = [kv] + [around(kv, j) for j in range(1, ways)]
    q = exchange(q)
    o, of, lse = attend(ids, seg, seg2, q, kvs)
    wo, wu, wd = gathered(w_out), gathered(w_up), gathered(w_down)
    gains = lax.all_gather(
        jnp.stack([gain_attn, gain_ffn, gain_final]), "dp", axis=1, tiled=True
    )
    ot = exchange(o).reshape(feat, tok)
    result, gy, gr, do, x1, h, df, dz, da, small = middle(
        ot, x, state_y[0], teacher[0], valid_mask, gains, wo, wu, wd
    )
    do = exchange(do.reshape(HEADS, size, tok))
    fast = sides == 2 and (feat // (sides * ctx)) % 16 == 0
    if fast:
        keep, send = ffn_grads(ids, ctx, x1, h, df, dz, ot, da, small)
        got = swap(send, "dp", 1)
        bit = 1
        while bit < ctx:
            keep, send = halve(ids, bit, keep, got)
            got = swap(send, "ctx", bit)
            bit *= 2
    dq, own, *others = attend_back(ids, seg, seg2, q, do, of, lse, kvs)
    for j, other in enumerate(others):
        own = own + around(other, -(j + 1)).astype(F32)
    back = exchange(jnp.concatenate([dq, own.astype(BF16)], axis=1))
    wide = wu.shape[1]
    if fast:
        gx, mine, sent = last(ids, ctx, back, x, gr, wq, wk, wv)
        pieces = mine + swap(sent, "dp", 1)
        pieces = lax.all_to_all(pieces, "ctx", 0, 0, tiled=True)
        loss, gx, gy, gq, gk, gv, go, gu, gd, g1, g2, g3 = finish(
            ids, keep, got, pieces, gx, gy, wide
        )
        gains_out = [g.reshape(-1) for g in (g1, g2, g3)]
        loss = loss.reshape(())
    else:
        both = ("dp", "ctx")
        total = lax.psum(small, both)
        inverse = 1.0 / total[3, 1]
        loss = total[3, 0] * inverse

        def scattered(block):
            block = block * inverse
            return lax.psum_scatter(block, both, scatter_dimension=0, tiled=True)

        parts = [back[:, j * size : (j + 1) * size, :].reshape(feat, tok) for j in range(3)]
        gx = gr
        for part, weight in zip(parts, (wq, wk, wv)):
            gx = gx + dot_t(part.T, weight)
        gq, gk, gv = [scattered(dot_t(x.T, part)) for part in parts]
        go = scattered(dot(ot, da))
        gu = scattered(dot(x1.T, dz))
        gd = scattered(dot(h.T, df))
        gx, gy = gx * inverse, gy * inverse
        step = feat // (sides * ctx)
        number = ids[0] * ctx + ids[1]
        gains_out = [
            lax.dynamic_slice_in_dim(total[k] * inverse, number * step, step)
            for k in range(3)
        ]
    return (
        loss,
        result[None],
        gx[None],
        gy[None],
        gq,
        gk,
        gv,
        go,
        gu,
        gd,
        gains_out[0],
        gains_out[1],
        gains_out[2],
    )


def solution(mesh):
    tokens = P("dp", "ctx", None)
    rows = P("dp", None)
    spread = P(("dp", "ctx"), None)
    gain = P(("dp", "ctx"))
    return jax.shard_map(
        body,
        mesh=mesh,
        in_specs=(tokens,) * 3 + (rows, P("dp", "ctx")) + (rows,) * 6 + (P("dp"),) * 3,
        out_specs=(P(), tokens, tokens, tokens) + (spread,) * 6 + (gain,) * 3,
        check_vma=False,
    )
```

```python
import functools

import jax
import jax.numpy as jnp
from jax import lax
from jax.experimental import pallas as pl
from jax.experimental.pallas import tpu as pltpu
from jax.sharding import PartitionSpec as P

HEADS = 8
EPS = 1e-05
LANES = 32
DOCS = 24
UNROLL = 4
INNER = (0, 1, 3, 2)
RING = (0, 2, 4, 6, 7, 5, 3, 1)
GROUP = 8
LOG2E = 1.4426950408889634
FAR = -(2.0**100)
CORE = 0.7978845608028654
CUBE = 0.044715
MIB = 1024 * 1024

BF16 = jnp.bfloat16
F32 = jnp.float32


def dot(left, right):
    return jnp.dot(left, right, preferred_element_type=F32)


def dot_t(left, right):
    return lax.dot_general(left, right, (((1,), (1,)), ((), ())), preferred_element_type=F32)


def vmem(count):
    return [pl.BlockSpec(memory_space=pltpu.VMEM) for _ in range(count)]


def hbm(count):
    return [pl.BlockSpec(memory_space=pltpu.HBM) for _ in range(count)]


def smem():
    return pl.BlockSpec(memory_space=pltpu.SMEM)


def kept(shape, dtype):
    return pltpu.VMEM(shape, dtype)


def near(array):
    return pltpu.with_memory_space_constraint(array, pltpu.VMEM)


def apart(shape, dtype):
    return pltpu.HBM(shape, dtype)


def far(array):
    return pltpu.with_memory_space_constraint(array, pltpu.HBM)


def shaped(shape, dtype):
    return jax.ShapeDtypeStruct(shape, dtype)


def cost(us):
    return pl.CostEstimate(flops=int(us * 1.1e9), bytes_accessed=1024, transcendentals=0)


def swap(block, axis, bit):
    size = lax.axis_size(axis)
    return lax.ppermute(block, axis, [(i, i ^ bit) for i in range(size)])


def rows_of(ids_ref, blocks, number, total):
    size = total // blocks
    if blocks == 1:
        return pl.ds(0, size)
    return pl.ds(pl.multiple_of((ids_ref[0] + number) % 2 * size, size), size)


def fetch(sources, targets, sems):
    copies = [
        pltpu.make_async_copy(source, target, sems.at[k])
        for k, (source, target) in enumerate(zip(sources, targets))
    ]
    for copy in copies:
        copy.start()
    return copies


def project_kernel(blocks, ids_ref, x_ref, *refs):
    out_ref, held, sems = refs[3 * blocks :]
    feat = x_ref.shape[1]
    size = feat // HEADS
    each = feat // blocks
    targets = [
        held.at[part, pl.ds(j * each, each), :] for part in range(3) for j in range(blocks)
    ]
    copies = fetch(refs[: 3 * blocks], targets, sems)
    x = jnp.concatenate(
        [x_ref[:, rows_of(ids_ref, blocks, j, feat)] for j in range(blocks)], axis=1
    )
    for part, scale in ((0, size**-0.5), (1, 1.0), (2, 1.0)):
        for copy in copies[part * blocks : (part + 1) * blocks]:
            copy.wait()
        turned = (dot(x, held[part]) * scale).astype(BF16).T
        for h in range(HEADS):
            out_ref[h, part * size : (part + 1) * size, :] = turned[h * size : (h + 1) * size, :]


def project(ids, x, weights):
    tok, feat = x.shape
    flat = [block for weight in weights for block in weight]
    return pl.pallas_call(
        functools.partial(project_kernel, len(weights[0])),
        out_shape=shaped((HEADS, 3 * feat // HEADS, tok), BF16),
        in_specs=[smem()] + vmem(1) + hbm(len(flat)),
        out_specs=vmem(1)[0],
        scratch_shapes=[
            pltpu.VMEM((3, feat, feat), BF16),
            pltpu.SemaphoreType.DMA((len(flat),)),
        ],
        compiler_params=pltpu.CompilerParams(vmem_limit_bytes=12 * MIB),
        cost_estimate=cost(1.4),
        name="project",
    )(ids, x, *map(far, flat))


def mask_rows(row, hit, miss, extra):
    number = lax.broadcasted_iota(jnp.int32, (LANES, row.shape[1]), 0)
    base = jnp.where(number == row, hit, miss)
    base = jnp.where(number < DOCS, base, 0.0)
    for k, value in enumerate(extra):
        base = jnp.where(number == DOCS + k, value, base)
    return base.astype(BF16)


def parts_of(value, count):
    found = []
    for _ in range(count):
        part = value.astype(BF16).astype(F32)
        found.append(part)
        value = value - part
    return found


def query_rows(q, row, extra):
    wide = q.astype(F32) * LOG2E
    high, low = parts_of(wide, 2)
    return jnp.concatenate(
        [high.astype(BF16), low.astype(BF16), mask_rows(row, 0.0, FAR, extra)], axis=0
    ).T


def key_rows(k, row):
    return jnp.concatenate([k, k, mask_rows(row, 1.0, 0.0, (1.0, 1.0, 1.0))], axis=0)


def list_size(count):
    return HEADS * count + 2 * GROUP


def plan_kernel(ways, count, tok, ids_ref, *refs):
    out_ref = refs[-1]
    rank = ids_ref[2]
    length = list_size(count)

    def number(at):
        if len(refs) == 2:
            return refs[0][at]
        return jnp.where(ids_ref[3] == 0, refs[0][at], refs[1][at])

    firsts = [number(c * tok) for c in range(count)]
    lasts = [number(c * tok + tok - 1) for c in range(count)]

    def one(i, found):
        chunk = i * ways + rank
        first = number(chunk * tok)
        last = number(chunk * tok + tok - 1)
        low = sum((value < first).astype(jnp.int32) for value in lasts)
        high = sum((value <= last).astype(jnp.int32) for value in firsts)

        def other(c, found):
            own = (lax.rem(c, ways) == rank).astype(jnp.int32)
            every, mine, rest = found
            out_ref[every] = i
            out_ref[length + every] = c
            at = jnp.where(own == 1, 2 * length + mine, 4 * length + rest)
            out_ref[at] = i
            out_ref[at + length] = c
            return every + 1, mine + own, rest + 1 - own

        return lax.fori_loop(low, high, other, found)

    found = lax.fori_loop(0, HEADS, one, (jnp.int32(0),) * 3)
    for k, ended in enumerate(found):
        for g in range(GROUP):
            out_ref[2 * k * length + ended + g] = HEADS
            out_ref[(2 * k + 1) * length + ended + g] = 0
        out_ref[6 * length + k] = (ended + GROUP - 1) // GROUP


def plan_of(ids, segs, ways, count, tok):
    size = 6 * list_size(count) + 8
    return pl.pallas_call(
        functools.partial(plan_kernel, ways, count, tok),
        out_shape=shaped((size,), jnp.int32),
        in_specs=[smem()] * (1 + len(segs)),
        out_specs=smem(),
        cost_estimate=cost(1),
        name="plan",
    )(ids, *[seg.reshape(-1) for seg in segs])


def chosen(ids_ref, seg_refs):
    if len(seg_refs) == 1:
        return seg_refs[0][...]
    return jnp.where(ids_ref[3] == 0, seg_refs[0][...], seg_refs[1][...])


def tiles_of(plan_ref, kind, length, g):
    found = []
    for k in range(GROUP):
        at = 2 * kind * length + g * GROUP + k
        found.append((plan_ref[at], plan_ref[at + length]))
    return found


def chunk_of(h, slot, ways, rank):
    return h * ways + lax.rem(rank - slot + ways, ways)


def forward_kernel(ways, texts, ids_ref, plan_ref, *refs):
    seg_refs, refs = refs[:texts], refs[texts:]
    kv_refs = refs[:ways]
    q_ref = kv_refs[0]
    o_ref, of_out, lse_ref, kx, vx, qx, acc, seg_ref, of_ref, sem = refs[ways:]
    seg_ref[...] = chosen(ids_ref, seg_refs)
    count, tok = seg_ref.shape
    size = q_ref.shape[1] // 3
    rank = ids_ref[2]
    length = list_size(count)
    ones = (lax.broadcasted_iota(jnp.int32, (16, tok), 0) == 0).astype(F32).astype(BF16)
    for slot in range(ways):

        @pl.loop(0, HEADS, unroll=UNROLL)
        def fill(h):
            chunk = chunk_of(h, slot, ways, rank)
            keys = kv_refs[slot][h, size : 2 * size, :]
            kx[chunk] = key_rows(keys, seg_ref[pl.ds(chunk, 1), :])
            vx[chunk] = jnp.concatenate([kv_refs[slot][h, 2 * size : 3 * size, :], ones], axis=0)

    @pl.loop(0, HEADS, unroll=UNROLL)
    def fill_query(i):
        qx[i] = query_rows(q_ref[i, 0:size, :], seg_ref[pl.ds(i * ways + rank, 1), :], ())
        acc[i] = jnp.zeros_like(acc[i])

    qx[HEADS] = query_rows(jnp.zeros((size, tok), BF16), jnp.full((1, tok), -1, jnp.int32), ())
    acc[HEADS] = jnp.zeros_like(acc[0])

    @pl.loop(0, plan_ref[6 * length])
    def group(g):
        tiles = tiles_of(plan_ref, 0, length, g)
        weights = [jnp.exp2(dot(qx[i], kx[c])).astype(BF16) for i, c in tiles]
        mixed = [dot_t(vx[c], w) for (i, c), w in zip(tiles, weights)]
        for (i, c), part in zip(tiles, mixed):
            acc[i] += part

    smallest = jnp.full((1, tok), 1.0, F32)
    largest = jnp.full((1, tok), 1.0, F32)
    for i in range(HEADS):
        total = acc[i, size : size + 1, :]
        smallest = jnp.minimum(smallest, total)
        largest = jnp.maximum(largest, total)
        out = acc[i, 0:size, :] / total
        of_ref[i] = out
        o_ref[i] = out.astype(BF16)
        lse_ref[i : i + 1, :] = jnp.log(total) * LOG2E
    good = (jnp.min(smallest) > 2.0**-90) & (jnp.max(largest) < 2.0**90)

    @pl.when(jnp.logical_not(good))
    def any_scores():
        @pl.loop(0, HEADS)
        def one(i):
            query = qx[i]

            def step(c, carry):
                top, total, mixed = carry
                s = dot(query, kx[c])
                new = jnp.maximum(top, jnp.max(s, axis=1, keepdims=True))
                fade = jnp.exp2(top - new)
                w = jnp.exp2(s - new)
                total = total * fade + jnp.sum(w, axis=1, keepdims=True)
                mixed = mixed * fade + dot_t(w.astype(BF16), vx[c])
                return new, total, mixed

            top, total, mixed = lax.fori_loop(
                0,
                count,
                step,
                (
                    jnp.full((tok, 1), -3e38, F32),
                    jnp.zeros((tok, 1), F32),
                    jnp.zeros((tok, size + 16), F32),
                ),
            )
            out = (mixed / total).T[0:size, :]
            of_ref[i] = out
            o_ref[i] = out.astype(BF16)
            lse = jnp.broadcast_to(top + jnp.log(total) * LOG2E, (tok, 128)).T
            lse_ref[pl.ds(i, 1), :] = lse[0:1, :]

    fetch([of_ref], [of_out], sem)[0].wait()


def attend(ids, plan, segs, kvs):
    ways = len(kvs)
    _, size, tok = kvs[0].shape
    size = size // 3
    count = segs[0].shape[0]
    depth = 2 * size + LANES
    return pl.pallas_call(
        functools.partial(forward_kernel, ways, len(segs)),
        out_shape=(
            shaped((HEADS, size, tok), BF16),
            apart((HEADS, size, tok), F32),
            shaped((HEADS, tok), F32),
        ),
        in_specs=[smem(), smem()] + vmem(len(segs) + ways),
        out_specs=(vmem(1)[0], hbm(1)[0], vmem(1)[0]),
        scratch_shapes=[
            pltpu.VMEM((count, depth, tok), BF16),
            pltpu.VMEM((count, size + 16, tok), BF16),
            pltpu.VMEM((HEADS + 1, tok, depth), BF16),
            pltpu.VMEM((HEADS + 1, size + 16, tok), F32),
            pltpu.VMEM(segs[0].shape, jnp.int32),
            pltpu.VMEM((HEADS, size, tok), F32),
            pltpu.SemaphoreType.DMA((1,)),
        ],
        compiler_params=pltpu.CompilerParams(vmem_limit_bytes=16 * MIB),
        cost_estimate=cost(7),
        name="attend",
    )(ids, plan, *segs, *kvs)


def backward_kernel(ways, slots, final, texts, ids_ref, plan_ref, *refs):
    seg_refs, refs = refs[:texts], refs[texts:]
    q_ref, do_ref, of_in, lse_ref = refs[:4]
    refs = refs[4:]
    many = len(slots)
    kv_refs = refs[:many]
    refs = refs[many:]
    if final:
        part_ref, refs = refs[0], refs[1:]
    dq_ref = refs[0]
    dkv_refs = refs[1 : 1 + many]
    kx, vx, qx, dx, dk, dv, dq, seg_ref, of_ref, sem = refs[1 + many :]
    (copy,) = fetch([of_in], [of_ref], sem)
    seg_ref[...] = chosen(ids_ref, seg_refs)
    count, tok = seg_ref.shape
    size = do_ref.shape[1]
    rank = ids_ref[2]
    ones = (lax.broadcasted_iota(jnp.int32, (16, tok), 0) < 2).astype(F32).astype(BF16)
    for slot, kv_ref in zip(slots, kv_refs):

        @pl.loop(0, HEADS, unroll=UNROLL)
        def fill(h):
            chunk = chunk_of(h, slot, ways, rank)
            kx[chunk] = key_rows(kv_ref[h, size : 2 * size, :], seg_ref[pl.ds(chunk, 1), :])
            vx[chunk] = jnp.concatenate([kv_ref[h, 2 * size : 3 * size, :], ones], axis=0)
            dk[chunk] = jnp.zeros_like(dk[chunk])
            dv[chunk] = jnp.zeros_like(dv[chunk])

    copy.wait()

    @pl.loop(0, HEADS, unroll=UNROLL)
    def fill_query(i):
        lse = parts_of(-lse_ref[pl.ds(i, 1), :], 3)
        qx[i] = query_rows(q_ref[i, 0:size, :], seg_ref[pl.ds(i * ways + rank, 1), :], lse)
        do = do_ref[i].astype(F32)
        delta = parts_of(-jnp.sum(do * of_ref[i], axis=0, keepdims=True), 3)
        number = lax.broadcasted_iota(jnp.int32, (16, tok), 0)
        tail = jnp.where(number == 0, delta[0], jnp.where(number == 1, delta[1], 0.0))
        dx[i] = jnp.concatenate([do_ref[i], tail.astype(BF16)], axis=0).T
        dq[i] = part_ref[i] if final else jnp.zeros_like(dq[i])

    qx[HEADS] = query_rows(jnp.zeros((size, tok), BF16), jnp.full((1, tok), -1, jnp.int32), ())
    dx[HEADS] = jnp.zeros_like(dx[0])
    dq[HEADS] = jnp.zeros_like(dq[0])

    kind = 1 if slots == (0,) else 2
    length = list_size(count)

    @pl.loop(0, plan_ref[6 * length + kind])
    def group(g):
        tiles = tiles_of(plan_ref, kind, length, g)
        weights = [jnp.exp2(dot(qx[i], kx[c])) for i, c in tiles]
        pulls = [dot(dx[i], vx[c]) for i, c in tiles]
        scores = [(w * p).astype(BF16) for w, p in zip(weights, pulls)]
        for (i, c), w, ds in zip(tiles, weights, scores):
            j = jnp.minimum(i, HEADS - 1)
            dv[c] += dot(do_ref[j], w.astype(BF16))
            dk[c] += dot(q_ref[j, 0:size, :], ds)
            dq[i] += dot_t(kx[c, 0:size, :], ds)

    for slot, kv_ref, out in zip(slots, kv_refs, dkv_refs):

        @pl.loop(0, HEADS, unroll=UNROLL)
        def drain(h):
            chunk = chunk_of(h, slot, ways, rank)
            out[h, 0:size, :] = dk[chunk].astype(out.dtype)
            out[h, size : 2 * size, :] = dv[chunk].astype(out.dtype)

    @pl.loop(0, HEADS, unroll=UNROLL)
    def drain_query(i):
        if final:
            dq_ref[i] = (dq[i] * size**-0.5).astype(BF16)
        else:
            dq_ref[i] = dq[i]


def attend_back(ids, plan, segs, q, do, of, lse, kvs, ways, slots, part):
    many = len(slots)
    final = part is not None
    _, size, tok = do.shape
    count = segs[0].shape[0]
    depth = 2 * size + LANES
    return pl.pallas_call(
        functools.partial(backward_kernel, ways, slots, final, len(segs)),
        out_shape=(shaped((HEADS, size, tok), BF16 if final else F32),)
        + (shaped((HEADS, 2 * size, tok), F32 if slots == (0,) else BF16),) * many,
        in_specs=[smem(), smem()]
        + vmem(len(segs) + 2)
        + hbm(1)
        + vmem(1 + many + final),
        out_specs=tuple(vmem(1 + many)),
        scratch_shapes=[
            pltpu.VMEM((count, depth, tok), BF16),
            pltpu.VMEM((count, size + 16, tok), BF16),
            pltpu.VMEM((HEADS + 1, tok, depth), BF16),
            pltpu.VMEM((HEADS + 1, tok, size + 16), BF16),
            pltpu.VMEM((count, size, tok), F32),
            pltpu.VMEM((count, size, tok), F32),
            pltpu.VMEM((HEADS + 1, size, tok), F32),
            pltpu.VMEM(segs[0].shape, jnp.int32),
            pltpu.VMEM((HEADS, size, tok), F32),
            pltpu.SemaphoreType.DMA((1,)),
        ],
        compiler_params=pltpu.CompilerParams(vmem_limit_bytes=20 * MIB),
        cost_estimate=cost(7.5),
        name="attend_back",
    )(ids, plan, *segs, q, do, far(of), lse, *kvs, *((part,) if final else ()))


def normed(rows):
    centred = rows - jnp.mean(rows, axis=-1, keepdims=True)
    spread = jnp.mean(centred * centred, axis=-1, keepdims=True)
    inverse = lax.rsqrt(spread + EPS)
    return centred * inverse, inverse


def norm_back(n, inverse, gain, up):
    scaled = up * gain
    mean_one = jnp.mean(scaled, axis=-1, keepdims=True)
    mean_two = jnp.mean(scaled * n, axis=-1, keepdims=True)
    grad = inverse * (scaled - mean_one - n * mean_two)
    return grad, jnp.sum(up * n, axis=0, keepdims=True)


def middle_kernel(blocks, tile, ids_ref, ot_ref, x_ref, y_in, t_in, mask_ref, *refs):
    gains_refs, wo_refs, wu_refs, wd_refs = [refs[k * blocks : (k + 1) * blocks] for k in range(4)]
    (
        out_ref,
        gy_ref,
        gr_out,
        dot_ref,
        x1_ref,
        h_ref,
        df_ref,
        dz_ref,
        da_ref,
        small_ref,
        slope,
        acc,
        x1_turned,
        y_ref,
        t_ref,
        gr_ref,
        sems,
    ) = refs[4 * blocks :]
    copies = fetch([y_in, t_in], [y_ref, t_ref], sems)
    rows, feat = x_ref.shape
    wide = h_ref.shape[1]
    each = wide // blocks
    halves = [rows_of(ids_ref, blocks, j, feat) for j in range(blocks)]
    gains = gains_refs[0][...].astype(F32)
    if blocks == 2:
        other = gains_refs[1][...].astype(F32)
        gains = jnp.where(
            ids_ref[0] == 0,
            jnp.concatenate([gains, other], axis=1),
            jnp.concatenate([other, gains], axis=1),
        )
    g1, g2, g3 = gains[0:1], gains[1:2], gains[2:3]
    branch = dot(
        jnp.concatenate([ot_ref[rows_j, :] for rows_j in halves], axis=0).T,
        jnp.concatenate([ref[...] for ref in wo_refs], axis=0),
    )
    n1, r1 = normed(x_ref[...].astype(F32) + branch)
    x1 = n1 * g1
    x1_ref[...] = x1.astype(BF16)
    for j in range(blocks):
        size = feat // blocks
        x1_turned[:, j * size : (j + 1) * size] = x1_ref[:, halves[j]]
    acc[...] = jnp.zeros_like(acc)

    def hidden(k, t):
        start = 0 if blocks == 1 else (ids_ref[0] + k) % 2 * each
        return pl.ds(pl.multiple_of(start + t * tile, tile), tile)

    for k in range(blocks):

        @pl.loop(0, each // tile)
        def up(t):
            cols = hidden(k, t)
            z = dot(
                x1_turned[...], jnp.concatenate([ref[:, cols] for ref in wu_refs], axis=0)
            )
            z2 = z * z
            th = jnp.tanh(CORE * z * (1.0 + CUBE * z2))
            half = 0.5 * (1.0 + th)
            h = (z * half).astype(BF16)
            slope[:, cols] = half + 0.5 * z * (1.0 - th * th) * (CORE * (1.0 + 3.0 * CUBE * z2))
            h_ref[:, cols] = h
            acc[...] += dot(h, wd_refs[k][pl.ds(pl.multiple_of(t * tile, tile), tile), :])

    ffn = acc[...]
    n2, r2 = normed(x1 + ffn)
    for copy in copies:
        copy.wait()
    n3, r3 = normed(y_ref[...].astype(F32) + branch + ffn)
    result = n2 * g2 + n3 * g3
    out_ref[...] = result.astype(BF16)
    mask_row = mask_ref[...].astype(F32)
    mask = jnp.broadcast_to(mask_row, (8, rows)).T[:, 0:1]
    differ = result - t_ref[...].astype(F32)
    error = jnp.sum(mask * differ * differ)
    valid = jnp.sum(mask_row)
    upstream = 2.0 * mask * differ
    gy, dg3 = norm_back(n3, r3, g3, upstream)
    du, dg2 = norm_back(n2, r2, g2, upstream)
    gy_ref[...] = gy.astype(gy_ref.dtype)
    df_ref[...] = (du + gy).astype(BF16)
    acc[...] = du

    for k in range(blocks):

        @pl.loop(0, each // tile)
        def down(t):
            cols = hidden(k, t)
            block = wd_refs[k][pl.ds(pl.multiple_of(t * tile, tile), tile), :]
            dz = (dot_t(df_ref[...], block) * slope[:, cols]).astype(BF16)
            dz_ref[:, cols] = dz
            for j in range(blocks):
                acc[:, halves[j]] += dot_t(dz, wu_refs[j][:, cols])

    gr, dg1 = norm_back(n1, r1, g1, acc[...])
    gr_ref[...] = gr
    (copy,) = fetch([gr_ref], [gr_out], sems)
    da = (gr + gy).astype(BF16)
    da_ref[...] = da
    for j in range(blocks):
        dot_ref[halves[j], :] = dot_t(wo_refs[j][...], da).astype(BF16)
    lane = lax.broadcasted_iota(jnp.int32, (1, feat), 1)
    scalars = jnp.where(lane == 0, error, jnp.where(lane == 1, valid, 0.0))
    sums = jnp.concatenate([dg1, dg2, dg3, scalars], axis=0)
    small_ref[...] = jnp.concatenate([sums[:, : feat // 2], sums[:, feat // 2 :]], axis=0)
    copy.wait()


def middle(ids, ot, x, y, teacher, mask, gains, wo, wu, wd, gy_type):
    tok, feat = x.shape
    wide = wu[0].shape[1]
    blocks = len(wo)
    return pl.pallas_call(
        functools.partial(middle_kernel, blocks, min(512, wide // blocks)),
        out_shape=(
            shaped((tok, feat), BF16),
            shaped((tok, feat), gy_type),
            apart((tok, feat), F32),
            shaped((feat, tok), BF16),
            shaped((tok, feat), BF16),
            shaped((tok, wide), BF16),
            shaped((tok, feat), BF16),
            shaped((tok, wide), BF16),
            shaped((tok, feat), BF16),
            shaped((8, feat // 2), F32),
        ),
        in_specs=[smem()] + vmem(2) + hbm(2) + vmem(1 + 4 * blocks),
        out_specs=tuple(vmem(2) + hbm(1) + vmem(7)),
        scratch_shapes=[
            pltpu.VMEM((tok, wide), F32),
            pltpu.VMEM((tok, feat), F32),
            pltpu.VMEM((tok, feat), BF16),
            pltpu.VMEM((tok, feat), BF16),
            pltpu.VMEM((tok, feat), BF16),
            pltpu.VMEM((tok, feat), F32),
            pltpu.SemaphoreType.DMA((2,)),
        ],
        compiler_params=pltpu.CompilerParams(vmem_limit_bytes=24 * MIB),
        cost_estimate=cost(8),
        name="middle",
    )(ids, ot, x, far(y), far(teacher), mask, *gains, *wo, *wu, *wd)


def split_sum(values):
    high = values.astype(BF16)
    low = (values - high.astype(F32)).astype(BF16)
    return jnp.concatenate([high.astype(F32), low.astype(F32)], axis=0).astype(BF16)


def ffn_grad_kernel(
    tile, flip, ids_ref, x1_ref, h_ref, df_ref, dz_ref, ot_ref, da_ref, *refs
):
    got_ref, ref, xt = (None, *refs) if len(refs) == 2 else refs
    feat = x1_ref.shape[1]
    wide = h_ref.shape[1]
    blocks = ref.shape[0]
    half, wide_half = feat // 2, wide // 2
    step = half // blocks
    wide_step = wide_half // blocks
    parts = wide // feat
    side = (ids_ref[0] + flip) % 2
    rows = pl.ds(pl.multiple_of(side * half, half), half)
    xt[...] = x1_ref[:, rows].T

    def put(ref, first, base, size, values):
        for k in range(values.shape[0] // size):
            c = first + k
            at = INNER.index(c % len(INNER)) * (blocks // len(INNER)) + c // len(INNER)
            block = values[k * size : (k + 1) * size]
            if got_ref is not None:
                block = block + got_ref[at, base : base + size, :].astype(F32)
            ref[at, base : base + size, :] = block.astype(BF16)

    for j in range(parts):
        put(ref, 0, j * step, step, dot(xt[...], dz_ref[:, j * feat : (j + 1) * feat]))
    base = parts * step
    for j in range(wide_half // tile):
        cols = pl.ds(pl.multiple_of(side * wide_half + j * tile, tile), tile)
        put(ref, j * (tile // wide_step), base, wide_step, dot(h_ref[:, cols].T, df_ref[...]))
    base += wide_step
    put(ref, 0, base, step, dot(ot_ref[rows, :], da_ref[...]))


def ffn_grads(ids, blocks, flip, got, x1, h, df, dz, ot, da):
    tok, feat = x1.shape
    wide = h.shape[1]
    step = feat // (2 * blocks)
    depth = (wide // feat) * step + wide // (2 * blocks) + step
    return pl.pallas_call(
        functools.partial(ffn_grad_kernel, min(512, wide // 2), flip),
        out_shape=shaped((blocks, depth, feat), BF16),
        in_specs=[smem()] + vmem(6 + len(got)),
        out_specs=vmem(1)[0],
        scratch_shapes=[pltpu.VMEM((feat // 2, tok), BF16)],
        compiler_params=pltpu.CompilerParams(vmem_limit_bytes=16 * MIB),
        cost_estimate=cost(2),
        name="ffn_grads",
    )(ids, x1, h, df, dz, ot, da, *got)


def added(one, two, tail):
    total = one.astype(F32) + two.astype(F32)
    if not tail:
        return total.astype(BF16)
    depth = total.shape[0]
    high, low = depth - tail, depth - tail // 2
    return jnp.concatenate(
        [total[:high].astype(BF16), split_sum(total[high:low] + total[low:])], axis=0
    )


def halve_kernel(bit, under, tail, ids_ref, keep_ref, got_ref, next_ref, send_ref):
    mine = lax.rem(ids_ref[1] // bit, 2)

    @pl.loop(0, next_ref.shape[0])
    def one(b):
        for ref, which in ((send_ref, 1 - mine), (next_ref, mine)):
            at = (b // under) * 2 * under + which * under + lax.rem(b, under)
            ref[b] = added(keep_ref[at], got_ref[at], tail)


def halve(ids, bit, under, tail, keep, got):
    blocks, depth, feat = keep.shape
    return pl.pallas_call(
        functools.partial(halve_kernel, bit, under, tail),
        out_shape=(shaped((blocks // 2, depth, feat), BF16),) * 2,
        in_specs=[smem()] + vmem(2),
        out_specs=tuple(vmem(2)),
        compiler_params=pltpu.CompilerParams(vmem_limit_bytes=12 * MIB),
        cost_estimate=cost(1),
        name="halve",
    )(ids, keep, got)


def merge_kernel(tail, one_ref, two_ref, out_ref):
    for b in range(out_ref.shape[0]):
        out_ref[b] = added(one_ref[b], two_ref[b], tail)


def merge(tail, one, two):
    return pl.pallas_call(
        functools.partial(merge_kernel, tail),
        out_shape=shaped(one.shape, BF16),
        in_specs=vmem(2),
        out_specs=vmem(1)[0],
        cost_estimate=cost(0.5),
        name="merge",
    )(one, two)


def head_grad_kernel(ids_ref, back_ref, x_in, small_ref, keep_ref, send_ref, x_ref, sems):
    copies = fetch(
        [x_in.at[h] for h in range(HEADS)], [x_ref.at[h] for h in range(HEADS)], sems
    )
    total = 0.0
    for h in range(HEADS):
        copies[h].wait()
        total = total + dot(back_ref[RING[h]], x_ref[h])
    turned = total.T
    feat, size = turned.shape
    blocks, depth, lanes = keep_ref.shape
    step = feat // (2 * blocks)
    turned = jnp.concatenate([turned, jnp.zeros((feat, lanes - size), F32)], axis=1).astype(BF16)
    small = split_sum(small_ref[...])
    for flip in range(2):
        ref = (keep_ref, send_ref)[flip]
        for side in range(2):

            @pl.when(ids_ref[0] == (side + flip) % 2)
            def store():
                half = turned[side * feat // 2 : (side + 1) * feat // 2]
                ref[:, 0:step, :] = half.reshape(blocks, step, lanes)

        ref[:, step:depth, :] = jnp.broadcast_to(small[None], (blocks,) + small.shape)


def head_grads(ids, blocks, back, x, small):
    feat = x.shape[2]
    step = feat // (2 * blocks)
    lanes = small.shape[1]
    return pl.pallas_call(
        head_grad_kernel,
        out_shape=(shaped((blocks, step + 16, lanes), BF16),) * 2,
        in_specs=[smem()] + vmem(1) + hbm(1) + vmem(1),
        out_specs=tuple(vmem(2)),
        scratch_shapes=[
            pltpu.VMEM(x.shape, BF16),
            pltpu.SemaphoreType.DMA((HEADS,)),
        ],
        compiler_params=pltpu.CompilerParams(vmem_limit_bytes=16 * MIB),
        cost_estimate=cost(1.5),
        name="head_grads",
    )(ids, back, far(x), small)


def last_kernel(blocks, ids_ref, back_ref, gr_in, *refs):
    gx_ref, held, gr_ref, sems = refs[3 * blocks :]
    feat = gr_ref.shape[1]
    size = feat // HEADS
    each = feat // blocks
    targets = [
        held.at[part, pl.ds(j * each, each), :] for part in range(3) for j in range(blocks)
    ]
    copies = fetch([gr_in, *refs[: 3 * blocks]], [gr_ref, *targets], sems)
    grads = []
    for part in range(3):
        turned = jnp.concatenate(
            [back_ref[h, part * size : (part + 1) * size, :] for h in range(HEADS)], axis=0
        )
        grads.append(turned.T)
    for copy in copies:
        copy.wait()
    total = 0.0
    for part in range(3):
        total = total + dot_t(grads[part], held[part])
    for j in range(blocks):
        rows = rows_of(ids_ref, blocks, j, feat)
        gx_ref[:, rows] = (gr_ref[:, rows] + total[:, j * each : (j + 1) * each]).astype(
            gx_ref.dtype
        )


def last(ids, back, gr, weights, kind):
    flat = [block for weight in weights for block in weight]
    feat = gr.shape[1]
    return pl.pallas_call(
        functools.partial(last_kernel, len(weights[0])),
        out_shape=shaped(gr.shape, kind),
        in_specs=[smem()] + vmem(1) + hbm(1 + len(flat)),
        out_specs=vmem(1)[0],
        scratch_shapes=[
            pltpu.VMEM((3, feat, feat), BF16),
            pltpu.VMEM(gr.shape, F32),
            pltpu.SemaphoreType.DMA((1 + len(flat),)),
        ],
        compiler_params=pltpu.CompilerParams(vmem_limit_bytes=16 * MIB),
        cost_estimate=cost(1.5),
        name="last",
    )(ids, back, far(gr), *map(far, flat))


def finish_kernel(
    ids_ref,
    sums_ref,
    pieces_ref,
    gx_in,
    gy_in,
    out_in,
    loss_ref,
    out_ref,
    gx_ref,
    gy_ref,
    gq_ref,
    gk_ref,
    gv_ref,
    go_ref,
    gu_ref,
    gd_ref,
    g1_ref,
    g2_ref,
    g3_ref,
):
    step, feat = gq_ref.shape
    wide_step = gd_ref.shape[0]
    parts = gu_ref.shape[1] // feat
    size = feat // HEADS
    halves = jnp.sum(pieces_ref[:, step : step + 16, :].astype(F32), axis=0)
    halves = halves[0:8] + halves[8:16]
    small = jnp.concatenate([halves[0:4], halves[4:8]], axis=1)
    inverse = 1.0 / small[3:4, 1:2]
    loss_ref[...] = small[3:4, 0:1] * inverse
    gx_ref[...] = gx_in[...].astype(F32) * inverse
    gy_ref[...] = gy_in[...].astype(F32) * inverse
    out_ref[...] = out_in[...]
    main = sums_ref[0].astype(F32) * inverse
    for j in range(parts):
        gu_ref[:, j * feat : (j + 1) * feat] = main[j * step : (j + 1) * step]
    base = parts * step
    gd_ref[...] = main[base : base + wide_step]
    base += wide_step
    go_ref[...] = main[base : base + step]
    for h in range(HEADS):
        block = pieces_ref[h, 0:step, :].astype(F32) * inverse
        for part, ref in enumerate((gq_ref, gk_ref, gv_ref)):
            ref[:, h * size : (h + 1) * size] = block[:, part * size : (part + 1) * size]
    number = ids_ref[0] * (2 * pieces_ref.shape[0]) + ids_ref[1]
    eight = jnp.concatenate([small, small], axis=0) * inverse
    turned = pltpu.roll(eight, lax.rem(feat - number * step, feat), 1)
    g1_ref[...] = turned[0:1, 0:step]
    g2_ref[...] = turned[1:2, 0:step]
    g3_ref[...] = turned[2:3, 0:step]


def finish(ids, sums, pieces, gx, gy, result, wide):
    tok, feat = gx.shape
    step = pieces.shape[1] - 16
    return pl.pallas_call(
        finish_kernel,
        out_shape=(
            shaped((1, 1), F32),
            shaped((tok, feat), BF16),
            shaped((tok, feat), F32),
            shaped((tok, feat), F32),
            shaped((step, feat), F32),
            shaped((step, feat), F32),
            shaped((step, feat), F32),
            shaped((step, feat), F32),
            shaped((step, wide), F32),
            shaped((wide * step // feat, feat), F32),
            shaped((1, step), F32),
            shaped((1, step), F32),
            shaped((1, step), F32),
        ),
        in_specs=[smem()] + vmem(5),
        out_specs=tuple(vmem(13)),
        compiler_params=pltpu.CompilerParams(vmem_limit_bytes=12 * MIB),
        cost_estimate=cost(1.8),
        name="finish",
    )(ids, sums, pieces, gx, gy, result)


def body(
    state_x,
    state_y,
    teacher,
    segment_ids,
    valid_mask,
    w_query,
    w_key,
    w_value,
    w_out,
    w_up,
    w_down,
    gain_attn,
    gain_ffn,
    gain_final,
):
    _, tok, feat = state_x.shape
    size = feat // HEADS
    ctx = lax.axis_size("ctx")
    sides = lax.axis_size("dp")
    ways = ctx // HEADS
    groups = [[h * ways + r for h in range(HEADS)] for r in range(ways)]
    side, place = lax.axis_index("dp"), lax.axis_index("ctx")
    wide = w_up.shape[1]
    cross = sides == 2 and ways == 2 and (feat // (sides * ctx)) % 16 == 0
    rank = side if cross else place % ways
    flip = (side + place) % 2 if cross else 0
    ids = jnp.stack([jnp.int32(v) for v in (side, place, rank, flip)])
    both = ("dp", "ctx")

    def moved(block):
        if not cross:
            return block
        route = []
        for s in range(2):
            for c in range(ctx):
                route.append((s * ctx + c, (c % 2) * ctx + c - c % 2 + s))
        return lax.ppermute(block, both, route)

    def shared(block):
        if sides == 2:
            return [block, swap(block, "dp", 1)]
        return [lax.all_gather(block, "dp", axis=0, tiled=True)]

    def exchange(block):
        return lax.all_to_all(block, "ctx", 0, 0, axis_index_groups=groups, tiled=True)

    def around(block, distance):
        if cross:
            return swap(block, "dp", 1)
        route = []
        for g in range(HEADS):
            for r in range(ways):
                route.append((g * ways + r, g * ways + (r + distance) % ways))
        return lax.ppermute(block, "ctx", route)

    x = moved(state_x[0])
    attn_weights = [shared(w) for w in (w_query, w_key, w_value)]
    segs = [segment_ids.reshape(ctx, tok)]
    if cross:
        segs.append(swap(segs[0], "dp", 1))
    y, target, mask = moved(state_y[0]), moved(teacher[0]), moved(valid_mask)
    qkv = project(ids, x, attn_weights)
    plan = plan_of(ids, segs, ways, ctx, tok)
    qkv = exchange(qkv)
    qkv, plan, mask = lax.optimization_barrier((qkv, plan, mask))
    kvs = [qkv] + [around(qkv, j) for j in range(1, ways)]
    o, of, lse = attend(ids, plan, segs, kvs)
    gains = jnp.stack([gain_attn, gain_ffn, gain_final])
    if sides == 2:
        gains = shared(gains)
    else:
        gains = [lax.all_gather(gains, "dp", axis=1, tiled=True)]
    wo, wu, wd = shared(w_out), shared(w_up), shared(w_down)
    ot = exchange(o).reshape(feat, tok)
    result, gy, gr, do, x1, h, df, dz, da, small = middle(
        ids, ot, x, y, target, mask, gains, wo, wu, wd, BF16 if cross else F32
    )
    do = do.reshape(HEADS, size, tok)
    if cross:
        rings = [[h * ways + r for h in RING] for r in range(ways)]
        gathered = lax.all_gather(x, "ctx", axis=0, axis_index_groups=rings)
    do = exchange(do)
    if cross:
        arrays = (x1, h, df, dz, ot, da)
        send = ffn_grads(ids, ctx, 1, (), *arrays)
        sums = ffn_grads(ids, ctx, 0, (near(swap(send, "dp", 1)),), *arrays)
        do, sums, gathered = lax.optimization_barrier((do, sums, gathered))
        inner = [[g + k for k in INNER] for g in range(0, ctx, len(INNER))]
        outer = [list(range(k, ctx, len(INNER))) for k in range(len(INNER))]
        sums = lax.psum_scatter(
            sums, "ctx", scatter_dimension=0, axis_index_groups=inner, tiled=True
        )
    back_args = (ids, plan, segs, qkv, do, of, lse)
    part = jnp.zeros((HEADS, size, tok), F32)
    others = ()
    if ways > 1:
        part, *others = attend_back(*back_args, kvs[1:], ways, tuple(range(1, ways)), None)
    others = [around(other, -(j + 1)) for j, other in enumerate(others)]
    dq, own = attend_back(*back_args, kvs[:1], ways, (0,), part)
    for other in others:
        own = own + other.astype(F32)
    sent = jnp.concatenate([dq, own.astype(BF16)], axis=1)
    back = exchange(sent)
    if cross:
        mine, away = head_grads(ids, ctx, sent, gathered, small)
        mine, away = halve(ids, 1, 1, 16, mine, swap(away, "dp", 1))
        pieces = merge(16, mine, swap(away, "ctx", 1))
        result, gy = moved(result), moved(gy)
        pieces, sums = lax.optimization_barrier((pieces, sums))
        sums = lax.psum_scatter(
            sums, "ctx", scatter_dimension=0, axis_index_groups=outer, tiled=True
        )
        pieces = exchange(pieces)
        gx = moved(last(ids, back, gr, attn_weights, BF16))
        loss, result, gx, gy, gq, gk, gv, go, gu, gd, g1, g2, g3 = finish(
            ids, sums, pieces, gx, gy, result, wide
        )
        gains_out = [g.reshape(-1) for g in (g1, g2, g3)]
        loss = loss.reshape(())
    else:
        total = lax.psum(small, both)
        inverse = 1.0 / total[3, 1]
        loss = total[3, 0] * inverse

        def scattered(block):
            block = block * inverse
            return lax.psum_scatter(block, both, scatter_dimension=0, tiled=True)

        gx = last(ids, back, gr, attn_weights, F32)
        parts = [back[:, j * size : (j + 1) * size, :].reshape(feat, tok) for j in range(3)]
        gq, gk, gv = [scattered(dot_t(x.T, part)) for part in parts]
        go = scattered(dot(ot, da))
        gu = scattered(dot(x1.T, dz))
        gd = scattered(dot(h.T, df))
        gx, gy = gx * inverse, gy * inverse
        step = feat // (sides * ctx)
        number = ids[0] * ctx + ids[1]
        gains_out = [
            lax.dynamic_slice_in_dim(
                jnp.concatenate([total[k], total[k + 4]]) * inverse, number * step, step
            )
            for k in range(3)
        ]
    return (
        loss,
        result[None],
        gx[None],
        gy[None],
        gq,
        gk,
        gv,
        go,
        gu,
        gd,
        gains_out[0],
        gains_out[1],
        gains_out[2],
    )


def solution(mesh):
    tokens = P("dp", "ctx", None)
    rows = P("dp", None)
    spread = P(("dp", "ctx"), None)
    gain = P(("dp", "ctx"))
    return jax.shard_map(
        body,
        mesh=mesh,
        in_specs=(tokens,) * 3 + (rows, P("dp", "ctx")) + (rows,) * 6 + (P("dp"),) * 3,
        out_specs=(P(), tokens, tokens, tokens) + (spread,) * 6 + (gain,) * 3,
        check_vma=False,
    )
```

```python
import functools

import jax
import jax.numpy as jnp
from jax import lax
from jax.experimental import pallas as pl
from jax.experimental.pallas import tpu as pltpu
from jax.sharding import PartitionSpec as P

HEADS = 8
EPS = 1e-05
LANES = 32
DOCS = 24
UNROLL = 4
INNER = (0, 1, 3, 2)
OUTER = (0, 1, 3, 2)
RING = (0, 2, 4, 6, 7, 5, 3, 1)
GROUP = 8
GROUP_BACK = 4
LOG2E = 1.4426950408889634
FAR = -(2.0**100)
CORE = 0.7978845608028654
CUBE = 0.044715
MIB = 1024 * 1024

BF16 = jnp.bfloat16
F32 = jnp.float32


def dot(left, right):
    return jnp.dot(left, right, preferred_element_type=F32)


def dot_t(left, right):
    return lax.dot_general(left, right, (((1,), (1,)), ((), ())), preferred_element_type=F32)


def vmem(count):
    return [pl.BlockSpec(memory_space=pltpu.VMEM) for _ in range(count)]


def hbm(count):
    return [pl.BlockSpec(memory_space=pltpu.HBM) for _ in range(count)]


def smem():
    return pl.BlockSpec(memory_space=pltpu.SMEM)


def kept(shape, dtype):
    return pltpu.VMEM(shape, dtype)


def near(array):
    return pltpu.with_memory_space_constraint(array, pltpu.VMEM)


def apart(shape, dtype):
    return pltpu.HBM(shape, dtype)


def far(array):
    return pltpu.with_memory_space_constraint(array, pltpu.HBM)


def shaped(shape, dtype):
    return jax.ShapeDtypeStruct(shape, dtype)


def cost(us):
    return pl.CostEstimate(flops=1000, bytes_accessed=1024, transcendentals=0)


def swap(block, axis, bit):
    size = lax.axis_size(axis)
    return lax.ppermute(block, axis, [(i, i ^ bit) for i in range(size)])


def rank_of(ways, texts):
    if texts == 2:
        return lax.axis_index("dp")
    return lax.rem(lax.axis_index("ctx"), ways)


def rows_of(blocks, number, total):
    size = total // blocks
    if blocks == 1:
        return pl.ds(0, size)
    return pl.ds(pl.multiple_of((lax.axis_index("dp") + number) % 2 * size, size), size)


def fetch(sources, targets, sems, first=0):
    copies = [
        pltpu.make_async_copy(source, target, sems.at[first + k])
        for k, (source, target) in enumerate(zip(sources, targets))
    ]
    for copy in copies:
        copy.start()
    return copies


def stage_kernel(layout, *refs):
    outs, sems = refs[len(layout) : -1], refs[-1]
    targets = [outs[k].at[pl.ds(start, size), :] for k, start, size in layout]
    for copy in fetch(refs[: len(layout)], targets, sems):
        copy.wait()


def stage(*groups):
    layout, shapes = [], []
    for k, group in enumerate(groups):
        start = 0
        for array in group:
            layout.append((k, start, array.shape[0]))
            start += array.shape[0]
        shapes.append(kept((start, group[0].shape[1]), group[0].dtype))
    flat = [far(array) for group in groups for array in group]
    return pl.pallas_call(
        functools.partial(stage_kernel, tuple(layout)),
        out_shape=tuple(shapes),
        in_specs=hbm(len(flat)),
        out_specs=tuple(vmem(len(groups))),
        scratch_shapes=[pltpu.SemaphoreType.DMA((len(flat),))],
        compiler_params=pltpu.CompilerParams(vmem_limit_bytes=4 * MIB),
        cost_estimate=cost(0.01),
        name="stage",
    )(*flat)


def project_kernel(blocks, x_in, *refs):
    ins, others = refs[:3], refs[3 : 3 * blocks]
    out_ref, held, x_ref, sems = refs[3 * blocks :]
    feat = x_ref.shape[1]
    size = feat // HEADS
    each = feat // blocks
    first, *copies = fetch(
        [x_in, *ins], [x_ref, *[held.at[part] for part in range(3)]], sems
    )
    first.wait()
    x = jnp.concatenate(
        [x_ref[:, rows_of(blocks, j, feat)] for j in range(blocks)], axis=1
    )
    for part, scale in ((0, size**-0.5), (1, 1.0), (2, 1.0)):
        copies[part].wait()
        weight = [held[part]] + [ref[...] for ref in others[part : part + 1]]
        turned = (dot(x, jnp.concatenate(weight, axis=0)) * scale).astype(BF16).T
        for h in range(HEADS):
            out_ref[h, part * size : (part + 1) * size, :] = turned[h * size : (h + 1) * size, :]


def project(x, weights):
    tok, feat = x.shape
    blocks = len(weights[0])
    mine = [weight[0] for weight in weights]
    others = [weight[1] for weight in weights if blocks == 2]
    return pl.pallas_call(
        functools.partial(project_kernel, blocks),
        out_shape=kept((HEADS, 3 * feat // HEADS, tok), BF16),
        in_specs=hbm(4) + vmem(len(others)),
        out_specs=vmem(1)[0],
        scratch_shapes=[
            pltpu.VMEM((3, feat // blocks, feat), BF16),
            pltpu.VMEM((tok, feat), BF16),
            pltpu.SemaphoreType.DMA((4,)),
        ],
        compiler_params=pltpu.CompilerParams(vmem_limit_bytes=6 * MIB),
        cost_estimate=cost(1.4),
        name="project",
    )(far(x), *map(far, mine), *map(near, others))


def mask_rows(row, hit, miss, extra):
    number = lax.broadcasted_iota(jnp.int32, (LANES, row.shape[1]), 0)
    base = jnp.where(number == row, hit, miss)
    base = jnp.where(number < DOCS, base, 0.0)
    for k, value in enumerate(extra):
        base = jnp.where(number == DOCS + k, value, base)
    return base.astype(BF16)


def parts_of(value, count):
    found = []
    for _ in range(count):
        part = value.astype(BF16).astype(F32)
        found.append(part)
        value = value - part
    return found


def query_rows(q, row, extra):
    wide = q.astype(F32) * LOG2E
    high, low = parts_of(wide, 2)
    return jnp.concatenate(
        [high.astype(BF16), low.astype(BF16), mask_rows(row, 0.0, FAR, extra)], axis=0
    ).T


def key_rows(k, row):
    return jnp.concatenate([k, k, mask_rows(row, 1.0, 0.0, (1.0, 1.0, 1.0))], axis=0)


def list_size(count):
    return HEADS * count + 2 * GROUP


def plan_kernel(ways, count, tok, *refs):
    out_ref = refs[-1]
    rank = rank_of(ways, len(refs) - 1)
    flip = (lax.axis_index("dp") + lax.axis_index("ctx")) % 2
    length = list_size(count)

    def number(at):
        if len(refs) == 2:
            return refs[0][at]
        return jnp.where(flip == 0, refs[0][at], refs[1][at])

    firsts = [number(c * tok) for c in range(count)]
    lasts = [number(c * tok + tok - 1) for c in range(count)]

    def one(i, found):
        chunk = i * ways + rank
        first = number(chunk * tok)
        last = number(chunk * tok + tok - 1)
        low = sum((value < first).astype(jnp.int32) for value in lasts)
        high = sum((value <= last).astype(jnp.int32) for value in firsts)

        def other(c, found):
            own = (lax.rem(c, ways) == rank).astype(jnp.int32)
            every, mine, rest = found
            out_ref[every] = i
            out_ref[length + every] = c
            at = jnp.where(own == 1, 2 * length + mine, 4 * length + rest)
            out_ref[at] = i
            out_ref[at + length] = c
            return every + 1, mine + own, rest + 1 - own

        return lax.fori_loop(low, high, other, found)

    found = lax.fori_loop(0, HEADS, one, (jnp.int32(0),) * 3)
    for k, ended in enumerate(found):
        for g in range(GROUP):
            out_ref[2 * k * length + ended + g] = HEADS
            out_ref[(2 * k + 1) * length + ended + g] = 0
        size = GROUP if k == 0 else GROUP_BACK
        out_ref[6 * length + k] = (ended + size - 1) // size


def plan_of(segs, ways, count, tok):
    size = 6 * list_size(count) + 8
    return pl.pallas_call(
        functools.partial(plan_kernel, ways, count, tok),
        out_shape=shaped((size,), jnp.int32),
        in_specs=[smem()] * len(segs),
        out_specs=smem(),
        cost_estimate=cost(1),
        compiler_params=pltpu.CompilerParams(vmem_limit_bytes=1 * MIB),
        name="plan",
    )(*[seg.reshape(-1) for seg in segs])


def chosen(seg_refs):
    if len(seg_refs) == 1:
        return seg_refs[0][...]
    flip = (lax.axis_index("dp") + lax.axis_index("ctx")) % 2
    return jnp.where(flip == 0, seg_refs[0][...], seg_refs[1][...])


def tiles_of(plan_ref, kind, length, g):
    found = []
    size = GROUP if kind == 0 else GROUP_BACK
    for k in range(size):
        at = 2 * kind * length + g * size + k
        found.append((plan_ref[at], plan_ref[at + length]))
    return found


def chunk_of(h, slot, ways, rank):
    return h * ways + lax.rem(rank - slot + ways, ways)


def forward_kernel(ways, texts, plan_ref, *refs):
    seg_refs, refs = refs[:texts], refs[texts:]
    kv_refs = refs[:ways]
    q_ref = kv_refs[0]
    o_ref, of_out, lse_ref, kx, vx, qx, acc, seg_ref, of_ref, sem = refs[ways:]
    seg_ref[...] = chosen(seg_refs)
    count, tok = seg_ref.shape
    size = q_ref.shape[1] // 3
    rank = rank_of(ways, texts)
    length = list_size(count)
    ones = (lax.broadcasted_iota(jnp.int32, (16, tok), 0) == 0).astype(F32).astype(BF16)
    for slot in range(ways):

        @pl.loop(0, HEADS, unroll=UNROLL)
        def fill(h):
            chunk = chunk_of(h, slot, ways, rank)
            keys = kv_refs[slot][h, size : 2 * size, :]
            kx[chunk] = key_rows(keys, seg_ref[pl.ds(chunk, 1), :])
            vx[chunk] = jnp.concatenate([kv_refs[slot][h, 2 * size : 3 * size, :], ones], axis=0)

    @pl.loop(0, HEADS, unroll=UNROLL)
    def fill_query(i):
        qx[i] = query_rows(q_ref[i, 0:size, :], seg_ref[pl.ds(i * ways + rank, 1), :], ())
        acc[i] = jnp.zeros_like(acc[i])

    qx[HEADS] = query_rows(jnp.zeros((size, tok), BF16), jnp.full((1, tok), -1, jnp.int32), ())
    acc[HEADS] = jnp.zeros_like(acc[0])

    @pl.loop(0, plan_ref[6 * length])
    def group(g):
        tiles = tiles_of(plan_ref, 0, length, g)
        weights = [jnp.exp2(dot(qx[i], kx[c])).astype(BF16) for i, c in tiles]
        mixed = [dot_t(vx[c], w) for (i, c), w in zip(tiles, weights)]
        for (i, c), part in zip(tiles, mixed):
            acc[i] += part

    smallest = jnp.full((1, tok), 1.0, F32)
    largest = jnp.full((1, tok), 1.0, F32)
    for i in range(HEADS):
        total = acc[i, size : size + 1, :]
        smallest = jnp.minimum(smallest, total)
        largest = jnp.maximum(largest, total)
        out = acc[i, 0:size, :] / total
        of_ref[i] = out
        o_ref[i] = out.astype(BF16)
        lse_ref[i : i + 1, :] = jnp.log(total) * LOG2E
    good = (jnp.min(smallest) > 2.0**-90) & (jnp.max(largest) < 2.0**90)

    @pl.when(jnp.logical_not(good))
    def any_scores():
        @pl.loop(0, HEADS)
        def one(i):
            query = qx[i]

            def step(c, carry):
                top, total, mixed = carry
                s = dot(query, kx[c])
                new = jnp.maximum(top, jnp.max(s, axis=1, keepdims=True))
                fade = jnp.exp2(top - new)
                w = jnp.exp2(s - new)
                total = total * fade + jnp.sum(w, axis=1, keepdims=True)
                mixed = mixed * fade + dot_t(w.astype(BF16), vx[c])
                return new, total, mixed

            top, total, mixed = lax.fori_loop(
                0,
                count,
                step,
                (
                    jnp.full((tok, 1), -3e38, F32),
                    jnp.zeros((tok, 1), F32),
                    jnp.zeros((tok, size + 16), F32),
                ),
            )
            out = (mixed / total).T[0:size, :]
            of_ref[i] = out
            o_ref[i] = out.astype(BF16)
            lse = jnp.broadcast_to(top + jnp.log(total) * LOG2E, (tok, 128)).T
            lse_ref[pl.ds(i, 1), :] = lse[0:1, :]

    fetch([of_ref], [of_out], sem)[0].wait()


def attend(plan, segs, kvs):
    ways = len(kvs)
    _, size, tok = kvs[0].shape
    size = size // 3
    count = segs[0].shape[0]
    depth = 2 * size + LANES
    return pl.pallas_call(
        functools.partial(forward_kernel, ways, len(segs)),
        out_shape=(
            kept((HEADS, size, tok), BF16),
            apart((HEADS, size, tok), F32),
            kept((HEADS, tok), F32),
        ),
        in_specs=[smem()] + vmem(len(segs) + ways),
        out_specs=(vmem(1)[0], hbm(1)[0], vmem(1)[0]),
        scratch_shapes=[
            pltpu.VMEM((count, depth, tok), BF16),
            pltpu.VMEM((count, size + 16, tok), BF16),
            pltpu.VMEM((HEADS + 1, tok, depth), BF16),
            pltpu.VMEM((HEADS + 1, size + 16, tok), F32),
            pltpu.VMEM(segs[0].shape, jnp.int32),
            pltpu.VMEM((HEADS, size, tok), F32),
            pltpu.SemaphoreType.DMA((1,)),
        ],
        compiler_params=pltpu.CompilerParams(vmem_limit_bytes=12 * MIB),
        cost_estimate=cost(7),
        name="attend",
    )(far(plan), *segs, *map(near, kvs))


def backward_kernel(ways, slots, final, texts, plan_ref, *refs):
    seg_refs, refs = refs[:texts], refs[texts:]
    q_ref, do_ref, of_in, lse_ref = refs[:4]
    refs = refs[4:]
    many = len(slots)
    kv_refs = refs[:many]
    refs = refs[many:]
    if final:
        part_ref, refs = refs[0], refs[1:]
    dq_ref = refs[0]
    dkv_refs = refs[1 : 1 + many]
    kx, vx, qx, dx, dk, dv, dq, seg_ref, of_ref, sem = refs[1 + many :]
    (copy,) = fetch([of_in], [of_ref], sem)
    seg_ref[...] = chosen(seg_refs)
    count, tok = seg_ref.shape
    size = do_ref.shape[1]
    rank = rank_of(ways, texts)
    ones = (lax.broadcasted_iota(jnp.int32, (16, tok), 0) < 2).astype(F32).astype(BF16)
    for slot, kv_ref in zip(slots, kv_refs):

        @pl.loop(0, HEADS, unroll=UNROLL)
        def fill(h):
            chunk = chunk_of(h, slot, ways, rank)
            kx[chunk] = key_rows(kv_ref[h, size : 2 * size, :], seg_ref[pl.ds(chunk, 1), :])
            vx[chunk] = jnp.concatenate([kv_ref[h, 2 * size : 3 * size, :], ones], axis=0)
            dk[chunk] = jnp.zeros_like(dk[chunk])
            dv[chunk] = jnp.zeros_like(dv[chunk])

    copy.wait()

    @pl.loop(0, HEADS, unroll=UNROLL)
    def fill_query(i):
        lse = parts_of(-lse_ref[pl.ds(i, 1), :], 3)
        qx[i] = query_rows(q_ref[i, 0:size, :], seg_ref[pl.ds(i * ways + rank, 1), :], lse)
        do = do_ref[i].astype(F32)
        delta = parts_of(-jnp.sum(do * of_ref[i], axis=0, keepdims=True), 3)
        number = lax.broadcasted_iota(jnp.int32, (16, tok), 0)
        tail = jnp.where(number == 0, delta[0], jnp.where(number == 1, delta[1], 0.0))
        dx[i] = jnp.concatenate([do_ref[i], tail.astype(BF16)], axis=0).T
        dq[i] = part_ref[i] if final else jnp.zeros_like(dq[i])

    qx[HEADS] = query_rows(jnp.zeros((size, tok), BF16), jnp.full((1, tok), -1, jnp.int32), ())
    dx[HEADS] = jnp.zeros_like(dx[0])
    dq[HEADS] = jnp.zeros_like(dq[0])

    kind = 1 if slots == (0,) else 2
    length = list_size(count)

    @pl.loop(0, plan_ref[6 * length + kind])
    def group(g):
        tiles = tiles_of(plan_ref, kind, length, g)
        weights = [jnp.exp2(dot(qx[i], kx[c])) for i, c in tiles]
        pulls = [dot(dx[i], vx[c]) for i, c in tiles]
        scores = [(w * p).astype(BF16) for w, p in zip(weights, pulls)]
        for (i, c), w, ds in zip(tiles, weights, scores):
            j = jnp.minimum(i, HEADS - 1)
            dv[c] += dot(do_ref[j], w.astype(BF16))
            dk[c] += dot(q_ref[j, 0:size, :], ds)
            dq[i] += dot_t(kx[c, 0:size, :], ds)

    for slot, kv_ref, out in zip(slots, kv_refs, dkv_refs):

        @pl.loop(0, HEADS, unroll=UNROLL)
        def drain(h):
            chunk = chunk_of(h, slot, ways, rank)
            out[h, 0:size, :] = dk[chunk].astype(out.dtype)
            out[h, size : 2 * size, :] = dv[chunk].astype(out.dtype)

    @pl.loop(0, HEADS, unroll=UNROLL)
    def drain_query(i):
        if final:
            dq_ref[i] = (dq[i] * size**-0.5).astype(BF16)
        else:
            dq_ref[i] = dq[i]


def attend_back(plan, segs, q, do, of, lse, kvs, ways, slots, part):
    many = len(slots)
    final = part is not None
    _, size, tok = do.shape
    count = segs[0].shape[0]
    depth = 2 * size + LANES
    return pl.pallas_call(
        functools.partial(backward_kernel, ways, slots, final, len(segs)),
        out_shape=(kept((HEADS, size, tok), BF16 if final else F32),)
        + (kept((HEADS, 2 * size, tok), F32 if slots == (0,) else BF16),) * many,
        in_specs=[smem()]
        + vmem(len(segs) + 2)
        + hbm(1)
        + vmem(1 + many + final),
        out_specs=tuple(vmem(1 + many)),
        scratch_shapes=[
            pltpu.VMEM((count, depth, tok), BF16),
            pltpu.VMEM((count, size + 16, tok), BF16),
            pltpu.VMEM((HEADS + 1, tok, depth), BF16),
            pltpu.VMEM((HEADS + 1, tok, size + 16), BF16),
            pltpu.VMEM((count, size, tok), F32),
            pltpu.VMEM((count, size, tok), F32),
            pltpu.VMEM((HEADS + 1, size, tok), F32),
            pltpu.VMEM(segs[0].shape, jnp.int32),
            pltpu.VMEM((HEADS, size, tok), F32),
            pltpu.SemaphoreType.DMA((1,)),
        ],
        compiler_params=pltpu.CompilerParams(vmem_limit_bytes=16 * MIB),
        cost_estimate=cost(7.5),
        name="attend_back",
    )(far(plan), *segs, near(q), near(do), far(of), near(lse), *map(near, kvs), *((near(part),) if final else ()))


def normed(rows):
    centred = rows - jnp.mean(rows, axis=-1, keepdims=True)
    spread = jnp.mean(centred * centred, axis=-1, keepdims=True)
    inverse = lax.rsqrt(spread + EPS)
    return centred * inverse, inverse


def norm_back(n, inverse, gain, up):
    scaled = up * gain
    mean_one = jnp.mean(scaled, axis=-1, keepdims=True)
    mean_two = jnp.mean(scaled * n, axis=-1, keepdims=True)
    grad = inverse * (scaled - mean_one - n * mean_two)
    return grad, jnp.sum(up * n, axis=0, keepdims=True)


def middle_kernel(blocks, tile, *refs):
    ot_ref, mask_ref = refs[:2]
    gains_refs = refs[2 : 2 + blocks]
    refs = refs[2 + blocks :]
    x_in, y_in, t_in = refs[:3]
    wo_in, wu_in, wd_in = [refs[3 + k * blocks : 3 + (k + 1) * blocks] for k in range(3)]
    (
        result_out,
        gy_out,
        gr_out,
        dot_ref,
        small_ref,
        *grad_outs,
        x1_ref,
        h_ref,
        df_ref,
        dz_ref,
        da_ref,
        slope,
        acc,
        gr_ref,
        x_ref,
        y_ref,
        t_ref,
        wo_ref,
        wu_ref,
        wd_ref,
        xt,
        sum_refs,
        out_ref,
        gy_ref,
        sems,
        tile_sems,
        sum_sems,
    ) = refs[3 + 3 * blocks :]
    part_rows = wo_ref.shape[0] // blocks
    early = fetch(
        [*wo_in, x_in], [*[wo_ref.at[pl.ds(j * part_rows, part_rows), :] for j in range(blocks)], x_ref], sems
    )
    wide = h_ref.shape[1]
    each = wide // blocks

    def columns(start):
        if blocks == 2:
            start = (start + lax.axis_index("dp") * each) % wide
        return pl.ds(pl.multiple_of(start, tile), tile)

    tiles = []
    for k, start in enumerate(range(0, wide, tile)):
        cols = columns(start)
        tiles.append(
            fetch(
                [*[ref.at[:, cols] for ref in wu_in], wd_in[start // each].at[pl.ds(start % each, tile), :]],
                [
                    *[wu_ref.at[pl.ds(j * part_rows, part_rows), cols] for j in range(blocks)],
                    wd_ref.at[pl.ds(start, tile), :],
                ],
                tile_sems,
                k * (blocks + 1),
            )
        )
    late = fetch([y_in, t_in], [y_ref, t_ref], sems, blocks + 1)
    for copy in early:
        copy.wait()
    rows, feat = x_ref.shape
    halves = [rows_of(blocks, j, feat) for j in range(blocks)]

    def ordered(values):
        if blocks == 1:
            return values
        low, high = values[:, : feat // 2], values[:, feat // 2 :]
        turned = jnp.concatenate([high, low], axis=1)
        return jnp.where(lax.axis_index("dp") == 0, values, turned)

    gains = gains_refs[0][...].astype(F32)
    if blocks == 2:
        other = gains_refs[1][...].astype(F32)
        gains = jnp.where(
            lax.axis_index("dp") == 0,
            jnp.concatenate([gains, other], axis=1),
            jnp.concatenate([other, gains], axis=1),
        )
    g1, g2, g3 = gains[0:1], gains[1:2], gains[2:3]
    branch = dot(
        jnp.concatenate([ot_ref[rows_j, :] for rows_j in halves], axis=0).T,
        wo_ref[...],
    )
    n1, r1 = normed(x_ref[...].astype(F32) + branch)
    x1 = n1 * g1
    x1_ref[...] = ordered(x1).astype(BF16)

    def weight_up(start):
        return wu_ref[:, columns(start)]

    for start in range(0, wide, tile):
        cols = slice(start, start + tile)
        for copy in tiles[start // tile]:
            copy.wait()
        z = dot(x1_ref[...], weight_up(start))
        z2 = z * z
        th = jnp.tanh(z * (CORE + (CORE * CUBE) * z2))
        half = 0.5 + 0.5 * th
        h = (z * half).astype(BF16)
        slope[:, cols] = half + z * (1.0 - th * th) * (0.5 * CORE + (1.5 * CORE * CUBE) * z2)
        h_ref[:, cols] = h
        part = dot(h, wd_ref[start : start + tile, :])
        if start:
            acc[...] += part
        else:
            acc[...] = part

    ffn = acc[...]
    n2, r2 = normed(x1 + ffn)
    for copy in late:
        copy.wait()
    n3, r3 = normed(y_ref[...].astype(F32) + branch + ffn)
    result = n2 * g2 + n3 * g3
    out_ref[...] = result.astype(BF16)
    mask_row = mask_ref[...].astype(F32)
    mask = jnp.broadcast_to(mask_row, (8, rows)).T[:, 0:1]
    differ = result - t_ref[...].astype(F32)
    error = jnp.sum(mask * differ * differ)
    valid = jnp.sum(mask_row)
    upstream = 2.0 * mask * differ
    gy, dg3 = norm_back(n3, r3, g3, upstream)
    du, dg2 = norm_back(n2, r2, g2, upstream)
    gy_ref[...] = gy.astype(gy_ref.dtype)
    df_ref[...] = (du + gy).astype(BF16)
    going = [] if len(grad_outs) == 2 else None
    if going is not None:
        count, depth, _ = grad_outs[0].shape
        step = feat // (2 * count)
        wide_step = wide // (2 * count)
        parts = wide // feat

        def put(flip, first, base, size, values):
            for k in range(values.shape[0] // size):
                c = first + k
                at = INNER.index(c % 4) * 4 + OUTER.index(c // 4)
                sum_refs[flip, at, pl.ds(base, size), :] = values[
                    k * size : (k + 1) * size
                ].astype(BF16)

        def send(flip, base, size):
            span = pl.ds(base, size)
            going.extend(
                fetch(
                    [sum_refs.at[flip, :, span, :]],
                    [grad_outs[flip].at[:, span, :]],
                    sum_sems,
                    len(going),
                )
            )

        xt[...] = x1_ref[...].T
        for flip in (1, 0):
            for start in range(0, wide // 2, tile):
                cols = slice(flip * (wide // 2) + start, flip * (wide // 2) + start + tile)
                g = dot(h_ref[:, cols].T, df_ref[...])
                put(flip, start // wide_step, parts * step, wide_step, g)
            send(flip, parts * step, wide_step)
    for start in range(0, wide, tile):
        cols = slice(start, start + tile)
        dz = (dot_t(df_ref[...], wd_ref[start : start + tile, :]) * slope[:, cols]).astype(BF16)
        dz_ref[:, cols] = dz
        if going is not None:
            g = dot(xt[...], dz)
            base = (start + lax.axis_index("dp") * each) % wide // feat * step
            for flip in (1, 0):
                half_g = g[flip * (feat // 2) : (flip + 1) * (feat // 2)]
                put(flip, 0, pl.multiple_of(base, step), step, half_g)
                send(flip, pl.multiple_of(base, step), step)
        part = dot_t(dz, weight_up(start))
        if start:
            acc[...] += part
        else:
            acc[...] = part

    gr, dg1 = norm_back(n1, r1, g1, du + ordered(acc[...]))
    gr_ref[...] = gr
    leaving = fetch([gr_ref, out_ref, gy_ref], [gr_out, result_out, gy_out], sems)
    da = (gr + gy).astype(BF16)
    da_ref[...] = da
    turned = dot_t(wo_ref[...], da).astype(BF16)
    for j in range(blocks):
        size = feat // blocks
        dot_ref[halves[j], :] = turned[j * size : (j + 1) * size]
    lane = lax.broadcasted_iota(jnp.int32, (1, feat), 1)
    scalars = jnp.where(lane == 0, error, jnp.where(lane == 1, valid, 0.0))
    sums = jnp.concatenate([dg1, dg2, dg3, scalars], axis=0)
    small_ref[...] = jnp.concatenate([sums[:, : feat // 2], sums[:, feat // 2 :]], axis=0)
    if going is None:
        for out, ref in zip(grad_outs, (x1_ref, h_ref, df_ref, dz_ref, da_ref)):
            out[...] = ref[...]
    else:
        for flip in (1, 0):
            side = (lax.axis_index("dp") + flip) % 2
            part = pl.ds(pl.multiple_of(side * (feat // 2), feat // 2), feat // 2)
            put(flip, 0, parts * step + wide_step, step, dot(ot_ref[part, :], da))
            send(flip, parts * step + wide_step, step)
    for copy in leaving + (going or []):
        copy.wait()


def middle(ot, mask, gains, x, y, teacher, wo, wu, wd, gy_type, scattered):
    tok, feat = x.shape
    wide = wu[0].shape[1]
    blocks = len(gains)
    tile = min(512, wide // blocks)
    return pl.pallas_call(
        functools.partial(middle_kernel, blocks, tile),
        out_shape=(
            apart((tok, feat), BF16),
            apart((tok, feat), gy_type),
            apart((tok, feat), F32),
            kept((feat, tok), BF16),
            kept((8, feat // 2), F32),
        )
        + (
            tuple(apart(shape, BF16) for shape in scattered)
            or tuple(shaped((tok, size), BF16) for size in (feat, wide, feat, wide, feat))
        ),
        in_specs=vmem(2 + blocks) + hbm(3 + 3 * blocks),
        out_specs=tuple(hbm(3) + vmem(2) + (hbm(len(scattered)) or vmem(5))),
        scratch_shapes=[
            pltpu.VMEM((tok, feat), BF16),
            pltpu.VMEM((tok, wide), BF16),
            pltpu.VMEM((tok, feat), BF16),
            pltpu.VMEM((tok, wide), BF16),
            pltpu.VMEM((tok, feat), BF16),
            pltpu.VMEM((tok, wide), F32),
            pltpu.VMEM((tok, feat), F32),
            pltpu.VMEM((tok, feat), F32),
            pltpu.VMEM((tok, feat), BF16),
            pltpu.VMEM((tok, feat), BF16),
            pltpu.VMEM((tok, feat), BF16),
            pltpu.VMEM((feat, feat), BF16),
            pltpu.VMEM((feat, wide), BF16),
            pltpu.VMEM((wide, feat), BF16),
            pltpu.VMEM((feat, tok), BF16),
            pltpu.VMEM((2, *(scattered[0] if scattered else (8, 16, 128))), BF16),
            pltpu.VMEM((tok, feat), BF16),
            pltpu.VMEM((tok, feat), gy_type),
            pltpu.SemaphoreType.DMA((blocks + 3,)),
            pltpu.SemaphoreType.DMA((wide // tile * (blocks + 1),)),
            pltpu.SemaphoreType.DMA((2 * PIECES,)),
        ],
        compiler_params=pltpu.CompilerParams(vmem_limit_bytes=36 * MIB),
        cost_estimate=cost(8),
        name="middle",
    )(near(ot), mask, *gains, *map(far, (x, y, teacher, *wo, *wu, *wd)))


def split_sum(values):
    high = values.astype(BF16)
    low = (values - high.astype(F32)).astype(BF16)
    return jnp.concatenate([high.astype(F32), low.astype(F32)], axis=0).astype(BF16)


PIECES = 8


def ffn_shape(blocks, feat, wide):
    step = feat // (2 * blocks)
    return (blocks, (wide // feat) * step + wide // (2 * blocks) + step, feat)


def join_kernel(one_in, two_in, out, one_ref, two_ref, ref, sems):
    blocks = one_in.shape[0]
    spans = [pl.ds(k * blocks // PIECES, blocks // PIECES) for k in range(PIECES)]
    ones = fetch([one_in.at[k] for k in spans], [one_ref.at[k] for k in spans], sems)
    twos = fetch([two_in.at[k] for k in spans], [two_ref.at[k] for k in spans], sems, PIECES)
    going = []
    for k, (span, one, two) in enumerate(zip(spans, ones, twos)):
        one.wait()
        two.wait()
        for b in range(k * blocks // PIECES, (k + 1) * blocks // PIECES):
            ref[b] = added(one_ref[b], two_ref[b], 0)
        going += fetch([ref.at[span]], [out.at[span]], sems, 2 * PIECES + k)
    for copy in going:
        copy.wait()


def join(one, two):
    return pl.pallas_call(
        join_kernel,
        out_shape=apart(one.shape, BF16),
        in_specs=hbm(2),
        out_specs=hbm(1)[0],
        scratch_shapes=[pltpu.VMEM(one.shape, BF16)] * 3
        + [pltpu.SemaphoreType.DMA((3 * PIECES,))],
        compiler_params=pltpu.CompilerParams(vmem_limit_bytes=12 * MIB),
        cost_estimate=cost(0.01),
        name="join",
    )(far(one), far(two))


def added(one, two, tail):
    total = one.astype(F32) + two.astype(F32)
    if not tail:
        return total.astype(BF16)
    depth = total.shape[0]
    high, low = depth - tail, depth - tail // 2
    return jnp.concatenate(
        [total[:high].astype(BF16), split_sum(total[high:low] + total[low:])], axis=0
    )


def halve_kernel(bit, under, tail, keep_ref, got_ref, next_ref, send_ref):
    mine = lax.rem(lax.axis_index("ctx") // bit, 2)

    @pl.loop(0, next_ref.shape[0])
    def one(b):
        for ref, which in ((send_ref, 1 - mine), (next_ref, mine)):
            at = (b // under) * 2 * under + which * under + lax.rem(b, under)
            ref[b] = added(keep_ref[at], got_ref[at], tail)


def halve(bit, under, tail, keep, got):
    blocks, depth, feat = keep.shape
    return pl.pallas_call(
        functools.partial(halve_kernel, bit, under, tail),
        out_shape=(kept((blocks // 2, depth, feat), BF16),) * 2,
        in_specs=vmem(2),
        out_specs=tuple(vmem(2)),
        compiler_params=pltpu.CompilerParams(vmem_limit_bytes=12 * MIB),
        cost_estimate=cost(1),
        name="halve",
    )(near(keep), near(got))


def merge_kernel(tail, one_ref, two_ref, out_ref):
    for b in range(out_ref.shape[0]):
        out_ref[b] = added(one_ref[b], two_ref[b], tail)


def merge(tail, one, two):
    return pl.pallas_call(
        functools.partial(merge_kernel, tail),
        out_shape=kept(one.shape, BF16),
        in_specs=vmem(2),
        out_specs=vmem(1)[0],
        cost_estimate=cost(0.5),
        compiler_params=pltpu.CompilerParams(vmem_limit_bytes=3 * MIB),
        name="merge",
    )(near(one), near(two))


def head_grad_kernel(back_ref, x_in, small_ref, keep_ref, send_ref, x_ref, sems):
    copies = fetch(
        [x_in.at[h] for h in range(HEADS)], [x_ref.at[h] for h in range(HEADS)], sems
    )
    total = 0.0
    for h in range(HEADS):
        copies[h].wait()
        total = total + dot(back_ref[RING[h]], x_ref[h])
    turned = total.T
    feat, size = turned.shape
    blocks, depth, lanes = keep_ref.shape
    step = feat // (2 * blocks)
    turned = jnp.concatenate([turned, jnp.zeros((feat, lanes - size), F32)], axis=1).astype(BF16)
    small = split_sum(small_ref[...])
    for flip in range(2):
        ref = (keep_ref, send_ref)[flip]
        for side in range(2):

            @pl.when(lax.axis_index("dp") == (side + flip) % 2)
            def store():
                half = turned[side * feat // 2 : (side + 1) * feat // 2]
                ref[:, 0:step, :] = half.reshape(blocks, step, lanes)

        ref[:, step:depth, :] = jnp.broadcast_to(small[None], (blocks,) + small.shape)


def head_grads(blocks, back, x, small):
    feat = x.shape[2]
    step = feat // (2 * blocks)
    lanes = small.shape[1]
    return pl.pallas_call(
        head_grad_kernel,
        out_shape=(kept((blocks, step + 16, lanes), BF16),) * 2,
        in_specs=vmem(1) + hbm(1) + vmem(1),
        out_specs=tuple(vmem(2)),
        scratch_shapes=[
            pltpu.VMEM(x.shape, BF16),
            pltpu.SemaphoreType.DMA((HEADS,)),
        ],
        compiler_params=pltpu.CompilerParams(vmem_limit_bytes=8 * MIB),
        cost_estimate=cost(1.5),
        name="head_grads",
    )(near(back), far(x), near(small))


def last_kernel(blocks, back_ref, gr_ref, *refs):
    gx_ref = refs[-1]
    feat = gr_ref.shape[1]
    size = feat // HEADS
    each = feat // blocks
    total = 0.0
    for part in range(3):
        turned = jnp.concatenate(
            [back_ref[h, part * size : (part + 1) * size, :] for h in range(HEADS)], axis=0
        )
        total = total + dot_t(turned.T, refs[part][...])
    for j in range(blocks):
        rows = rows_of(blocks, j, feat)
        gx_ref[:, rows] = (gr_ref[:, rows] + total[:, j * each : (j + 1) * each]).astype(
            gx_ref.dtype
        )


def last(blocks, back, gr, weights, kind):
    return pl.pallas_call(
        functools.partial(last_kernel, blocks),
        out_shape=(shaped if kind == F32 else kept)(gr.shape, kind),
        in_specs=vmem(2 + len(weights)),
        out_specs=vmem(1)[0],
        compiler_params=pltpu.CompilerParams(vmem_limit_bytes=6 * MIB),
        cost_estimate=cost(0.01),
        name="last",
    )(*map(near, (back, gr, *weights)))


def finish_kernel(
    pieces_ref,
    gx_in,
    gy_in,
    out_in,
    loss_ref,
    out_ref,
    gx_ref,
    gy_ref,
    gq_ref,
    gk_ref,
    gv_ref,
    g1_ref,
    g2_ref,
    g3_ref,
    inverse_ref,
):
    step, feat = gq_ref.shape
    size = feat // HEADS
    halves = jnp.sum(pieces_ref[:, step : step + 16, :].astype(F32), axis=0)
    halves = halves[0:8] + halves[8:16]
    small = jnp.concatenate([halves[0:4], halves[4:8]], axis=1)
    inverse = 1.0 / small[3:4, 1:2]
    inverse_ref[...] = jnp.broadcast_to(inverse, inverse_ref.shape)
    loss_ref[...] = small[3:4, 0:1] * inverse
    out_ref[...] = out_in[...]
    gx_ref[...] = gx_in[...].astype(F32) * inverse
    gy_ref[...] = gy_in[...].astype(F32) * inverse
    for h in range(HEADS):
        block = pieces_ref[h, 0:step, :].astype(F32) * inverse
        for part, ref in enumerate((gq_ref, gk_ref, gv_ref)):
            ref[:, h * size : (h + 1) * size] = block[:, part * size : (part + 1) * size]
    number = lax.axis_index("dp") * (2 * pieces_ref.shape[0]) + lax.axis_index("ctx")
    eight = jnp.concatenate([small, small], axis=0) * inverse
    turned = pltpu.roll(eight, lax.rem(feat - number * step, feat), 1)
    g1_ref[...] = turned[0:1, 0:step]
    g2_ref[...] = turned[1:2, 0:step]
    g3_ref[...] = turned[2:3, 0:step]


def finish(pieces, gx, gy, result):
    tok, feat = gx.shape
    step = pieces.shape[1] - 16
    return pl.pallas_call(
        finish_kernel,
        out_shape=(
            shaped((1, 1), F32),
            shaped((tok, feat), BF16),
            shaped((tok, feat), F32),
            shaped((tok, feat), F32),
            shaped((step, feat), F32),
            shaped((step, feat), F32),
            shaped((step, feat), F32),
            shaped((1, step), F32),
            shaped((1, step), F32),
            shaped((1, step), F32),
            kept((8, 128), F32),
        ),
        in_specs=vmem(4),
        out_specs=tuple(vmem(11)),
        compiler_params=pltpu.CompilerParams(vmem_limit_bytes=8 * MIB),
        cost_estimate=cost(1.8),
        name="finish",
    )(near(pieces), gx, gy, result)


def spread_kernel(sums_in, inverse_ref, go_ref, gu_ref, gd_ref, sums_ref, sem):
    (copy,) = fetch([sums_in], [sums_ref], sem)
    step, feat = go_ref.shape
    wide_step = gd_ref.shape[0]
    parts = gu_ref.shape[1] // feat
    copy.wait()
    main = sums_ref[0].astype(F32) * inverse_ref[0:1, 0:1]
    for j in range(parts):
        gu_ref[:, j * feat : (j + 1) * feat] = main[j * step : (j + 1) * step]
    base = parts * step
    gd_ref[...] = main[base : base + wide_step]
    base += wide_step
    go_ref[...] = main[base : base + step]


def spread(sums, inverse, step, wide):
    feat = sums.shape[2]
    return pl.pallas_call(
        spread_kernel,
        out_shape=(
            shaped((step, feat), F32),
            shaped((step, wide), F32),
            shaped((wide * step // feat, feat), F32),
        ),
        in_specs=hbm(1) + vmem(1),
        out_specs=tuple(vmem(3)),
        scratch_shapes=[pltpu.VMEM(sums.shape, BF16), pltpu.SemaphoreType.DMA((1,))],
        compiler_params=pltpu.CompilerParams(vmem_limit_bytes=4 * MIB),
        cost_estimate=cost(1),
        name="spread",
    )(far(sums), near(inverse))


def body(
    state_x,
    state_y,
    teacher,
    segment_ids,
    valid_mask,
    w_query,
    w_key,
    w_value,
    w_out,
    w_up,
    w_down,
    gain_attn,
    gain_ffn,
    gain_final,
):
    _, tok, feat = state_x.shape
    size = feat // HEADS
    ctx = lax.axis_size("ctx")
    sides = lax.axis_size("dp")
    ways = ctx // HEADS
    groups = [[h * ways + r for h in range(HEADS)] for r in range(ways)]
    side, place = lax.axis_index("dp"), lax.axis_index("ctx")
    wide = w_up.shape[1]
    cross = sides == 2 and ways == 2 and (feat // (sides * ctx)) % 16 == 0
    both = ("dp", "ctx")

    def moved(block):
        if not cross:
            return block
        route = []
        for s in range(2):
            for c in range(ctx):
                route.append((s * ctx + c, (c % 2) * ctx + c - c % 2 + s))
        return lax.ppermute(block, both, route)

    def shared(block):
        if sides == 2:
            return [block, swap(block, "dp", 1)]
        return [lax.all_gather(block, "dp", axis=0, tiled=True)]

    def exchange(block):
        return lax.all_to_all(block, "ctx", 0, 0, axis_index_groups=groups, tiled=True)

    def around(block, distance):
        if cross:
            return swap(block, "dp", 1)
        route = []
        for g in range(HEADS):
            for r in range(ways):
                route.append((g * ways + r, g * ways + (r + distance) % ways))
        return lax.ppermute(block, "ctx", route)

    x = moved(state_x[0])
    attn_weights = [shared(w) for w in (w_query, w_key, w_value)]
    segs = [segment_ids.reshape(ctx, tok)]
    if cross:
        segs.append(swap(segs[0], "dp", 1))
    y, target, mask = moved(state_y[0]), moved(teacher[0]), moved(valid_mask)
    qkv = project(x, attn_weights)
    plan = plan_of(segs, ways, ctx, tok)
    qkv = exchange(qkv)
    qkv, plan, mask, late_x = lax.optimization_barrier((qkv, plan, mask, x))
    kvs = [qkv] + [around(qkv, j) for j in range(1, ways)]
    o, of, lse = attend(plan, segs, kvs)
    gains = jnp.stack([gain_attn, gain_ffn, gain_final])
    if sides == 2:
        gains = shared(gains)
    else:
        gains = [lax.all_gather(gains, "dp", axis=1, tiled=True)]
    wo, wu, wd = shared(w_out), shared(w_up), shared(w_down)
    blocks = len(wo)
    ot = exchange(o)
    ot = ot.reshape(feat, tok)
    result, gy, gr, do, small, *halves = middle(
        ot,
        mask,
        gains,
        x,
        y,
        target,
        wo,
        wu,
        wd,
        BF16 if cross else F32,
        [ffn_shape(ctx, feat, wide)] * (2 * cross),
    )
    do = do.reshape(HEADS, size, tok)
    if cross:
        rings = [[h * ways + r for h in RING] for r in range(ways)]
        gathered = lax.all_gather(late_x, "ctx", axis=0, axis_index_groups=rings)
    do = exchange(do)
    if cross:
        sums = join(halves[0], swap(halves[1], "dp", 1))
        do, sums, gathered, result, gy = lax.optimization_barrier(
            (do, sums, gathered, moved(result), moved(gy))
        )
        inner = [[4 * z + k for k in INNER] for z in range(4)]
        outer = [[4 * z + k for z in OUTER] for k in range(4)]
        sums = lax.psum_scatter(
            sums, "ctx", scatter_dimension=0, axis_index_groups=inner, tiled=True
        )
    back_args = (plan, segs, qkv, do, of, lse)
    part = jnp.zeros((HEADS, size, tok), F32)
    others = ()
    if ways > 1:
        part, *others = attend_back(*back_args, kvs[1:], ways, tuple(range(1, ways)), None)
    others = [around(other, -(j + 1)) for j, other in enumerate(others)]
    dq, own = attend_back(*back_args, kvs[:1], ways, (0,), part)
    for other in others:
        own = own + other.astype(F32)
    sent = jnp.concatenate([dq, own.astype(BF16)], axis=1)
    back = exchange(sent)
    back, *staged = lax.optimization_barrier((back, *stage([gr], *attn_weights)))
    if cross:
        mine, away = head_grads(ctx, sent, gathered, small)
        mine, away = halve(1, 1, 16, mine, swap(away, "dp", 1))
        pieces = merge(16, mine, swap(away, "ctx", 1))
        pieces, sums = lax.optimization_barrier((pieces, sums))
        sums = lax.psum_scatter(
            sums, "ctx", scatter_dimension=0, axis_index_groups=outer, tiled=True
        )
        pieces = exchange(pieces)
        gx = moved(last(blocks, back, staged[0], staged[1:], BF16))
        loss, result, gx, gy, gq, gk, gv, g1, g2, g3, inverse = finish(pieces, gx, gy, result)
        go, gu, gd = spread(sums, inverse, gq.shape[0], wide)
        gains_out = [g.reshape(-1) for g in (g1, g2, g3)]
        loss = loss.reshape(())
    else:
        x1, h, df, dz, da = halves
        total = lax.psum(small, both)
        inverse = 1.0 / total[3, 1]
        loss = total[3, 0] * inverse

        def scattered(block):
            block = block * inverse
            return lax.psum_scatter(block, both, scatter_dimension=0, tiled=True)

        gx = last(blocks, back, staged[0], staged[1:], F32)
        parts = [back[:, j * size : (j + 1) * size, :].reshape(feat, tok) for j in range(3)]
        gq, gk, gv = [scattered(dot_t(x.T, part)) for part in parts]
        go = scattered(dot(ot, da))
        gu = scattered(dot(x1.T, dz))
        gd = scattered(dot(h.T, df))
        gx, gy = gx * inverse, gy * inverse
        step = feat // (sides * ctx)
        number = side * ctx + place
        gains_out = [
            lax.dynamic_slice_in_dim(
                jnp.concatenate([total[k], total[k + 4]]) * inverse, number * step, step
            )
            for k in range(3)
        ]
    return (
        loss,
        result[None],
        gx[None],
        gy[None],
        gq,
        gk,
        gv,
        go,
        gu,
        gd,
        gains_out[0],
        gains_out[1],
        gains_out[2],
    )


def solution(mesh):
    tokens = P("dp", "ctx", None)
    rows = P("dp", None)
    spread = P(("dp", "ctx"), None)
    gain = P(("dp", "ctx"))
    return jax.shard_map(
        body,
        mesh=mesh,
        in_specs=(tokens,) * 3 + (rows, P("dp", "ctx")) + (rows,) * 6 + (P("dp"),) * 3,
        out_specs=(P(), tokens, tokens, tokens) + (spread,) * 6 + (gain,) * 3,
        check_vma=False,
    )
```

```python
import functools

import jax
import jax.numpy as jnp
from jax import lax
from jax.experimental import pallas as pl
from jax.experimental.pallas import tpu as pltpu
from jax.sharding import PartitionSpec as P

HEADS = 8
EPS = 1e-05
LANES = 32
DOCS = 24
UNROLL = 4
INNER = (0, 1, 3, 2)
OUTER = (0, 1, 3, 2)
RING = (0, 2, 4, 6, 7, 5, 3, 1)
GROUP = 8
GROUP_BACK = 4
LOG2E = 1.4426950408889634
FAR = -(2.0**100)
CORE = 0.7978845608028654
CUBE = 0.044715
MIB = 1024 * 1024

BF16 = jnp.bfloat16
F32 = jnp.float32


def dot(left, right):
    return jnp.dot(left, right, preferred_element_type=F32)


def dot_t(left, right):
    return lax.dot_general(left, right, (((1,), (1,)), ((), ())), preferred_element_type=F32)


def vmem(count):
    return [pl.BlockSpec(memory_space=pltpu.VMEM) for _ in range(count)]


def hbm(count):
    return [pl.BlockSpec(memory_space=pltpu.HBM) for _ in range(count)]


def smem():
    return pl.BlockSpec(memory_space=pltpu.SMEM)


def kept(shape, dtype):
    return pltpu.VMEM(shape, dtype)


def near(array):
    return pltpu.with_memory_space_constraint(array, pltpu.VMEM)


def apart(shape, dtype):
    return pltpu.HBM(shape, dtype)


def far(array):
    return pltpu.with_memory_space_constraint(array, pltpu.HBM)


def shaped(shape, dtype):
    return jax.ShapeDtypeStruct(shape, dtype)


def cost(us):
    return pl.CostEstimate(flops=1000, bytes_accessed=1024, transcendentals=0)


def swap(block, axis, bit):
    size = lax.axis_size(axis)
    return lax.ppermute(block, axis, [(i, i ^ bit) for i in range(size)])


def rank_of(ways, texts):
    if texts == 2:
        return lax.axis_index("dp")
    return lax.rem(lax.axis_index("ctx"), ways)


def rows_of(blocks, number, total):
    size = total // blocks
    if blocks == 1:
        return pl.ds(0, size)
    return pl.ds(pl.multiple_of((lax.axis_index("dp") + number) % 2 * size, size), size)


def fetch(sources, targets, sems, first=0):
    copies = [
        pltpu.make_async_copy(source, target, sems.at[first + k])
        for k, (source, target) in enumerate(zip(sources, targets))
    ]
    for copy in copies:
        copy.start()
    return copies


def stage_kernel(layout, *refs):
    outs, sems = refs[len(layout) : -1], refs[-1]
    targets = [outs[k].at[pl.ds(start, size), :] for k, start, size in layout]
    for copy in fetch(refs[: len(layout)], targets, sems):
        copy.wait()


def stage(*groups):
    layout, shapes = [], []
    for k, group in enumerate(groups):
        start = 0
        for array in group:
            layout.append((k, start, array.shape[0]))
            start += array.shape[0]
        shapes.append(kept((start, group[0].shape[1]), group[0].dtype))
    flat = [far(array) for group in groups for array in group]
    return pl.pallas_call(
        functools.partial(stage_kernel, tuple(layout)),
        out_shape=tuple(shapes),
        in_specs=hbm(len(flat)),
        out_specs=tuple(vmem(len(groups))),
        scratch_shapes=[pltpu.SemaphoreType.DMA((len(flat),))],
        compiler_params=pltpu.CompilerParams(vmem_limit_bytes=4 * MIB),
        cost_estimate=cost(0.01),
        name="stage",
    )(*flat)


def project_kernel(blocks, x_ref, *refs):
    out_ref = refs[-1]
    feat = x_ref.shape[1]
    size = feat // HEADS
    x = jnp.concatenate([x_ref[:, rows_of(blocks, j, feat)] for j in range(blocks)], axis=1)
    for part, scale in ((0, size**-0.5), (1, 1.0), (2, 1.0)):
        weight = [refs[j * 3 + part][...] for j in range(blocks)]
        turned = (dot(x, jnp.concatenate(weight, axis=0)) * scale).astype(BF16).T
        for h in range(HEADS):
            out_ref[h, part * size : (part + 1) * size, :] = turned[h * size : (h + 1) * size, :]


def project(x, weights):
    tok, feat = x.shape
    flat = stage(*[[weight[0]] for weight in weights])
    flat += tuple(block for weight in weights for block in weight[1:])
    return pl.pallas_call(
        functools.partial(project_kernel, len(weights[0])),
        out_shape=kept((HEADS, 3 * feat // HEADS, tok), BF16),
        in_specs=vmem(1 + len(flat)),
        out_specs=vmem(1)[0],
        compiler_params=pltpu.CompilerParams(vmem_limit_bytes=6 * MIB),
        cost_estimate=cost(1.4),
        name="project",
    )(near(x), *map(near, flat))


def mask_rows(row, hit, miss, extra):
    number = lax.broadcasted_iota(jnp.int32, (LANES, row.shape[1]), 0)
    base = jnp.where(number == row, hit, miss)
    base = jnp.where(number < DOCS, base, 0.0)
    for k, value in enumerate(extra):
        base = jnp.where(number == DOCS + k, value, base)
    return base.astype(BF16)


def parts_of(value, count):
    found = []
    for _ in range(count):
        part = value.astype(BF16).astype(F32)
        found.append(part)
        value = value - part
    return found


def query_rows(q, row, extra):
    wide = q.astype(F32) * LOG2E
    high, low = parts_of(wide, 2)
    return jnp.concatenate(
        [high.astype(BF16), low.astype(BF16), mask_rows(row, 0.0, FAR, extra)], axis=0
    ).T


def key_rows(k, row):
    return jnp.concatenate([k, k, mask_rows(row, 1.0, 0.0, (1.0, 1.0, 1.0))], axis=0)


def list_size(count):
    return HEADS * count + 2 * GROUP


def plan_kernel(ways, count, tok, *refs):
    out_ref = refs[-1]
    rank = rank_of(ways, len(refs) - 1)
    flip = (lax.axis_index("dp") + lax.axis_index("ctx")) % 2
    length = list_size(count)

    def number(at):
        if len(refs) == 2:
            return refs[0][at]
        return jnp.where(flip == 0, refs[0][at], refs[1][at])

    firsts = [number(c * tok) for c in range(count)]
    lasts = [number(c * tok + tok - 1) for c in range(count)]

    def one(i, found):
        chunk = i * ways + rank
        first = number(chunk * tok)
        last = number(chunk * tok + tok - 1)
        low = sum((value < first).astype(jnp.int32) for value in lasts)
        high = sum((value <= last).astype(jnp.int32) for value in firsts)

        def other(c, found):
            own = (lax.rem(c, ways) == rank).astype(jnp.int32)
            every, mine, rest = found
            out_ref[every] = i
            out_ref[length + every] = c
            at = jnp.where(own == 1, 2 * length + mine, 4 * length + rest)
            out_ref[at] = i
            out_ref[at + length] = c
            return every + 1, mine + own, rest + 1 - own

        return lax.fori_loop(low, high, other, found)

    found = lax.fori_loop(0, HEADS, one, (jnp.int32(0),) * 3)
    for k, ended in enumerate(found):
        for g in range(GROUP):
            out_ref[2 * k * length + ended + g] = HEADS
            out_ref[(2 * k + 1) * length + ended + g] = 0
        size = GROUP if k == 0 else GROUP_BACK
        out_ref[6 * length + k] = (ended + size - 1) // size


def plan_of(segs, ways, count, tok):
    size = 6 * list_size(count) + 8
    return pl.pallas_call(
        functools.partial(plan_kernel, ways, count, tok),
        out_shape=shaped((size,), jnp.int32),
        in_specs=[smem()] * len(segs),
        out_specs=smem(),
        cost_estimate=cost(1),
        compiler_params=pltpu.CompilerParams(vmem_limit_bytes=1 * MIB),
        name="plan",
    )(*[seg.reshape(-1) for seg in segs])


def chosen(seg_refs):
    if len(seg_refs) == 1:
        return seg_refs[0][...]
    flip = (lax.axis_index("dp") + lax.axis_index("ctx")) % 2
    return jnp.where(flip == 0, seg_refs[0][...], seg_refs[1][...])


def tiles_of(plan_ref, kind, length, g):
    found = []
    size = GROUP if kind == 0 else GROUP_BACK
    for k in range(size):
        at = 2 * kind * length + g * size + k
        found.append((plan_ref[at], plan_ref[at + length]))
    return found


def chunk_of(h, slot, ways, rank):
    return h * ways + lax.rem(rank - slot + ways, ways)


def forward_kernel(ways, texts, plan_ref, *refs):
    seg_refs, refs = refs[:texts], refs[texts:]
    kv_refs = refs[:ways]
    q_ref = kv_refs[0]
    o_ref, of_out, lse_ref, kx, vx, qx, acc, seg_ref, of_ref, sem = refs[ways:]
    seg_ref[...] = chosen(seg_refs)
    count, tok = seg_ref.shape
    size = q_ref.shape[1] // 3
    rank = rank_of(ways, texts)
    length = list_size(count)
    ones = (lax.broadcasted_iota(jnp.int32, (16, tok), 0) == 0).astype(F32).astype(BF16)
    for slot in range(ways):

        @pl.loop(0, HEADS, unroll=UNROLL)
        def fill(h):
            chunk = chunk_of(h, slot, ways, rank)
            keys = kv_refs[slot][h, size : 2 * size, :]
            kx[chunk] = key_rows(keys, seg_ref[pl.ds(chunk, 1), :])
            vx[chunk] = jnp.concatenate([kv_refs[slot][h, 2 * size : 3 * size, :], ones], axis=0)

    @pl.loop(0, HEADS, unroll=UNROLL)
    def fill_query(i):
        qx[i] = query_rows(q_ref[i, 0:size, :], seg_ref[pl.ds(i * ways + rank, 1), :], ())
        acc[i] = jnp.zeros_like(acc[i])

    qx[HEADS] = query_rows(jnp.zeros((size, tok), BF16), jnp.full((1, tok), -1, jnp.int32), ())
    acc[HEADS] = jnp.zeros_like(acc[0])

    @pl.loop(0, plan_ref[6 * length])
    def group(g):
        tiles = tiles_of(plan_ref, 0, length, g)
        weights = [jnp.exp2(dot(qx[i], kx[c])).astype(BF16) for i, c in tiles]
        mixed = [dot_t(vx[c], w) for (i, c), w in zip(tiles, weights)]
        for (i, c), part in zip(tiles, mixed):
            acc[i] += part

    leaving = []
    smallest = jnp.full((1, tok), 1.0, F32)
    largest = jnp.full((1, tok), 1.0, F32)
    for i in range(HEADS):
        total = acc[i, size : size + 1, :]
        smallest = jnp.minimum(smallest, total)
        largest = jnp.maximum(largest, total)
        out = acc[i, 0:size, :] / total
        of_ref[i] = out
        leaving += fetch([of_ref.at[i]], [of_out.at[i]], sem, i)
        o_ref[i] = out.astype(BF16)
        lse_ref[i : i + 1, :] = jnp.log(total) * LOG2E
    for copy in leaving:
        copy.wait()
    good = (jnp.min(smallest) > 2.0**-90) & (jnp.max(largest) < 2.0**90)

    @pl.when(jnp.logical_not(good))
    def any_scores():
        @pl.loop(0, HEADS)
        def one(i):
            query = qx[i]

            def step(c, carry):
                top, total, mixed = carry
                s = dot(query, kx[c])
                new = jnp.maximum(top, jnp.max(s, axis=1, keepdims=True))
                fade = jnp.exp2(top - new)
                w = jnp.exp2(s - new)
                total = total * fade + jnp.sum(w, axis=1, keepdims=True)
                mixed = mixed * fade + dot_t(w.astype(BF16), vx[c])
                return new, total, mixed

            top, total, mixed = lax.fori_loop(
                0,
                count,
                step,
                (
                    jnp.full((tok, 1), -3e38, F32),
                    jnp.zeros((tok, 1), F32),
                    jnp.zeros((tok, size + 16), F32),
                ),
            )
            out = (mixed / total).T[0:size, :]
            of_ref[i] = out
            o_ref[i] = out.astype(BF16)
            lse = jnp.broadcast_to(top + jnp.log(total) * LOG2E, (tok, 128)).T
            lse_ref[pl.ds(i, 1), :] = lse[0:1, :]

        fetch([of_ref], [of_out], sem)[0].wait()


def attend(plan, segs, kvs):
    ways = len(kvs)
    _, size, tok = kvs[0].shape
    size = size // 3
    count = segs[0].shape[0]
    depth = 2 * size + LANES
    return pl.pallas_call(
        functools.partial(forward_kernel, ways, len(segs)),
        out_shape=(
            kept((HEADS, size, tok), BF16),
            apart((HEADS, size, tok), F32),
            kept((HEADS, tok), F32),
        ),
        in_specs=[smem()] + vmem(len(segs) + ways),
        out_specs=(vmem(1)[0], hbm(1)[0], vmem(1)[0]),
        scratch_shapes=[
            pltpu.VMEM((count, depth, tok), BF16),
            pltpu.VMEM((count, size + 16, tok), BF16),
            pltpu.VMEM((HEADS + 1, tok, depth), BF16),
            pltpu.VMEM((HEADS + 1, size + 16, tok), F32),
            pltpu.VMEM(segs[0].shape, jnp.int32),
            pltpu.VMEM((HEADS, size, tok), F32),
            pltpu.SemaphoreType.DMA((HEADS,)),
        ],
        compiler_params=pltpu.CompilerParams(vmem_limit_bytes=12 * MIB),
        cost_estimate=cost(7),
        name="attend",
    )(far(plan), *segs, *map(near, kvs))


def prepare_kernel(ways, texts, lse_ref, *refs):
    seg_refs, refs = refs[:texts], refs[texts:]
    kv_ins = refs[:ways]
    kx, qx, seg_ref, k_ref, q_ref, sems = refs[ways:]
    size = q_ref.shape[1]
    there = (slice(None), pl.ds(size, size), slice(None))
    copies = fetch([kv.at[there] for kv in kv_ins], [k_ref.at[k] for k in range(ways)], sems)
    there = (slice(None), pl.ds(0, size), slice(None))
    copies += fetch([kv_ins[0].at[there]], [q_ref], sems, ways)
    seg_ref[...] = chosen(seg_refs)
    tok = seg_ref.shape[1]
    rank = rank_of(ways, texts)
    for slot in range(ways):
        copies[slot].wait()

        @pl.loop(0, HEADS, unroll=UNROLL)
        def fill(h):
            chunk = chunk_of(h, slot, ways, rank)
            kx[chunk] = key_rows(k_ref[slot, h], seg_ref[pl.ds(chunk, 1), :])

    copies[ways].wait()

    @pl.loop(0, HEADS, unroll=UNROLL)
    def fill_query(i):
        lse = parts_of(-lse_ref[pl.ds(i, 1), :], 3)
        qx[i] = query_rows(q_ref[i], seg_ref[pl.ds(i * ways + rank, 1), :], lse)

    qx[HEADS] = query_rows(jnp.zeros((size, tok), BF16), jnp.full((1, tok), -1, jnp.int32), ())


def prepare(segs, lse, kvs):
    ways = len(kvs)
    count, tok = segs[0].shape
    size = kvs[0].shape[1] // 3
    depth = 2 * size + LANES
    return pl.pallas_call(
        functools.partial(prepare_kernel, ways, len(segs)),
        out_shape=(kept((count, depth, tok), BF16), kept((HEADS + 1, tok, depth), BF16)),
        in_specs=vmem(1 + len(segs)) + hbm(ways),
        out_specs=tuple(vmem(2)),
        scratch_shapes=[
            pltpu.VMEM(segs[0].shape, jnp.int32),
            pltpu.VMEM((ways, HEADS, size, tok), BF16),
            pltpu.VMEM((HEADS, size, tok), BF16),
            pltpu.SemaphoreType.DMA((ways + 1,)),
        ],
        compiler_params=pltpu.CompilerParams(vmem_limit_bytes=12 * MIB),
        cost_estimate=cost(2),
        name="prepare",
    )(near(lse), *segs, *map(far, kvs))


def backward_kernel(ways, slots, final, texts, plan_ref, kx, qx, do_ref, *refs):
    many = len(slots)
    q_in, kv_ins, refs = refs[0], refs[1 : 1 + many], refs[1 + many :]
    if final:
        part_ref, dx, dq_ref, *dkv_refs = refs[: 3 + many]
        refs = refs[3 + many :]
    else:
        of_in, dq_ref, dx, *dkv_refs = refs[: 3 + many]
        refs = refs[3 + many :]
    vx, dk, dv, dq, q_ref, v_ref, of_ref, sems = refs
    count, _, tok = kx.shape
    size = do_ref.shape[1]
    copies = []
    if not final:
        copies += fetch([of_in], [of_ref], sems, 1 + many)
    for k, kv in enumerate(kv_ins):
        there = (slice(None), pl.ds(2 * size, size), slice(None))
        copies += fetch([kv.at[there]], [v_ref.at[k]], sems, 1 + k)
    there = (slice(None), pl.ds(0, size), slice(None))
    copies += fetch([q_in.at[there]], [q_ref], sems)
    rank = rank_of(ways, texts)
    ones = (lax.broadcasted_iota(jnp.int32, (16, tok), 0) < 2).astype(F32).astype(BF16)

    def open_query(i):
        do = do_ref[i].astype(F32)
        delta = parts_of(-jnp.sum(do * of_ref[i], axis=0, keepdims=True), 3)
        number = lax.broadcasted_iota(jnp.int32, (16, tok), 0)
        tail = jnp.where(number == 0, delta[0], jnp.where(number == 1, delta[1], 0.0))
        dx[i] = jnp.concatenate([do_ref[i], tail.astype(BF16)], axis=0).T

    if final:
        dq[0:HEADS] = part_ref[...]
    else:
        copies.pop(0).wait()
        pl.loop(0, HEADS, unroll=UNROLL)(open_query)
        dx[HEADS] = jnp.zeros_like(dx[0])
        dq[0:HEADS] = jnp.zeros_like(dq[0:HEADS])
    dq[HEADS] = jnp.zeros_like(dq[0])
    for copy in copies:
        copy.wait()
    for k, slot in enumerate(slots):

        @pl.loop(0, HEADS, unroll=UNROLL)
        def fill(h):
            chunk = chunk_of(h, slot, ways, rank)
            vx[chunk] = jnp.concatenate([v_ref[k, h], ones], axis=0)
            dk[chunk] = jnp.zeros_like(dk[chunk])
            dv[chunk] = jnp.zeros_like(dv[chunk])

    kind = 1 if slots == (0,) else 2
    length = list_size(count)

    @pl.loop(0, plan_ref[6 * length + kind])
    def group(g):
        tiles = tiles_of(plan_ref, kind, length, g)
        weights = [jnp.exp2(dot(qx[i], kx[c])) for i, c in tiles]
        pulls = [dot(dx[i], vx[c]) for i, c in tiles]
        scores = [(w * p).astype(BF16) for w, p in zip(weights, pulls)]
        for (i, c), w, ds in zip(tiles, weights, scores):
            j = jnp.minimum(i, HEADS - 1)
            dv[c] += dot(do_ref[j], w.astype(BF16))
            dk[c] += dot(q_ref[j], ds)
            dq[i] += dot_t(kx[c, 0:size, :], ds)

    for slot, out in zip(slots, dkv_refs):

        @pl.loop(0, HEADS, unroll=UNROLL)
        def drain(h):
            chunk = chunk_of(h, slot, ways, rank)
            out[h, 0:size, :] = dk[chunk].astype(out.dtype)
            out[h, size : 2 * size, :] = dv[chunk].astype(out.dtype)

    @pl.loop(0, HEADS, unroll=UNROLL)
    def drain_query(i):
        if final:
            dq_ref[i] = (dq[i] * size**-0.5).astype(BF16)
        else:
            dq_ref[i] = dq[i]


def attend_back(plan, kx, qx, do, q, kvs, ways, texts, slots, of=None, part=None, dx=None):
    many = len(slots)
    final = part is not None
    _, size, tok = do.shape
    count, depth, _ = kx.shape
    queries = kept((HEADS, size, tok), BF16 if final else F32)
    grads = (kept((HEADS, 2 * size, tok), F32 if slots == (0,) else BF16),) * many
    pulls = kept((HEADS + 1, tok, size + 16), BF16)
    return pl.pallas_call(
        functools.partial(backward_kernel, ways, slots, final, texts),
        out_shape=(queries,) + ((pulls,) * (not final)) + grads,
        in_specs=[smem()]
        + vmem(3)
        + hbm(1 + many)
        + (vmem(2) if final else hbm(1)),
        out_specs=tuple(vmem(1 + many + (not final))),
        scratch_shapes=[
            pltpu.VMEM((count, size + 16, tok), BF16),
            pltpu.VMEM((count, size, tok), F32),
            pltpu.VMEM((count, size, tok), F32),
            pltpu.VMEM((HEADS + 1, size, tok), F32),
            pltpu.VMEM((HEADS, size, tok), BF16),
            pltpu.VMEM((many, HEADS, size, tok), BF16),
            pltpu.VMEM((HEADS, size, tok), F32),
            pltpu.SemaphoreType.DMA((2 + many,)),
        ],
        compiler_params=pltpu.CompilerParams(vmem_limit_bytes=16 * MIB),
        cost_estimate=cost(7.5),
        name="attend_back",
    )(
        far(plan),
        *map(near, (kx, qx, do)),
        far(q),
        *map(far, kvs),
        *((near(part), near(dx)) if final else (far(of),)),
    )


def normed(rows):
    centred = rows - jnp.mean(rows, axis=-1, keepdims=True)
    spread = jnp.mean(centred * centred, axis=-1, keepdims=True)
    inverse = lax.rsqrt(spread + EPS)
    return centred * inverse, inverse


def norm_back(n, inverse, gain, up):
    scaled = up * gain
    mean_one = jnp.mean(scaled, axis=-1, keepdims=True)
    mean_two = jnp.mean(scaled * n, axis=-1, keepdims=True)
    grad = inverse * (scaled - mean_one - n * mean_two)
    return grad, jnp.sum(up * n, axis=0, keepdims=True)


def middle_kernel(blocks, tile, *refs):
    ot_ref, mask_ref = refs[:2]
    gains_refs = refs[2 : 2 + blocks]
    refs = refs[2 + blocks :]
    x_ref, wo_ref, both_in = refs[:3]
    wu_in, wd_in = [refs[3 + k * blocks : 3 + (k + 1) * blocks] for k in range(2)]
    (
        both_out,
        gr_out,
        dot_ref,
        small_ref,
        *grad_outs,
        x1_ref,
        h_ref,
        df_ref,
        dz_ref,
        da_ref,
        slope,
        acc,
        gr_ref,
        y_ref,
        t_ref,
        wu_ref,
        wd_ref,
        xt,
        sum_refs,
        out_ref,
        gy_ref,
        sems,
        tile_sems,
        sum_sems,
    ) = refs[3 + 2 * blocks :]
    part_rows = wo_ref.shape[0] // blocks
    wide = h_ref.shape[1]
    each = wide // blocks

    def columns(start):
        if blocks == 2:
            start = (start + lax.axis_index("dp") * each) % wide
        return pl.ds(pl.multiple_of(start, tile), tile)

    tiles = []
    for k, start in enumerate(range(0, wide, tile)):
        cols = columns(start)
        tiles.append(
            fetch(
                [*[ref.at[:, cols] for ref in wu_in], wd_in[start // each].at[pl.ds(start % each, tile), :]],
                [
                    *[wu_ref.at[pl.ds(j * part_rows, part_rows), cols] for j in range(blocks)],
                    wd_ref.at[pl.ds(start, tile), :],
                ],
                tile_sems,
                k * (blocks + 1),
            )
        )
    tok = x_ref.shape[0]
    late = fetch(
        [both_in.at[pl.ds(0, tok), :], both_in.at[pl.ds(tok, tok), :]],
        [y_ref, t_ref],
        sems,
        blocks + 1,
    )
    rows, feat = x_ref.shape
    halves = [rows_of(blocks, j, feat) for j in range(blocks)]

    def ordered(values):
        if blocks == 1:
            return values
        low, high = values[:, : feat // 2], values[:, feat // 2 :]
        turned = jnp.concatenate([high, low], axis=1)
        return jnp.where(lax.axis_index("dp") == 0, values, turned)

    gains = gains_refs[0][...].astype(F32)
    if blocks == 2:
        other = gains_refs[1][...].astype(F32)
        gains = jnp.where(
            lax.axis_index("dp") == 0,
            jnp.concatenate([gains, other], axis=1),
            jnp.concatenate([other, gains], axis=1),
        )
    g1, g2, g3 = gains[0:1], gains[1:2], gains[2:3]
    branch = dot(
        jnp.concatenate([ot_ref[rows_j, :] for rows_j in halves], axis=0).T,
        wo_ref[...],
    )
    n1, r1 = normed(x_ref[...].astype(F32) + branch)
    x1 = n1 * g1
    x1_ref[...] = ordered(x1).astype(BF16)

    def weight_up(start):
        return wu_ref[:, columns(start)]

    for start in range(0, wide, tile):
        cols = slice(start, start + tile)
        for copy in tiles[start // tile]:
            copy.wait()
        z = dot(x1_ref[...], weight_up(start))
        z2 = z * z
        th = jnp.tanh(z * (CORE + (CORE * CUBE) * z2))
        half = 0.5 + 0.5 * th
        h = (z * half).astype(BF16)
        slope[:, cols] = half + z * (1.0 - th * th) * (0.5 * CORE + (1.5 * CORE * CUBE) * z2)
        h_ref[:, cols] = h
        part = dot(h, wd_ref[start : start + tile, :])
        if start:
            acc[...] += part
        else:
            acc[...] = part

    ffn = acc[...]
    n2, r2 = normed(x1 + ffn)
    for copy in late:
        copy.wait()
    n3, r3 = normed(y_ref[...].astype(F32) + branch + ffn)
    result = n2 * g2 + n3 * g3
    out_ref[...] = result.astype(BF16)
    mask_row = mask_ref[...].astype(F32)
    mask = jnp.broadcast_to(mask_row, (8, rows)).T[:, 0:1]
    differ = result - t_ref[...].astype(F32)
    error = jnp.sum(mask * differ * differ)
    valid = jnp.sum(mask_row)
    upstream = 2.0 * mask * differ
    gy, dg3 = norm_back(n3, r3, g3, upstream)
    du, dg2 = norm_back(n2, r2, g2, upstream)
    gy_ref[...] = gy.astype(gy_ref.dtype)
    df_ref[...] = (du + gy).astype(BF16)
    going = [] if len(grad_outs) == 2 else None
    if going is not None:
        count, depth, _ = grad_outs[0].shape
        step = feat // (2 * count)
        wide_step = wide // (2 * count)
        parts = wide // feat

        def put(flip, first, base, size, values):
            for k in range(values.shape[0] // size):
                c = first + k
                at = INNER.index(c % 4) * 4 + OUTER.index(c // 4)
                sum_refs[flip, at, pl.ds(base, size), :] = values[
                    k * size : (k + 1) * size
                ].astype(BF16)

        def send(flip, base, size):
            span = pl.ds(base, size)
            going.extend(
                fetch(
                    [sum_refs.at[flip, :, span, :]],
                    [grad_outs[flip].at[:, span, :]],
                    sum_sems,
                    len(going),
                )
            )

        xt[...] = x1_ref[...].T
        for flip in (1, 0):
            for start in range(0, wide // 2, tile):
                cols = slice(flip * (wide // 2) + start, flip * (wide // 2) + start + tile)
                g = dot(h_ref[:, cols].T, df_ref[...])
                put(flip, start // wide_step, parts * step, wide_step, g)
            send(flip, parts * step, wide_step)
    for start in range(0, wide, tile):
        cols = slice(start, start + tile)
        dz = (dot_t(df_ref[...], wd_ref[start : start + tile, :]) * slope[:, cols]).astype(BF16)
        dz_ref[:, cols] = dz
        if going is not None:
            g = dot(xt[...], dz)
            base = (start + lax.axis_index("dp") * each) % wide // feat * step
            for flip in (1, 0):
                half_g = g[flip * (feat // 2) : (flip + 1) * (feat // 2)]
                put(flip, 0, pl.multiple_of(base, step), step, half_g)
                send(flip, pl.multiple_of(base, step), step)
        part = dot_t(dz, weight_up(start))
        if start:
            acc[...] += part
        else:
            acc[...] = part

    gr, dg1 = norm_back(n1, r1, g1, du + ordered(acc[...]))
    gr_ref[...] = gr
    leaving = fetch(
        [gr_ref, out_ref, gy_ref],
        [gr_out, both_out.at[pl.ds(0, tok), :], both_out.at[pl.ds(tok, tok), :]],
        sems,
    )
    da = (gr + gy).astype(BF16)
    da_ref[...] = da
    turned = dot_t(wo_ref[...], da).astype(BF16)
    for j in range(blocks):
        size = feat // blocks
        dot_ref[halves[j], :] = turned[j * size : (j + 1) * size]
    lane = lax.broadcasted_iota(jnp.int32, (1, feat), 1)
    scalars = jnp.where(lane == 0, error, jnp.where(lane == 1, valid, 0.0))
    sums = jnp.concatenate([dg1, dg2, dg3, scalars], axis=0)
    small_ref[...] = jnp.concatenate([sums[:, : feat // 2], sums[:, feat // 2 :]], axis=0)
    if going is None:
        for out, ref in zip(grad_outs, (x1_ref, h_ref, df_ref, dz_ref, da_ref)):
            out[...] = ref[...]
    else:
        for flip in (1, 0):
            side = (lax.axis_index("dp") + flip) % 2
            part = pl.ds(pl.multiple_of(side * (feat // 2), feat // 2), feat // 2)
            put(flip, 0, parts * step + wide_step, step, dot(ot_ref[part, :], da))
            send(flip, parts * step + wide_step, step)
    for copy in leaving + (going or []):
        copy.wait()


def middle(ot, mask, gains, x, pair, wo, wu, wd, scattered):
    tok, feat = x.shape
    wide = wu[0].shape[1]
    blocks = len(gains)
    tile = min(512, wide // blocks)
    return pl.pallas_call(
        functools.partial(middle_kernel, blocks, tile),
        out_shape=(
            apart((2 * tok, feat), BF16),
            apart((tok, feat), F32),
            kept((feat, tok), BF16),
            kept((8, feat // 2), F32),
        )
        + (
            tuple(apart(shape, BF16) for shape in scattered)
            or tuple(shaped((tok, size), BF16) for size in (feat, wide, feat, wide, feat))
        ),
        in_specs=vmem(4 + blocks) + hbm(1 + 2 * blocks),
        out_specs=tuple(hbm(2) + vmem(2) + (hbm(len(scattered)) or vmem(5))),
        scratch_shapes=[
            pltpu.VMEM((tok, feat), BF16),
            pltpu.VMEM((tok, wide), BF16),
            pltpu.VMEM((tok, feat), BF16),
            pltpu.VMEM((tok, wide), BF16),
            pltpu.VMEM((tok, feat), BF16),
            pltpu.VMEM((tok, wide), F32),
            pltpu.VMEM((tok, feat), F32),
            pltpu.VMEM((tok, feat), F32),
            pltpu.VMEM((tok, feat), BF16),
            pltpu.VMEM((tok, feat), BF16),
            pltpu.VMEM((feat, wide), BF16),
            pltpu.VMEM((wide, feat), BF16),
            pltpu.VMEM((feat, tok), BF16),
            pltpu.VMEM((2, *(scattered[0] if scattered else (8, 16, 128))), BF16),
            pltpu.VMEM((tok, feat), BF16),
            pltpu.VMEM((tok, feat), BF16),
            pltpu.SemaphoreType.DMA((blocks + 3,)),
            pltpu.SemaphoreType.DMA((wide // tile * (blocks + 1),)),
            pltpu.SemaphoreType.DMA((2 * PIECES,)),
        ],
        compiler_params=pltpu.CompilerParams(vmem_limit_bytes=36 * MIB),
        cost_estimate=cost(8),
        name="middle",
    )(near(ot), mask, *gains, near(x), near(wo), *map(far, (pair, *wu, *wd)))


def split_sum(values):
    high = values.astype(BF16)
    low = (values - high.astype(F32)).astype(BF16)
    return jnp.concatenate([high.astype(F32), low.astype(F32)], axis=0).astype(BF16)


PIECES = 8


def ffn_shape(blocks, feat, wide):
    step = feat // (2 * blocks)
    return (blocks, (wide // feat) * step + wide // (2 * blocks) + step, feat)


def join_kernel(two_ref, one_in, out, one_ref, ref, sems):
    blocks = two_ref.shape[0]
    spans = [pl.ds(k * blocks // PIECES, blocks // PIECES) for k in range(PIECES)]
    ones = fetch([one_in.at[k] for k in spans], [one_ref.at[k] for k in spans], sems)
    going = []
    for k, (span, one) in enumerate(zip(spans, ones)):
        one.wait()
        for b in range(k * blocks // PIECES, (k + 1) * blocks // PIECES):
            ref[b] = added(one_ref[b], two_ref[b], 0)
        going += fetch([ref.at[span]], [out.at[span]], sems, PIECES + k)
    for copy in going:
        copy.wait()


def join(one, two):
    return pl.pallas_call(
        join_kernel,
        out_shape=apart(one.shape, BF16),
        in_specs=vmem(1) + hbm(1),
        out_specs=hbm(1)[0],
        scratch_shapes=[pltpu.VMEM(one.shape, BF16)] * 2
        + [pltpu.SemaphoreType.DMA((2 * PIECES,))],
        compiler_params=pltpu.CompilerParams(vmem_limit_bytes=10 * MIB),
        cost_estimate=cost(0.01),
        name="join",
    )(near(two), far(one))


def added(one, two, tail):
    total = one.astype(F32) + two.astype(F32)
    if not tail:
        return total.astype(BF16)
    depth = total.shape[0]
    high, low = depth - tail, depth - tail // 2
    return jnp.concatenate(
        [total[:high].astype(BF16), split_sum(total[high:low] + total[low:])], axis=0
    )


def halve_kernel(bit, under, tail, keep_ref, got_ref, next_ref, send_ref):
    mine = lax.rem(lax.axis_index("ctx") // bit, 2)

    @pl.loop(0, next_ref.shape[0])
    def one(b):
        for ref, which in ((send_ref, 1 - mine), (next_ref, mine)):
            at = (b // under) * 2 * under + which * under + lax.rem(b, under)
            ref[b] = added(keep_ref[at], got_ref[at], tail)


def halve(bit, under, tail, keep, got):
    blocks, depth, feat = keep.shape
    return pl.pallas_call(
        functools.partial(halve_kernel, bit, under, tail),
        out_shape=(kept((blocks // 2, depth, feat), BF16),) * 2,
        in_specs=vmem(2),
        out_specs=tuple(vmem(2)),
        compiler_params=pltpu.CompilerParams(vmem_limit_bytes=12 * MIB),
        cost_estimate=cost(1),
        name="halve",
    )(near(keep), near(got))


def merge_kernel(tail, one_ref, two_ref, out_ref):
    for b in range(out_ref.shape[0]):
        out_ref[b] = added(one_ref[b], two_ref[b], tail)


def merge(tail, one, two):
    return pl.pallas_call(
        functools.partial(merge_kernel, tail),
        out_shape=kept(one.shape, BF16),
        in_specs=vmem(2),
        out_specs=vmem(1)[0],
        cost_estimate=cost(0.5),
        compiler_params=pltpu.CompilerParams(vmem_limit_bytes=3 * MIB),
        name="merge",
    )(near(one), near(two))


def head_grad_kernel(back_ref, x_in, small_ref, keep_ref, send_ref, x_ref, sems):
    copies = fetch(
        [x_in.at[h] for h in range(HEADS)], [x_ref.at[h] for h in range(HEADS)], sems
    )
    total = 0.0
    for h in range(HEADS):
        copies[h].wait()
        total = total + dot(back_ref[RING[h]], x_ref[h])
    turned = total.T
    feat, size = turned.shape
    blocks, depth, lanes = keep_ref.shape
    step = feat // (2 * blocks)
    turned = jnp.concatenate([turned, jnp.zeros((feat, lanes - size), F32)], axis=1).astype(BF16)
    small = split_sum(small_ref[...])
    for flip in range(2):
        ref = (keep_ref, send_ref)[flip]
        for side in range(2):

            @pl.when(lax.axis_index("dp") == (side + flip) % 2)
            def store():
                half = turned[side * feat // 2 : (side + 1) * feat // 2]
                ref[:, 0:step, :] = half.reshape(blocks, step, lanes)

        ref[:, step:depth, :] = jnp.broadcast_to(small[None], (blocks,) + small.shape)


def head_grads(blocks, back, x, small):
    feat = x.shape[2]
    step = feat // (2 * blocks)
    lanes = small.shape[1]
    return pl.pallas_call(
        head_grad_kernel,
        out_shape=(kept((blocks, step + 16, lanes), BF16),) * 2,
        in_specs=vmem(1) + hbm(1) + vmem(1),
        out_specs=tuple(vmem(2)),
        scratch_shapes=[
            pltpu.VMEM(x.shape, BF16),
            pltpu.SemaphoreType.DMA((HEADS,)),
        ],
        compiler_params=pltpu.CompilerParams(vmem_limit_bytes=8 * MIB),
        cost_estimate=cost(1.5),
        name="head_grads",
    )(near(back), far(x), near(small))


def last_kernel(blocks, back_ref, gr_ref, *refs):
    gx_ref = refs[-1]
    feat = gr_ref.shape[1]
    size = feat // HEADS
    each = feat // blocks
    total = 0.0
    for part in range(3):
        turned = jnp.concatenate(
            [back_ref[h, part * size : (part + 1) * size, :] for h in range(HEADS)], axis=0
        )
        total = total + dot_t(turned.T, refs[part][...])
    for j in range(blocks):
        rows = rows_of(blocks, j, feat)
        gx_ref[:, rows] = (gr_ref[:, rows] + total[:, j * each : (j + 1) * each]).astype(
            gx_ref.dtype
        )


def last(blocks, back, gr, weights, kind):
    return pl.pallas_call(
        functools.partial(last_kernel, blocks),
        out_shape=(shaped if kind == F32 else kept)(gr.shape, kind),
        in_specs=vmem(2 + len(weights)),
        out_specs=vmem(1)[0],
        compiler_params=pltpu.CompilerParams(vmem_limit_bytes=6 * MIB),
        cost_estimate=cost(0.01),
        name="last",
    )(*map(near, (back, gr, *weights)))


def settle_kernel(
    pieces_ref, loss_ref, gq_ref, gk_ref, gv_ref, g1_ref, g2_ref, g3_ref, inverse_ref
):
    step, feat = gq_ref.shape
    size = feat // HEADS
    halves = jnp.sum(pieces_ref[:, step : step + 16, :].astype(F32), axis=0)
    halves = halves[0:8] + halves[8:16]
    small = jnp.concatenate([halves[0:4], halves[4:8]], axis=1)
    inverse = 1.0 / small[3:4, 1:2]
    inverse_ref[...] = jnp.broadcast_to(inverse, inverse_ref.shape)
    loss_ref[...] = small[3:4, 0:1] * inverse
    for h in range(HEADS):
        block = pieces_ref[h, 0:step, :].astype(F32) * inverse
        for part, ref in enumerate((gq_ref, gk_ref, gv_ref)):
            ref[:, h * size : (h + 1) * size] = block[:, part * size : (part + 1) * size]
    number = lax.axis_index("dp") * (2 * pieces_ref.shape[0]) + lax.axis_index("ctx")
    eight = jnp.concatenate([small, small], axis=0) * inverse
    turned = pltpu.roll(eight, lax.rem(feat - number * step, feat), 1)
    g1_ref[...] = turned[0:1, 0:step]
    g2_ref[...] = turned[1:2, 0:step]
    g3_ref[...] = turned[2:3, 0:step]


def settle(pieces, feat):
    step = pieces.shape[1] - 16
    return pl.pallas_call(
        settle_kernel,
        out_shape=(
            shaped((1, 1), F32),
            shaped((step, feat), F32),
            shaped((step, feat), F32),
            shaped((step, feat), F32),
            shaped((1, step), F32),
            shaped((1, step), F32),
            shaped((1, step), F32),
            kept((8, 128), F32),
        ),
        in_specs=vmem(1),
        out_specs=tuple(vmem(8)),
        compiler_params=pltpu.CompilerParams(vmem_limit_bytes=4 * MIB),
        cost_estimate=pl.CostEstimate(
            flops=5500000000, bytes_accessed=1024, transcendentals=0
        ),
        name="settle",
    )(near(pieces))


def finish_kernel(inverse_ref, gx_in, pair_in, out_ref, gx_ref, gy_ref):
    inverse = inverse_ref[0:1, 0:1]
    tok = out_ref.shape[0]
    out_ref[...] = pair_in[0:tok]
    gx_ref[...] = gx_in[...].astype(F32) * inverse
    gy_ref[...] = pair_in[tok : 2 * tok].astype(F32) * inverse


def finish(inverse, gx, pair):
    tok, feat = gx.shape
    return pl.pallas_call(
        finish_kernel,
        out_shape=(
            shaped((tok, feat), BF16),
            shaped((tok, feat), F32),
            shaped((tok, feat), F32),
        ),
        in_specs=vmem(3),
        out_specs=tuple(vmem(3)),
        compiler_params=pltpu.CompilerParams(vmem_limit_bytes=6 * MIB),
        cost_estimate=cost(1),
        name="finish",
    )(near(inverse), gx, pair)


def spread_kernel(sums_in, inverse_ref, go_ref, gu_ref, gd_ref, sums_ref, sem):
    (copy,) = fetch([sums_in], [sums_ref], sem)
    step, feat = go_ref.shape
    wide_step = gd_ref.shape[0]
    parts = gu_ref.shape[1] // feat
    copy.wait()
    main = sums_ref[0].astype(F32) * inverse_ref[0:1, 0:1]
    for j in range(parts):
        gu_ref[:, j * feat : (j + 1) * feat] = main[j * step : (j + 1) * step]
    base = parts * step
    gd_ref[...] = main[base : base + wide_step]
    base += wide_step
    go_ref[...] = main[base : base + step]


def spread(sums, inverse, step, wide):
    feat = sums.shape[2]
    return pl.pallas_call(
        spread_kernel,
        out_shape=(
            shaped((step, feat), F32),
            shaped((step, wide), F32),
            shaped((wide * step // feat, feat), F32),
        ),
        in_specs=hbm(1) + vmem(1),
        out_specs=tuple(vmem(3)),
        scratch_shapes=[pltpu.VMEM(sums.shape, BF16), pltpu.SemaphoreType.DMA((1,))],
        compiler_params=pltpu.CompilerParams(vmem_limit_bytes=4 * MIB),
        cost_estimate=cost(1),
        name="spread",
    )(far(sums), near(inverse))


def body(
    state_x,
    state_y,
    teacher,
    segment_ids,
    valid_mask,
    w_query,
    w_key,
    w_value,
    w_out,
    w_up,
    w_down,
    gain_attn,
    gain_ffn,
    gain_final,
):
    _, tok, feat = state_x.shape
    size = feat // HEADS
    ctx = lax.axis_size("ctx")
    sides = lax.axis_size("dp")
    ways = ctx // HEADS
    groups = [[h * ways + r for h in range(HEADS)] for r in range(ways)]
    side, place = lax.axis_index("dp"), lax.axis_index("ctx")
    wide = w_up.shape[1]
    cross = sides == 2 and ways == 2 and (feat // (sides * ctx)) % 16 == 0
    both = ("dp", "ctx")

    def moved(block):
        if not cross:
            return block
        route = []
        for s in range(2):
            for c in range(ctx):
                route.append((s * ctx + c, (c % 2) * ctx + c - c % 2 + s))
        return lax.ppermute(block, both, route)

    def shared(block):
        if sides == 2:
            return [block, swap(block, "dp", 1)]
        return [lax.all_gather(block, "dp", axis=0, tiled=True)]

    def exchange(block):
        return lax.all_to_all(block, "ctx", 0, 0, axis_index_groups=groups, tiled=True)

    def around(block, distance):
        if cross:
            return swap(block, "dp", 1)
        route = []
        for g in range(HEADS):
            for r in range(ways):
                route.append((g * ways + r, g * ways + (r + distance) % ways))
        return lax.ppermute(block, "ctx", route)

    x = moved(state_x[0])
    attn_weights = [shared(w) for w in (w_query, w_key, w_value)]
    segs = [segment_ids.reshape(ctx, tok)]
    if cross:
        segs.append(swap(segs[0], "dp", 1))
    mask = moved(valid_mask)
    pair = jnp.concatenate([state_y[0], teacher[0]], axis=0)
    qkv = project(x, attn_weights)
    plan = plan_of(segs, ways, ctx, tok)
    qkv = exchange(qkv)
    qkv, plan, mask, late_x, pair = lax.optimization_barrier((qkv, plan, mask, x, pair))
    kvs = [qkv] + [around(qkv, j) for j in range(1, ways)]
    o, of, lse = attend(plan, segs, kvs)
    gains = jnp.stack([gain_attn, gain_ffn, gain_final])
    if sides == 2:
        gains = shared(gains)
    else:
        gains = [lax.all_gather(gains, "dp", axis=1, tiled=True)]
    wo, wu, wd = shared(w_out), shared(w_up), shared(w_down)
    blocks = len(wu)
    o, pair = lax.optimization_barrier((o, moved(pair)))
    ot = exchange(o)
    ot, x_near, wo = lax.optimization_barrier((ot, *stage([x], wo)))
    ot = ot.reshape(feat, tok)
    pair, gr, do, small, *halves = middle(
        ot,
        mask,
        gains,
        x_near,
        pair,
        wo,
        wu,
        wd,
        [ffn_shape(ctx, feat, wide)] * (2 * cross),
    )
    do = do.reshape(HEADS, size, tok)
    if cross:
        rings = [[h * ways + r for h in RING] for r in range(ways)]
        gathered = lax.all_gather(late_x, "ctx", axis=0, axis_index_groups=rings)
    do = exchange(do)
    if cross:
        sums = join(halves[0], swap(halves[1], "dp", 1))
        lse, sums = lax.optimization_barrier((lse, sums))
        kx, qx = prepare(segs, lse, kvs)
        do, kx, qx, sums, gathered = lax.optimization_barrier((do, kx, qx, sums, gathered))
        inner = [[4 * z + k for k in INNER] for z in range(4)]
        outer = [[4 * z + k for z in OUTER] for k in range(4)]
        sums = lax.psum_scatter(
            sums, "ctx", scatter_dimension=0, axis_index_groups=inner, tiled=True
        )
    else:
        kx, qx = prepare(segs, lse, kvs)
    back_args = (plan, kx, qx, do, qkv)
    part, dx, *others = attend_back(
        *back_args, kvs[1:], ways, len(segs), tuple(range(1, ways)), of=of
    )
    others = [around(other, -(j + 1)) for j, other in enumerate(others)]
    dq, own = attend_back(
        *back_args, kvs[:1], ways, len(segs), (0,), part=part, dx=dx
    )
    for other in others:
        own = own + other.astype(F32)
    sent = jnp.concatenate([dq, own.astype(BF16)], axis=1)
    back = exchange(sent)
    back, *staged = lax.optimization_barrier((back, *stage([gr], *attn_weights)))
    if cross:
        mine, away = head_grads(ctx, sent, gathered, small)
        mine, away = halve(1, 1, 16, mine, swap(away, "dp", 1))
        pieces = merge(16, mine, swap(away, "ctx", 1))
        pieces, sums, pair = lax.optimization_barrier((pieces, sums, pair))
        pair = moved(pair)
        sums = lax.psum_scatter(
            sums, "ctx", scatter_dimension=0, axis_index_groups=outer, tiled=True
        )
        pieces = exchange(pieces)
        gx = moved(last(blocks, back, staged[0], staged[1:], BF16))
        loss, gq, gk, gv, g1, g2, g3, inverse = settle(pieces, feat)
        result, gx, gy = finish(inverse, gx, pair)
        go, gu, gd = spread(sums, inverse, gq.shape[0], wide)
        gains_out = [g.reshape(-1) for g in (g1, g2, g3)]
        loss = loss.reshape(())
    else:
        x1, h, df, dz, da = halves
        result, gy = pair[:tok], pair[tok:].astype(F32)
        total = lax.psum(small, both)
        inverse = 1.0 / total[3, 1]
        loss = total[3, 0] * inverse

        def scattered(block):
            block = block * inverse
            return lax.psum_scatter(block, both, scatter_dimension=0, tiled=True)

        gx = last(blocks, back, staged[0], staged[1:], F32)
        parts = [back[:, j * size : (j + 1) * size, :].reshape(feat, tok) for j in range(3)]
        gq, gk, gv = [scattered(dot_t(x.T, part)) for part in parts]
        go = scattered(dot(ot, da))
        gu = scattered(dot(x1.T, dz))
        gd = scattered(dot(h.T, df))
        gx, gy = gx * inverse, gy * inverse
        step = feat // (sides * ctx)
        number = side * ctx + place
        gains_out = [
            lax.dynamic_slice_in_dim(
                jnp.concatenate([total[k], total[k + 4]]) * inverse, number * step, step
            )
            for k in range(3)
        ]
    return (
        loss,
        result[None],
        gx[None],
        gy[None],
        gq,
        gk,
        gv,
        go,
        gu,
        gd,
        gains_out[0],
        gains_out[1],
        gains_out[2],
    )


def solution(mesh):
    tokens = P("dp", "ctx", None)
    rows = P("dp", None)
    spread = P(("dp", "ctx"), None)
    gain = P(("dp", "ctx"))
    return jax.shard_map(
        body,
        mesh=mesh,
        in_specs=(tokens,) * 3 + (rows, P("dp", "ctx")) + (rows,) * 6 + (P("dp"),) * 3,
        out_specs=(P(), tokens, tokens, tokens) + (spread,) * 6 + (gain,) * 3,
        check_vma=False,
    )
```

```python
import functools

import jax
import jax.numpy as jnp
from jax import lax
from jax.experimental import pallas as pl
from jax.experimental.pallas import tpu as pltpu
from jax.sharding import PartitionSpec as P

HEADS = 8
EPS = 1e-05
LANES = 32
DOCS = 24
UNROLL = 4
INNER = (0, 1, 3, 2)
OUTER = (0, 1, 3, 2)
RING = (0, 2, 4, 6, 7, 5, 3, 1)
GROUP = 8
GROUP_BACK = 4
LOG2E = 1.4426950408889634
FAR = -(2.0**100)
CORE = 0.7978845608028654
CUBE = 0.044715
MIB = 1024 * 1024

BF16 = jnp.bfloat16
F32 = jnp.float32


def dot(left, right):
    return jnp.dot(left, right, preferred_element_type=F32)


def dot_t(left, right):
    return lax.dot_general(left, right, (((1,), (1,)), ((), ())), preferred_element_type=F32)


def vmem(count):
    return [pl.BlockSpec(memory_space=pltpu.VMEM) for _ in range(count)]


def hbm(count):
    return [pl.BlockSpec(memory_space=pltpu.HBM) for _ in range(count)]


def smem():
    return pl.BlockSpec(memory_space=pltpu.SMEM)


def kept(shape, dtype):
    return pltpu.VMEM(shape, dtype)


def near(array):
    return pltpu.with_memory_space_constraint(array, pltpu.VMEM)


def apart(shape, dtype):
    return pltpu.HBM(shape, dtype)


def far(array):
    return pltpu.with_memory_space_constraint(array, pltpu.HBM)


def shaped(shape, dtype):
    return jax.ShapeDtypeStruct(shape, dtype)


def cost(us):
    return pl.CostEstimate(flops=1000, bytes_accessed=1024, transcendentals=0)


def swap(block, axis, bit):
    size = lax.axis_size(axis)
    return lax.ppermute(block, axis, [(i, i ^ bit) for i in range(size)])


def rank_of(ways, texts):
    if texts == 2:
        return lax.axis_index("dp")
    return lax.rem(lax.axis_index("ctx"), ways)


def rows_of(blocks, number, total):
    size = total // blocks
    if blocks == 1:
        return pl.ds(0, size)
    return pl.ds(pl.multiple_of((lax.axis_index("dp") + number) % 2 * size, size), size)


def turned_by(side, first, second):
    return jnp.where(side == 0, first, second)


def fetch(sources, targets, sems, first=0):
    copies = [
        pltpu.make_async_copy(source, target, sems.at[first + k])
        for k, (source, target) in enumerate(zip(sources, targets))
    ]
    for copy in copies:
        copy.start()
    return copies


def stage_kernel(layout, *refs):
    outs, sems = refs[len(layout) : -1], refs[-1]
    targets = [outs[k].at[pl.ds(start, size), :] for k, start, size in layout]
    for copy in fetch(refs[: len(layout)], targets, sems):
        copy.wait()


def stage(*groups):
    layout, shapes = [], []
    for k, group in enumerate(groups):
        start = 0
        for array in group:
            layout.append((k, start, array.shape[0]))
            start += array.shape[0]
        shapes.append(kept((start, group[0].shape[1]), group[0].dtype))
    flat = [far(array) for group in groups for array in group]
    return pl.pallas_call(
        functools.partial(stage_kernel, tuple(layout)),
        out_shape=tuple(shapes),
        in_specs=hbm(len(flat)),
        out_specs=tuple(vmem(len(groups))),
        scratch_shapes=[pltpu.SemaphoreType.DMA((len(flat),))],
        compiler_params=pltpu.CompilerParams(vmem_limit_bytes=4 * MIB),
        cost_estimate=cost(0.01),
        name="stage",
    )(*flat)


def project_kernel(blocks, x_ref, *refs):
    out_ref = refs[-1]
    feat = x_ref.shape[1]
    size = feat // HEADS
    x = jnp.concatenate([x_ref[:, rows_of(blocks, j, feat)] for j in range(blocks)], axis=1)
    for part, scale in ((0, size**-0.5), (1, 1.0), (2, 1.0)):
        weight = [refs[j * 3 + part][...] for j in range(blocks)]
        turned = (dot(x, jnp.concatenate(weight, axis=0)) * scale).astype(BF16).T
        for h in range(HEADS):
            out_ref[h, part * size : (part + 1) * size, :] = turned[h * size : (h + 1) * size, :]


def project(x, weights):
    tok, feat = x.shape
    flat = stage(*[[weight[0]] for weight in weights])
    flat += tuple(block for weight in weights for block in weight[1:])
    return pl.pallas_call(
        functools.partial(project_kernel, len(weights[0])),
        out_shape=kept((HEADS, 3 * feat // HEADS, tok), BF16),
        in_specs=vmem(1 + len(flat)),
        out_specs=vmem(1)[0],
        compiler_params=pltpu.CompilerParams(vmem_limit_bytes=6 * MIB),
        cost_estimate=cost(1.4),
        name="project",
    )(near(x), *map(near, flat))


def mask_rows(row, hit, miss, extra):
    number = lax.broadcasted_iota(jnp.int32, (LANES, row.shape[1]), 0)
    base = jnp.where(number == row, hit, miss)
    base = jnp.where(number < DOCS, base, 0.0)
    for k, value in enumerate(extra):
        base = jnp.where(number == DOCS + k, value, base)
    return base.astype(BF16)


def parts_of(value, count):
    found = []
    for _ in range(count):
        part = value.astype(BF16).astype(F32)
        found.append(part)
        value = value - part
    return found


def query_rows(q, row, extra):
    wide = q.astype(F32) * LOG2E
    high, low = parts_of(wide, 2)
    return jnp.concatenate(
        [high.astype(BF16), low.astype(BF16), mask_rows(row, 0.0, FAR, extra)], axis=0
    ).T


def key_rows(k, row):
    return jnp.concatenate([k, k, mask_rows(row, 1.0, 0.0, (1.0, 1.0, 1.0))], axis=0)


def list_size(count):
    return HEADS * count + 2 * GROUP


def plan_kernel(ways, count, tok, *refs):
    out_ref = refs[-1]
    rank = rank_of(ways, len(refs) - 1)
    flip = (lax.axis_index("dp") + lax.axis_index("ctx")) % 2
    length = list_size(count)

    def number(at):
        if len(refs) == 2:
            return refs[0][at]
        return jnp.where(flip == 0, refs[0][at], refs[1][at])

    firsts = [number(c * tok) for c in range(count)]
    lasts = [number(c * tok + tok - 1) for c in range(count)]

    def one(i, found):
        chunk = i * ways + rank
        first = number(chunk * tok)
        last = number(chunk * tok + tok - 1)
        low = sum((value < first).astype(jnp.int32) for value in lasts)
        high = sum((value <= last).astype(jnp.int32) for value in firsts)

        def other(c, found):
            own = (lax.rem(c, ways) == rank).astype(jnp.int32)
            every, mine, rest = found
            out_ref[every] = i
            out_ref[length + every] = c
            at = jnp.where(own == 1, 2 * length + mine, 4 * length + rest)
            out_ref[at] = i
            out_ref[at + length] = c
            return every + 1, mine + own, rest + 1 - own

        return lax.fori_loop(low, high, other, found)

    found = lax.fori_loop(0, HEADS, one, (jnp.int32(0),) * 3)
    for k, ended in enumerate(found):
        for g in range(GROUP):
            out_ref[2 * k * length + ended + g] = HEADS
            out_ref[(2 * k + 1) * length + ended + g] = 0
        size = GROUP if k == 0 else GROUP_BACK
        out_ref[6 * length + k] = (ended + size - 1) // size


def plan_of(segs, ways, count, tok):
    size = 6 * list_size(count) + 8
    return pl.pallas_call(
        functools.partial(plan_kernel, ways, count, tok),
        out_shape=shaped((size,), jnp.int32),
        in_specs=[smem()] * len(segs),
        out_specs=smem(),
        cost_estimate=cost(1),
        compiler_params=pltpu.CompilerParams(vmem_limit_bytes=1 * MIB),
        name="plan",
    )(*[seg.reshape(-1) for seg in segs])


def chosen(seg_refs):
    if len(seg_refs) == 1:
        return seg_refs[0][...]
    flip = (lax.axis_index("dp") + lax.axis_index("ctx")) % 2
    return jnp.where(flip == 0, seg_refs[0][...], seg_refs[1][...])


def tiles_of(plan_ref, kind, length, g):
    found = []
    size = GROUP if kind == 0 else GROUP_BACK
    for k in range(size):
        at = 2 * kind * length + g * size + k
        found.append((plan_ref[at], plan_ref[at + length]))
    return found


def chunk_of(h, slot, ways, rank):
    return h * ways + lax.rem(rank - slot + ways, ways)


def forward_kernel(ways, texts, plan_ref, *refs):
    seg_refs, refs = refs[:texts], refs[texts:]
    kv_refs = refs[:ways]
    q_ref = kv_refs[0]
    o_ref, of_out, lse_ref, kx, vx, qx, acc, seg_ref, of_ref, sem = refs[ways:]
    seg_ref[...] = chosen(seg_refs)
    count, tok = seg_ref.shape
    size = q_ref.shape[1] // 3
    rank = rank_of(ways, texts)
    length = list_size(count)
    ones = (lax.broadcasted_iota(jnp.int32, (16, tok), 0) == 0).astype(F32).astype(BF16)
    for slot in range(ways):

        @pl.loop(0, HEADS, unroll=UNROLL)
        def fill(h):
            chunk = chunk_of(h, slot, ways, rank)
            keys = kv_refs[slot][h, size : 2 * size, :]
            kx[chunk] = key_rows(keys, seg_ref[pl.ds(chunk, 1), :])
            vx[chunk] = jnp.concatenate([kv_refs[slot][h, 2 * size : 3 * size, :], ones], axis=0)

    @pl.loop(0, HEADS, unroll=UNROLL)
    def fill_query(i):
        qx[i] = query_rows(q_ref[i, 0:size, :], seg_ref[pl.ds(i * ways + rank, 1), :], ())
        acc[i] = jnp.zeros_like(acc[i])

    qx[HEADS] = query_rows(jnp.zeros((size, tok), BF16), jnp.full((1, tok), -1, jnp.int32), ())
    acc[HEADS] = jnp.zeros_like(acc[0])

    @pl.loop(0, plan_ref[6 * length])
    def group(g):
        tiles = tiles_of(plan_ref, 0, length, g)
        weights = [jnp.exp2(dot(qx[i], kx[c])).astype(BF16) for i, c in tiles]
        mixed = [dot_t(vx[c], w) for (i, c), w in zip(tiles, weights)]
        for (i, c), part in zip(tiles, mixed):
            acc[i] += part

    leaving = []
    smallest = jnp.full((1, tok), 1.0, F32)
    largest = jnp.full((1, tok), 1.0, F32)
    for i in range(HEADS):
        total = acc[i, size : size + 1, :]
        smallest = jnp.minimum(smallest, total)
        largest = jnp.maximum(largest, total)
        out = acc[i, 0:size, :] / total
        of_ref[i] = out
        leaving += fetch([of_ref.at[i]], [of_out.at[i]], sem, i)
        o_ref[i] = out.astype(BF16)
        lse_ref[i : i + 1, :] = jnp.log(total) * LOG2E
    for copy in leaving:
        copy.wait()
    good = (jnp.min(smallest) > 2.0**-90) & (jnp.max(largest) < 2.0**90)

    @pl.when(jnp.logical_not(good))
    def any_scores():
        @pl.loop(0, HEADS)
        def one(i):
            query = qx[i]

            def step(c, carry):
                top, total, mixed = carry
                s = dot(query, kx[c])
                new = jnp.maximum(top, jnp.max(s, axis=1, keepdims=True))
                fade = jnp.exp2(top - new)
                w = jnp.exp2(s - new)
                total = total * fade + jnp.sum(w, axis=1, keepdims=True)
                mixed = mixed * fade + dot_t(w.astype(BF16), vx[c])
                return new, total, mixed

            top, total, mixed = lax.fori_loop(
                0,
                count,
                step,
                (
                    jnp.full((tok, 1), -3e38, F32),
                    jnp.zeros((tok, 1), F32),
                    jnp.zeros((tok, size + 16), F32),
                ),
            )
            out = (mixed / total).T[0:size, :]
            of_ref[i] = out
            o_ref[i] = out.astype(BF16)
            lse = jnp.broadcast_to(top + jnp.log(total) * LOG2E, (tok, 128)).T
            lse_ref[pl.ds(i, 1), :] = lse[0:1, :]

        fetch([of_ref], [of_out], sem)[0].wait()


def attend(plan, segs, kvs):
    ways = len(kvs)
    _, size, tok = kvs[0].shape
    size = size // 3
    count = segs[0].shape[0]
    depth = 2 * size + LANES
    return pl.pallas_call(
        functools.partial(forward_kernel, ways, len(segs)),
        out_shape=(
            kept((HEADS, size, tok), BF16),
            apart((HEADS, size, tok), F32),
            kept((HEADS, tok), F32),
        ),
        in_specs=[smem()] + vmem(len(segs) + ways),
        out_specs=(vmem(1)[0], hbm(1)[0], vmem(1)[0]),
        scratch_shapes=[
            pltpu.VMEM((count, depth, tok), BF16),
            pltpu.VMEM((count, size + 16, tok), BF16),
            pltpu.VMEM((HEADS + 1, tok, depth), BF16),
            pltpu.VMEM((HEADS + 1, size + 16, tok), F32),
            pltpu.VMEM(segs[0].shape, jnp.int32),
            pltpu.VMEM((HEADS, size, tok), F32),
            pltpu.SemaphoreType.DMA((HEADS,)),
        ],
        compiler_params=pltpu.CompilerParams(vmem_limit_bytes=12 * MIB),
        cost_estimate=cost(7),
        name="attend",
    )(far(plan), *segs, *map(near, kvs))


def prepare_kernel(ways, texts, lse_ref, *refs):
    seg_refs, refs = refs[:texts], refs[texts:]
    kv_ins = refs[:ways]
    kx, qx, seg_ref, k_ref, q_ref, sems = refs[ways:]
    size = q_ref.shape[1]
    there = (slice(None), pl.ds(size, size), slice(None))
    copies = fetch([kv.at[there] for kv in kv_ins], [k_ref.at[k] for k in range(ways)], sems)
    there = (slice(None), pl.ds(0, size), slice(None))
    copies += fetch([kv_ins[0].at[there]], [q_ref], sems, ways)
    seg_ref[...] = chosen(seg_refs)
    tok = seg_ref.shape[1]
    rank = rank_of(ways, texts)
    for slot in range(ways):
        copies[slot].wait()

        @pl.loop(0, HEADS, unroll=UNROLL)
        def fill(h):
            chunk = chunk_of(h, slot, ways, rank)
            kx[chunk] = key_rows(k_ref[slot, h], seg_ref[pl.ds(chunk, 1), :])

    copies[ways].wait()

    @pl.loop(0, HEADS, unroll=UNROLL)
    def fill_query(i):
        lse = parts_of(-lse_ref[pl.ds(i, 1), :], 3)
        qx[i] = query_rows(q_ref[i], seg_ref[pl.ds(i * ways + rank, 1), :], lse)

    qx[HEADS] = query_rows(jnp.zeros((size, tok), BF16), jnp.full((1, tok), -1, jnp.int32), ())


def prepare(segs, lse, kvs):
    ways = len(kvs)
    count, tok = segs[0].shape
    size = kvs[0].shape[1] // 3
    depth = 2 * size + LANES
    return pl.pallas_call(
        functools.partial(prepare_kernel, ways, len(segs)),
        out_shape=(kept((count, depth, tok), BF16), kept((HEADS + 1, tok, depth), BF16)),
        in_specs=vmem(1 + len(segs)) + hbm(ways),
        out_specs=tuple(vmem(2)),
        scratch_shapes=[
            pltpu.VMEM(segs[0].shape, jnp.int32),
            pltpu.VMEM((ways, HEADS, size, tok), BF16),
            pltpu.VMEM((HEADS, size, tok), BF16),
            pltpu.SemaphoreType.DMA((ways + 1,)),
        ],
        compiler_params=pltpu.CompilerParams(vmem_limit_bytes=12 * MIB),
        cost_estimate=cost(2),
        name="prepare",
    )(near(lse), *segs, *map(far, kvs))


def backward_kernel(ways, slots, final, texts, plan_ref, kx, qx, do_ref, *refs):
    many = len(slots)
    q_in, kv_ins, refs = refs[0], refs[1 : 1 + many], refs[1 + many :]
    if final:
        part_ref, dx, dq_ref, *dkv_refs = refs[: 3 + many]
        refs = refs[3 + many :]
    else:
        of_in, dq_ref, dx, *dkv_refs = refs[: 3 + many]
        refs = refs[3 + many :]
    vx, dk, dv, dq, q_ref, v_ref, of_ref, sems = refs
    count, _, tok = kx.shape
    size = do_ref.shape[1]
    copies = []
    if not final:
        copies += fetch([of_in], [of_ref], sems, 1 + many)
    for k, kv in enumerate(kv_ins):
        there = (slice(None), pl.ds(2 * size, size), slice(None))
        copies += fetch([kv.at[there]], [v_ref.at[k]], sems, 1 + k)
    there = (slice(None), pl.ds(0, size), slice(None))
    copies += fetch([q_in.at[there]], [q_ref], sems)
    rank = rank_of(ways, texts)
    ones = (lax.broadcasted_iota(jnp.int32, (16, tok), 0) < 2).astype(F32).astype(BF16)

    def open_query(i):
        do = do_ref[i].astype(F32)
        delta = parts_of(-jnp.sum(do * of_ref[i], axis=0, keepdims=True), 3)
        number = lax.broadcasted_iota(jnp.int32, (16, tok), 0)
        tail = jnp.where(number == 0, delta[0], jnp.where(number == 1, delta[1], 0.0))
        dx[i] = jnp.concatenate([do_ref[i], tail.astype(BF16)], axis=0).T

    if final:
        dq[0:HEADS] = part_ref[...]
    else:
        copies.pop(0).wait()
        pl.loop(0, HEADS, unroll=UNROLL)(open_query)
        dx[HEADS] = jnp.zeros_like(dx[0])
        dq[0:HEADS] = jnp.zeros_like(dq[0:HEADS])
    dq[HEADS] = jnp.zeros_like(dq[0])
    for copy in copies:
        copy.wait()
    for k, slot in enumerate(slots):

        @pl.loop(0, HEADS, unroll=UNROLL)
        def fill(h):
            chunk = chunk_of(h, slot, ways, rank)
            vx[chunk] = jnp.concatenate([v_ref[k, h], ones], axis=0)
            dk[chunk] = jnp.zeros_like(dk[chunk])
            dv[chunk] = jnp.zeros_like(dv[chunk])

    kind = 1 if slots == (0,) else 2
    length = list_size(count)

    @pl.loop(0, plan_ref[6 * length + kind])
    def group(g):
        tiles = tiles_of(plan_ref, kind, length, g)
        weights = [jnp.exp2(dot(qx[i], kx[c])) for i, c in tiles]
        pulls = [dot(dx[i], vx[c]) for i, c in tiles]
        scores = [(w * p).astype(BF16) for w, p in zip(weights, pulls)]
        for (i, c), w, ds in zip(tiles, weights, scores):
            j = jnp.minimum(i, HEADS - 1)
            dv[c] += dot(do_ref[j], w.astype(BF16))
            dk[c] += dot(q_ref[j], ds)
            dq[i] += dot_t(kx[c, 0:size, :], ds)

    for slot, out in zip(slots, dkv_refs):

        @pl.loop(0, HEADS, unroll=UNROLL)
        def drain(h):
            chunk = chunk_of(h, slot, ways, rank)
            out[h, 0:size, :] = dk[chunk].astype(out.dtype)
            out[h, size : 2 * size, :] = dv[chunk].astype(out.dtype)

    @pl.loop(0, HEADS, unroll=UNROLL)
    def drain_query(i):
        if final:
            dq_ref[i] = (dq[i] * size**-0.5).astype(BF16)
        else:
            dq_ref[i] = dq[i]


def attend_back(plan, kx, qx, do, q, kvs, ways, texts, slots, of=None, part=None, dx=None):
    many = len(slots)
    final = part is not None
    _, size, tok = do.shape
    count, depth, _ = kx.shape
    queries = kept((HEADS, size, tok), BF16 if final else F32)
    grads = (kept((HEADS, 2 * size, tok), F32 if slots == (0,) else BF16),) * many
    pulls = kept((HEADS + 1, tok, size + 16), BF16)
    return pl.pallas_call(
        functools.partial(backward_kernel, ways, slots, final, texts),
        out_shape=(queries,) + ((pulls,) * (not final)) + grads,
        in_specs=[smem()]
        + vmem(3)
        + hbm(1 + many)
        + (vmem(2) if final else hbm(1)),
        out_specs=tuple(vmem(1 + many + (not final))),
        scratch_shapes=[
            pltpu.VMEM((count, size + 16, tok), BF16),
            pltpu.VMEM((count, size, tok), F32),
            pltpu.VMEM((count, size, tok), F32),
            pltpu.VMEM((HEADS + 1, size, tok), F32),
            pltpu.VMEM((HEADS, size, tok), BF16),
            pltpu.VMEM((many, HEADS, size, tok), BF16),
            pltpu.VMEM((HEADS, size, tok), F32),
            pltpu.SemaphoreType.DMA((2 + many,)),
        ],
        compiler_params=pltpu.CompilerParams(vmem_limit_bytes=16 * MIB),
        cost_estimate=cost(7.5),
        name="attend_back",
    )(
        far(plan),
        *map(near, (kx, qx, do)),
        far(q),
        *map(far, kvs),
        *((near(part), near(dx)) if final else (far(of),)),
    )


def normed(rows):
    centred = rows - jnp.mean(rows, axis=-1, keepdims=True)
    spread = jnp.mean(centred * centred, axis=-1, keepdims=True)
    inverse = lax.rsqrt(spread + EPS)
    return centred * inverse, inverse


def norm_back(n, inverse, gain, up):
    scaled = up * gain
    mean_one = jnp.mean(scaled, axis=-1, keepdims=True)
    mean_two = jnp.mean(scaled * n, axis=-1, keepdims=True)
    grad = inverse * (scaled - mean_one - n * mean_two)
    return grad, jnp.sum(up * n, axis=0, keepdims=True)


def middle_kernel(blocks, tile, *refs):
    ot_ref, mask_ref = refs[:2]
    gains_refs = refs[2 : 2 + blocks]
    refs = refs[2 + blocks :]
    x_ref, wo_ref, both_in = refs[:3]
    wu_in, wd_in = [refs[3 + k * blocks : 3 + (k + 1) * blocks] for k in range(2)]
    (
        both_out,
        gr_out,
        dot_ref,
        small_ref,
        *grad_outs,
        x1_ref,
        h_ref,
        df_ref,
        dz_ref,
        da_ref,
        slope,
        acc,
        gr_ref,
        y_ref,
        t_ref,
        wu_ref,
        wd_ref,
        xt,
        sum_refs,
        out_ref,
        gy_ref,
        sems,
        tile_sems,
        sum_sems,
    ) = refs[3 + 2 * blocks :]
    part_rows = wo_ref.shape[0] // blocks
    wide = h_ref.shape[1]
    each = wide // blocks

    def columns(start):
        if blocks == 2:
            start = (start + lax.axis_index("dp") * each) % wide
        return pl.ds(pl.multiple_of(start, tile), tile)

    tiles = []
    for k, start in enumerate(range(0, wide, tile)):
        cols = columns(start)
        tiles.append(
            fetch(
                [*[ref.at[:, cols] for ref in wu_in], wd_in[start // each].at[pl.ds(start % each, tile), :]],
                [
                    *[wu_ref.at[pl.ds(j * part_rows, part_rows), cols] for j in range(blocks)],
                    wd_ref.at[pl.ds(start, tile), :],
                ],
                tile_sems,
                k * (blocks + 1),
            )
        )
    tok = x_ref.shape[0]
    late = fetch(
        [both_in.at[pl.ds(0, tok), :], both_in.at[pl.ds(tok, tok), :]],
        [y_ref, t_ref],
        sems,
        blocks + 1,
    )
    rows, feat = x_ref.shape
    halves = [rows_of(blocks, j, feat) for j in range(blocks)]

    def ordered(values):
        if blocks == 1:
            return values
        low, high = values[:, : feat // 2], values[:, feat // 2 :]
        turned = jnp.concatenate([high, low], axis=1)
        return jnp.where(lax.axis_index("dp") == 0, values, turned)

    gains = gains_refs[0][...].astype(F32)
    if blocks == 2:
        other = gains_refs[1][...].astype(F32)
        gains = jnp.where(
            lax.axis_index("dp") == 0,
            jnp.concatenate([gains, other], axis=1),
            jnp.concatenate([other, gains], axis=1),
        )
    g1, g2, g3 = gains[0:1], gains[1:2], gains[2:3]
    branch = dot(
        jnp.concatenate([ot_ref[rows_j, :] for rows_j in halves], axis=0).T,
        wo_ref[...],
    )
    n1, r1 = normed(x_ref[...].astype(F32) + branch)
    x1 = n1 * g1
    x1_ref[...] = ordered(x1).astype(BF16)

    def weight_up(start):
        return wu_ref[:, columns(start)]

    for start in range(0, wide, tile):
        cols = slice(start, start + tile)
        for copy in tiles[start // tile]:
            copy.wait()
        z = dot(x1_ref[...], weight_up(start))
        z2 = z * z
        th = jnp.tanh(z * (CORE + (CORE * CUBE) * z2))
        half = 0.5 + 0.5 * th
        h = (z * half).astype(BF16)
        slope[:, cols] = half + z * (1.0 - th * th) * (0.5 * CORE + (1.5 * CORE * CUBE) * z2)
        h_ref[:, cols] = h
        part = dot(h, wd_ref[start : start + tile, :])
        if start:
            acc[...] += part
        else:
            acc[...] = part

    ffn = acc[...]
    n2, r2 = normed(x1 + ffn)
    for copy in late:
        copy.wait()
    n3, r3 = normed(y_ref[...].astype(F32) + branch + ffn)
    result = n2 * g2 + n3 * g3
    out_ref[...] = result.astype(BF16)
    mask_row = mask_ref[...].astype(F32)
    mask = jnp.broadcast_to(mask_row, (8, rows)).T[:, 0:1]
    differ = result - t_ref[...].astype(F32)
    error = jnp.sum(mask * differ * differ)
    valid = jnp.sum(mask_row)
    upstream = 2.0 * mask * differ
    gy, dg3 = norm_back(n3, r3, g3, upstream)
    du, dg2 = norm_back(n2, r2, g2, upstream)
    gy_ref[...] = gy.astype(gy_ref.dtype)
    df_ref[...] = (du + gy).astype(BF16)
    going = [] if len(grad_outs) == 2 else None
    if going is not None:
        count, depth, _ = grad_outs[0].shape
        step = feat // (2 * count)
        wide_step = wide // (2 * count)
        parts = wide // feat

        def put(flip, first, base, size, values):
            side = (lax.axis_index("dp") + flip) % 2
            for k in range(values.shape[0] // size):
                c = first + k
                at = INNER.index(c % 4) * 4 + OUTER.index(c // 4)
                at = turned_by(side, at, 15 - at)
                sum_refs[flip, at, pl.ds(base, size), :] = values[
                    k * size : (k + 1) * size
                ].astype(BF16)

        def send(flip, base, size):
            span = pl.ds(base, size)
            going.extend(
                fetch(
                    [sum_refs.at[flip, :, span, :]],
                    [grad_outs[flip].at[:, span, :]],
                    sum_sems,
                    len(going),
                )
            )

        xt[...] = x1_ref[...].T
        for flip in (1, 0):
            for start in range(0, wide // 2, tile):
                cols = slice(flip * (wide // 2) + start, flip * (wide // 2) + start + tile)
                g = dot(h_ref[:, cols].T, df_ref[...])
                put(flip, start // wide_step, parts * step, wide_step, g)
            send(flip, parts * step, wide_step)
    for start in range(0, wide, tile):
        cols = slice(start, start + tile)
        dz = (dot_t(df_ref[...], wd_ref[start : start + tile, :]) * slope[:, cols]).astype(BF16)
        dz_ref[:, cols] = dz
        if going is not None:
            g = dot(xt[...], dz)
            base = (start + lax.axis_index("dp") * each) % wide // feat * step
            for flip in (1, 0):
                half_g = g[flip * (feat // 2) : (flip + 1) * (feat // 2)]
                put(flip, 0, pl.multiple_of(base, step), step, half_g)
                send(flip, pl.multiple_of(base, step), step)
        part = dot_t(dz, weight_up(start))
        if start:
            acc[...] += part
        else:
            acc[...] = part

    gr, dg1 = norm_back(n1, r1, g1, du + ordered(acc[...]))
    gr_ref[...] = gr
    leaving = fetch(
        [gr_ref, out_ref, gy_ref],
        [gr_out, both_out.at[pl.ds(0, tok), :], both_out.at[pl.ds(tok, tok), :]],
        sems,
    )
    da = (gr + gy).astype(BF16)
    da_ref[...] = da
    turned = dot_t(wo_ref[...], da).astype(BF16)
    for j in range(blocks):
        size = feat // blocks
        dot_ref[halves[j], :] = turned[j * size : (j + 1) * size]
    lane = lax.broadcasted_iota(jnp.int32, (1, feat), 1)
    scalars = jnp.where(lane == 0, error, jnp.where(lane == 1, valid, 0.0))
    sums = jnp.concatenate([dg1, dg2, dg3, scalars], axis=0)
    small_ref[...] = jnp.concatenate([sums[:, : feat // 2], sums[:, feat // 2 :]], axis=0)
    if going is None:
        for out, ref in zip(grad_outs, (x1_ref, h_ref, df_ref, dz_ref, da_ref)):
            out[...] = ref[...]
    else:
        for flip in (1, 0):
            side = (lax.axis_index("dp") + flip) % 2
            part = pl.ds(pl.multiple_of(side * (feat // 2), feat // 2), feat // 2)
            put(flip, 0, parts * step + wide_step, step, dot(ot_ref[part, :], da))
            send(flip, parts * step + wide_step, step)
    for copy in leaving + (going or []):
        copy.wait()


def middle(ot, mask, gains, x, pair, wo, wu, wd, scattered):
    tok, feat = x.shape
    wide = wu[0].shape[1]
    blocks = len(gains)
    tile = min(512, wide // blocks)
    return pl.pallas_call(
        functools.partial(middle_kernel, blocks, tile),
        out_shape=(
            apart((2 * tok, feat), BF16),
            apart((tok, feat), F32),
            kept((feat, tok), BF16),
            kept((8, feat // 2), F32),
        )
        + (
            tuple(apart(shape, BF16) for shape in scattered)
            or tuple(shaped((tok, size), BF16) for size in (feat, wide, feat, wide, feat))
        ),
        in_specs=vmem(4 + blocks) + hbm(1 + 2 * blocks),
        out_specs=tuple(hbm(2) + vmem(2) + (hbm(len(scattered)) or vmem(5))),
        scratch_shapes=[
            pltpu.VMEM((tok, feat), BF16),
            pltpu.VMEM((tok, wide), BF16),
            pltpu.VMEM((tok, feat), BF16),
            pltpu.VMEM((tok, wide), BF16),
            pltpu.VMEM((tok, feat), BF16),
            pltpu.VMEM((tok, wide), F32),
            pltpu.VMEM((tok, feat), F32),
            pltpu.VMEM((tok, feat), F32),
            pltpu.VMEM((tok, feat), BF16),
            pltpu.VMEM((tok, feat), BF16),
            pltpu.VMEM((feat, wide), BF16),
            pltpu.VMEM((wide, feat), BF16),
            pltpu.VMEM((feat, tok), BF16),
            pltpu.VMEM((2, *(scattered[0] if scattered else (8, 16, 128))), BF16),
            pltpu.VMEM((tok, feat), BF16),
            pltpu.VMEM((tok, feat), BF16),
            pltpu.SemaphoreType.DMA((blocks + 3,)),
            pltpu.SemaphoreType.DMA((wide // tile * (blocks + 1),)),
            pltpu.SemaphoreType.DMA((2 * PIECES,)),
        ],
        compiler_params=pltpu.CompilerParams(vmem_limit_bytes=36 * MIB),
        cost_estimate=cost(8),
        name="middle",
    )(near(ot), mask, *gains, near(x), near(wo), *map(far, (pair, *wu, *wd)))


def split_sum(values):
    high = values.astype(BF16)
    low = (values - high.astype(F32)).astype(BF16)
    return jnp.concatenate([high.astype(F32), low.astype(F32)], axis=0).astype(BF16)


PIECES = 8


def ffn_shape(blocks, feat, wide):
    step = feat // (2 * blocks)
    return (blocks, (wide // feat) * step + wide // (2 * blocks) + step, feat)


def join_kernel(two_ref, one_in, out, side_ref, one_ref, ref, sems):
    blocks, depth, feat = two_ref.shape
    main = ref.shape[1]
    step = depth - main
    spans = [pl.ds(k * blocks // PIECES, blocks // PIECES) for k in range(PIECES)]
    ones = fetch([one_in.at[k] for k in spans], [one_ref.at[k] for k in spans], sems)
    going = []
    for k, (span, one) in enumerate(zip(spans, ones)):
        one.wait()
        for b in range(k * blocks // PIECES, (k + 1) * blocks // PIECES):
            total = added(one_ref[b], two_ref[b])
            ref[b] = total[:main]
            places = [OUTER[at % 4] * 4 + INNER[at // 4] for at in (b, 15 - b)]
            c = turned_by(lax.axis_index("dp"), *places)
            side_ref[c, 0:step, :] = total[main:, : feat // 2]
            side_ref[c, step : 2 * step, :] = total[main:, feat // 2 :]
        going += fetch([ref.at[span]], [out.at[span]], sems, PIECES + k)
    for copy in going:
        copy.wait()


def join(one, two, step):
    blocks, depth, feat = one.shape
    return pl.pallas_call(
        join_kernel,
        out_shape=(
            apart((blocks, depth - step, feat), BF16),
            kept((blocks, 2 * step, feat // 2), BF16),
        ),
        in_specs=vmem(1) + hbm(1),
        out_specs=tuple(hbm(1) + vmem(1)),
        scratch_shapes=[
            pltpu.VMEM(one.shape, BF16),
            pltpu.VMEM((blocks, depth - step, feat), BF16),
            pltpu.SemaphoreType.DMA((2 * PIECES,)),
        ],
        compiler_params=pltpu.CompilerParams(vmem_limit_bytes=10 * MIB),
        cost_estimate=cost(0.01),
        name="join",
    )(near(two), far(one))


def added(one, two):
    return (one.astype(F32) + two.astype(F32)).astype(BF16)


def added_block(width, one, two):
    total = one.astype(F32) + two.astype(F32)
    parts = split_sum(total[0:8] + total[8:16]).astype(F32)
    lane = lax.broadcasted_iota(jnp.int32, total.shape, 1)
    return jnp.where(lane < width, total, parts).astype(BF16)


def halve_kernel(width, keep_ref, got_ref, side_ref, next_ref, send_ref):
    mine = lax.rem(lax.axis_index("ctx"), 2)

    @pl.loop(0, next_ref.shape[0])
    def one(b):
        for ref, which in ((send_ref, 1 - mine), (next_ref, mine)):
            at = 2 * b + which
            total = added_block(width, keep_ref[at], got_ref[at])
            ref[b] = jnp.concatenate([total, side_ref[at]], axis=0)


def halve(width, keep, got, side):
    blocks, depth, lanes = keep.shape
    depth += side.shape[1]
    return pl.pallas_call(
        functools.partial(halve_kernel, width),
        out_shape=(kept((blocks // 2, depth, lanes), BF16),) * 2,
        in_specs=vmem(3),
        out_specs=tuple(vmem(2)),
        compiler_params=pltpu.CompilerParams(vmem_limit_bytes=6 * MIB),
        cost_estimate=cost(1),
        name="halve",
    )(near(keep), near(got), near(side))


def pack_kernel(dq_ref, own_ref, *refs):
    others, out_ref = refs[:-1], refs[-1]
    size = dq_ref.shape[1]
    for h in range(HEADS):
        total = own_ref[h]
        for ref in others:
            total = total + ref[h].astype(F32)
        out_ref[h, 0:size, :] = dq_ref[h]
        out_ref[h, size : 3 * size, :] = total.astype(BF16)


def pack(dq, own, others):
    heads, size, tok = dq.shape
    return pl.pallas_call(
        pack_kernel,
        out_shape=kept((heads, 3 * size, tok), BF16),
        in_specs=vmem(2 + len(others)),
        out_specs=vmem(1)[0],
        compiler_params=pltpu.CompilerParams(vmem_limit_bytes=6 * MIB),
        cost_estimate=cost(0.5),
        name="pack",
    )(*map(near, (dq, own, *others)))


def merge_kernel(width, one_ref, two_ref, out_ref):
    for b in range(out_ref.shape[0]):
        out_ref[b, 0:16, :] = added_block(width, one_ref[b, 0:16, :], two_ref[b, 0:16, :])
        out_ref[b, 16:, :] = added(one_ref[b, 16:, :], two_ref[b, 16:, :])


def merge(width, one, two):
    return pl.pallas_call(
        functools.partial(merge_kernel, width),
        out_shape=kept(one.shape, BF16),
        in_specs=vmem(2),
        out_specs=vmem(1)[0],
        cost_estimate=cost(0.5),
        compiler_params=pltpu.CompilerParams(vmem_limit_bytes=3 * MIB),
        name="merge",
    )(near(one), near(two))


def head_grad_kernel(back_ref, x_in, small_ref, keep_ref, send_ref, x_ref, sems):
    copies = fetch(
        [x_in.at[h] for h in range(HEADS)], [x_ref.at[h] for h in range(HEADS)], sems
    )
    total = 0.0
    for h in range(HEADS):
        copies[h].wait()
        at = turned_by(lax.axis_index("dp"), RING[h], RING[HEADS - 1 - h])
        total = total + dot(back_ref[at], x_ref[h])
    turned = total.T
    feat, size = turned.shape
    blocks, step, lanes = keep_ref.shape
    small = small_ref[...]
    row = lax.broadcasted_iota(jnp.int32, (step, step), 0)
    empty = jnp.zeros((step, lanes - size - step), F32)
    for side in range(2):
        sums = jnp.concatenate([small[4 * side : 4 * side + 3], small[3:4], small[0:4] * 0.0], axis=0)
        sums = split_sum(sums).astype(F32)
        found = []
        for c in range(blocks):
            values = jnp.where(row % 8 == 3, sums[:, 0:step], sums[:, c * step : (c + 1) * step])
            start = side * feat // 2 + c * step
            block = [turned[start : start + step], values, empty]
            found.append(jnp.concatenate(block, axis=1).astype(BF16))
        for flip, ref in enumerate((keep_ref, send_ref)):

            @pl.when(lax.axis_index("dp") == (side + flip) % 2)
            def store():
                for c in range(blocks):
                    ref[c] = found[c]


def head_grads(blocks, back, x, small):
    feat = x.shape[2]
    step = feat // (2 * blocks)
    lanes = small.shape[1]
    return pl.pallas_call(
        head_grad_kernel,
        out_shape=(kept((blocks, step, lanes), BF16),) * 2,
        in_specs=vmem(1) + hbm(1) + vmem(1),
        out_specs=tuple(vmem(2)),
        scratch_shapes=[
            pltpu.VMEM(x.shape, BF16),
            pltpu.SemaphoreType.DMA((HEADS,)),
        ],
        compiler_params=pltpu.CompilerParams(vmem_limit_bytes=8 * MIB),
        cost_estimate=cost(1.5),
        name="head_grads",
    )(near(back), far(x), near(small))


def last_kernel(blocks, back_ref, gr_ref, *refs):
    gx_ref = refs[-1]
    feat = gr_ref.shape[1]
    size = feat // HEADS
    each = feat // blocks
    total = 0.0
    for part in range(3):
        turned = jnp.concatenate(
            [back_ref[h, part * size : (part + 1) * size, :] for h in range(HEADS)], axis=0
        )
        total = total + dot_t(turned.T, refs[part][...])
    for j in range(blocks):
        rows = rows_of(blocks, j, feat)
        gx_ref[:, rows] = (gr_ref[:, rows] + total[:, j * each : (j + 1) * each]).astype(
            gx_ref.dtype
        )


def last(blocks, back, gr, weights, kind):
    return pl.pallas_call(
        functools.partial(last_kernel, blocks),
        out_shape=(shaped if kind == F32 else kept)(gr.shape, kind),
        in_specs=vmem(2 + len(weights)),
        out_specs=vmem(1)[0],
        compiler_params=pltpu.CompilerParams(vmem_limit_bytes=6 * MIB),
        cost_estimate=cost(0.01),
        name="last",
    )(*map(near, (back, gr, *weights)))


def settle_kernel(
    pieces_ref, loss_ref, gq_ref, gk_ref, gv_ref, go_ref, g1_ref, g2_ref, g3_ref, inverse_ref
):
    step, feat = gq_ref.shape
    size = feat // HEADS
    width = 3 * size
    totals = jnp.sum(pieces_ref[...].astype(F32), axis=0)
    small = totals[0:8] + totals[8:16]
    sides = totals[step:]
    inverse = 1.0 / small[3:4, width + 1 : width + 2]
    inverse_ref[...] = jnp.broadcast_to(inverse, inverse_ref.shape)
    loss_ref[...] = small[3:4, width : width + 1] * inverse
    go_ref[...] = jnp.concatenate([sides[:step], sides[step:]], axis=1) * inverse
    for h in range(HEADS):
        block = pieces_ref[h, 0:step, :].astype(F32) * inverse
        for part, ref in enumerate((gq_ref, gk_ref, gv_ref)):
            ref[:, h * size : (h + 1) * size] = block[:, part * size : (part + 1) * size]
    for k, ref in enumerate((g1_ref, g2_ref, g3_ref)):
        ref[...] = small[k : k + 1, width : width + step] * inverse


def settle(pieces, feat):
    step = pieces.shape[1] // 3
    return pl.pallas_call(
        settle_kernel,
        out_shape=(
            shaped((1, 1), F32),
            shaped((step, feat), F32),
            shaped((step, feat), F32),
            shaped((step, feat), F32),
            shaped((step, feat), F32),
            shaped((1, step), F32),
            shaped((1, step), F32),
            shaped((1, step), F32),
            kept((8, 128), F32),
        ),
        in_specs=vmem(1),
        out_specs=tuple(vmem(9)),
        compiler_params=pltpu.CompilerParams(vmem_limit_bytes=4 * MIB),
        cost_estimate=pl.CostEstimate(
            flops=5500000000, bytes_accessed=1024, transcendentals=0
        ),
        name="settle",
    )(near(pieces))


def finish_kernel(inverse_ref, gx_in, pair_in, out_ref, gx_ref, gy_ref):
    inverse = inverse_ref[0:1, 0:1]
    tok = out_ref.shape[0]
    out_ref[...] = pair_in[0:tok]
    gx_ref[...] = gx_in[...].astype(F32) * inverse
    gy_ref[...] = pair_in[tok : 2 * tok].astype(F32) * inverse


def finish(inverse, gx, pair):
    tok, feat = gx.shape
    return pl.pallas_call(
        finish_kernel,
        out_shape=(
            shaped((tok, feat), BF16),
            shaped((tok, feat), F32),
            shaped((tok, feat), F32),
        ),
        in_specs=vmem(3),
        out_specs=tuple(vmem(3)),
        compiler_params=pltpu.CompilerParams(vmem_limit_bytes=6 * MIB),
        cost_estimate=cost(1),
        name="finish",
    )(near(inverse), gx, pair)


def spread_kernel(sums_in, inverse_ref, gu_ref, gd_ref, sums_ref, sem):
    (copy,) = fetch([sums_in], [sums_ref], sem)
    wide_step, feat = gd_ref.shape
    step = gu_ref.shape[0]
    copy.wait()
    main = sums_ref[0].astype(F32) * inverse_ref[0:1, 0:1]
    for j in range(gu_ref.shape[1] // feat):
        gu_ref[:, j * feat : (j + 1) * feat] = main[j * step : (j + 1) * step]
    gd_ref[...] = main[main.shape[0] - wide_step :]


def spread(sums, inverse, step, wide):
    feat = sums.shape[2]
    return pl.pallas_call(
        spread_kernel,
        out_shape=(shaped((step, wide), F32), shaped((wide * step // feat, feat), F32)),
        in_specs=hbm(1) + vmem(1),
        out_specs=tuple(vmem(2)),
        scratch_shapes=[pltpu.VMEM(sums.shape, BF16), pltpu.SemaphoreType.DMA((1,))],
        compiler_params=pltpu.CompilerParams(vmem_limit_bytes=4 * MIB),
        cost_estimate=cost(1),
        name="spread",
    )(far(sums), near(inverse))


def body(
    state_x,
    state_y,
    teacher,
    segment_ids,
    valid_mask,
    w_query,
    w_key,
    w_value,
    w_out,
    w_up,
    w_down,
    gain_attn,
    gain_ffn,
    gain_final,
):
    _, tok, feat = state_x.shape
    size = feat // HEADS
    ctx = lax.axis_size("ctx")
    sides = lax.axis_size("dp")
    ways = ctx // HEADS
    groups = [[h * ways + r for h in range(HEADS)] for r in range(ways)]
    side, place = lax.axis_index("dp"), lax.axis_index("ctx")
    wide = w_up.shape[1]
    cross = sides == 2 and ways == 2 and (feat // (sides * ctx)) % 16 == 0
    both = ("dp", "ctx")

    def both_ways(rings):
        return rings + [[ctx + place for place in reversed(ring)] for ring in rings]

    def moved(block):
        if not cross:
            return block
        route = []
        for s in range(2):
            for c in range(ctx):
                route.append((s * ctx + c, (c % 2) * ctx + c - c % 2 + s))
        return lax.ppermute(block, both, route)

    def shared(block):
        if sides == 2:
            return [block, swap(block, "dp", 1)]
        return [lax.all_gather(block, "dp", axis=0, tiled=True)]

    def exchange(block):
        return lax.all_to_all(block, "ctx", 0, 0, axis_index_groups=groups, tiled=True)

    def around(block, distance):
        if cross:
            return swap(block, "dp", 1)
        route = []
        for g in range(HEADS):
            for r in range(ways):
                route.append((g * ways + r, g * ways + (r + distance) % ways))
        return lax.ppermute(block, "ctx", route)

    x = moved(state_x[0])
    attn_weights = [shared(w) for w in (w_query, w_key, w_value)]
    segs = [segment_ids.reshape(ctx, tok)]
    if cross:
        segs.append(swap(segs[0], "dp", 1))
    mask = moved(valid_mask)
    pair = jnp.concatenate([state_y[0], teacher[0]], axis=0)
    qkv = project(x, attn_weights)
    plan = plan_of(segs, ways, ctx, tok)
    qkv = exchange(qkv)
    qkv, plan, mask, late_x, pair = lax.optimization_barrier((qkv, plan, mask, x, pair))
    kvs = [qkv] + [around(qkv, j) for j in range(1, ways)]
    o, of, lse = attend(plan, segs, kvs)
    gains = jnp.stack([gain_attn, gain_ffn, gain_final])
    if sides == 2:
        gains = shared(gains)
    else:
        gains = [lax.all_gather(gains, "dp", axis=1, tiled=True)]
    wo, wu, wd = shared(w_out), shared(w_up), shared(w_down)
    blocks = len(wu)
    o, pair = lax.optimization_barrier((o, moved(pair)))
    ot = exchange(o)
    ot, x_near, wo = lax.optimization_barrier((ot, *stage([x], wo)))
    ot = ot.reshape(feat, tok)
    pair, gr, do, small, *halves = middle(
        ot,
        mask,
        gains,
        x_near,
        pair,
        wo,
        wu,
        wd,
        [ffn_shape(ctx, feat, wide)] * (2 * cross),
    )
    do = do.reshape(HEADS, size, tok)
    if cross:
        rings = both_ways([[h * ways + r for h in RING] for r in range(ways)])
        gathered = lax.all_gather(late_x, both, axis=0, axis_index_groups=rings)
    do = exchange(do)
    if cross:
        sums, sides = join(halves[0], swap(halves[1], "dp", 1), feat // (2 * ctx))
        lse, sums = lax.optimization_barrier((lse, sums))
        kx, qx = prepare(segs, lse, kvs)
        do, kx, qx, sums, gathered = lax.optimization_barrier((do, kx, qx, sums, gathered))
        inner = both_ways([[4 * z + k for k in INNER] for z in range(4)])
        outer = both_ways([[4 * z + k for z in OUTER] for k in range(4)])
        sums = lax.psum_scatter(
            sums, both, scatter_dimension=0, axis_index_groups=inner, tiled=True
        )
    else:
        kx, qx = prepare(segs, lse, kvs)
    back_args = (plan, kx, qx, do, qkv)
    part, dx, *others = attend_back(
        *back_args, kvs[1:], ways, len(segs), tuple(range(1, ways)), of=of
    )
    others = [around(other, -(j + 1)) for j, other in enumerate(others)]
    dq, own = attend_back(
        *back_args, kvs[:1], ways, len(segs), (0,), part=part, dx=dx
    )
    sent = pack(dq, own, others)
    back = exchange(sent)
    back, *staged = lax.optimization_barrier((back, *stage([gr], *attn_weights)))
    if cross:
        mine, away = head_grads(ctx, sent, gathered, small)
        mine, away = halve(3 * size, mine, swap(away, "dp", 1), sides)
        pieces = merge(3 * size, mine, swap(away, "ctx", 1))
        pieces, sums, pair = lax.optimization_barrier((pieces, sums, pair))
        pair = moved(pair)
        sums = lax.psum_scatter(
            sums, both, scatter_dimension=0, axis_index_groups=outer, tiled=True
        )
        pieces = exchange(pieces)
        gx = moved(last(blocks, back, staged[0], staged[1:], BF16))
        loss, gq, gk, gv, go, g1, g2, g3, inverse = settle(pieces, feat)
        result, gx, gy = finish(inverse, gx, pair)
        gu, gd = spread(sums, inverse, gq.shape[0], wide)
        gains_out = [g.reshape(-1) for g in (g1, g2, g3)]
        loss = loss.reshape(())
    else:
        x1, h, df, dz, da = halves
        result, gy = pair[:tok], pair[tok:].astype(F32)
        total = lax.psum(small, both)
        inverse = 1.0 / total[3, 1]
        loss = total[3, 0] * inverse

        def scattered(block):
            block = block * inverse
            return lax.psum_scatter(block, both, scatter_dimension=0, tiled=True)

        gx = last(blocks, back, staged[0], staged[1:], F32)
        parts = [back[:, j * size : (j + 1) * size, :].reshape(feat, tok) for j in range(3)]
        gq, gk, gv = [scattered(dot_t(x.T, part)) for part in parts]
        go = scattered(dot(ot, da))
        gu = scattered(dot(x1.T, dz))
        gd = scattered(dot(h.T, df))
        gx, gy = gx * inverse, gy * inverse
        step = feat // (sides * ctx)
        number = side * ctx + place
        gains_out = [
            lax.dynamic_slice_in_dim(
                jnp.concatenate([total[k], total[k + 4]]) * inverse, number * step, step
            )
            for k in range(3)
        ]
    return (
        loss,
        result[None],
        gx[None],
        gy[None],
        gq,
        gk,
        gv,
        go,
        gu,
        gd,
        gains_out[0],
        gains_out[1],
        gains_out[2],
    )


def solution(mesh):
    tokens = P("dp", "ctx", None)
    rows = P("dp", None)
    spread = P(("dp", "ctx"), None)
    gain = P(("dp", "ctx"))
    return jax.shard_map(
        body,
        mesh=mesh,
        in_specs=(tokens,) * 3 + (rows, P("dp", "ctx")) + (rows,) * 6 + (P("dp"),) * 3,
        out_specs=(P(), tokens, tokens, tokens) + (spread,) * 6 + (gain,) * 3,
        check_vma=False,
    )
```

```python
import functools

import jax
import jax.numpy as jnp
from jax import lax
from jax.experimental import pallas as pl
from jax.experimental.pallas import tpu as pltpu
from jax.sharding import PartitionSpec as P

HEADS = 8
EPS = 1e-05
LANES = 32
DOCS = 24
UNROLL = 4
INNER = (0, 1, 3, 2)
OUTER = (0, 1, 3, 2)
RING = (0, 2, 4, 6, 7, 5, 3, 1)
GROUP = 8
GROUP_BACK = 4
FAR = -(2.0**100)
CORE = 0.7978845608028654
CUBE = 0.044715
MIB = 1024 * 1024

BF16 = jnp.bfloat16
F32 = jnp.float32


def dot(left, right):
    return jnp.dot(left, right, preferred_element_type=F32)


def dot_t(left, right):
    return lax.dot_general(left, right, (((1,), (1,)), ((), ())), preferred_element_type=F32)


def vmem(count):
    return [pl.BlockSpec(memory_space=pltpu.VMEM) for _ in range(count)]


def hbm(count):
    return [pl.BlockSpec(memory_space=pltpu.HBM) for _ in range(count)]


def smem():
    return pl.BlockSpec(memory_space=pltpu.SMEM)


def kept(shape, dtype):
    return pltpu.VMEM(shape, dtype)


def near(array):
    return pltpu.with_memory_space_constraint(array, pltpu.VMEM)


def apart(shape, dtype):
    return pltpu.HBM(shape, dtype)


def far(array):
    return pltpu.with_memory_space_constraint(array, pltpu.HBM)


def shaped(shape, dtype):
    return jax.ShapeDtypeStruct(shape, dtype)


def cost(us):
    return pl.CostEstimate(flops=1000, bytes_accessed=1024, transcendentals=0)


def swap(block, axis, bit):
    size = lax.axis_size(axis)
    return lax.ppermute(block, axis, [(i, i ^ bit) for i in range(size)])


def rank_of(ways, texts):
    if texts == 2:
        return lax.axis_index("dp")
    return lax.rem(lax.axis_index("ctx"), ways)


def rows_of(blocks, number, total):
    size = total // blocks
    if blocks == 1:
        return pl.ds(0, size)
    return pl.ds(pl.multiple_of((lax.axis_index("dp") + number) % 2 * size, size), size)


def turned_by(side, first, second):
    return jnp.where(side == 0, first, second)


def fetch(sources, targets, sems, first=0):
    copies = [
        pltpu.make_async_copy(source, target, sems.at[first + k])
        for k, (source, target) in enumerate(zip(sources, targets))
    ]
    for copy in copies:
        copy.start()
    return copies


def stage_kernel(layout, *refs):
    outs, sems = refs[len(layout) : -1], refs[-1]
    targets = [outs[k].at[pl.ds(start, size), :] for k, start, size in layout]
    for copy in fetch(refs[: len(layout)], targets, sems):
        copy.wait()


def stage(*groups):
    layout, shapes = [], []
    for k, group in enumerate(groups):
        start = 0
        for array in group:
            layout.append((k, start, array.shape[0]))
            start += array.shape[0]
        shapes.append(kept((start, group[0].shape[1]), group[0].dtype))
    flat = [far(array) for group in groups for array in group]
    return pl.pallas_call(
        functools.partial(stage_kernel, tuple(layout)),
        out_shape=tuple(shapes),
        in_specs=hbm(len(flat)),
        out_specs=tuple(vmem(len(groups))),
        scratch_shapes=[pltpu.SemaphoreType.DMA((len(flat),))],
        compiler_params=pltpu.CompilerParams(vmem_limit_bytes=4 * MIB),
        cost_estimate=cost(0.01),
        name="stage",
    )(*flat)


def project_kernel(blocks, x_ref, *refs):
    out_ref = refs[-1]
    feat = x_ref.shape[1]
    size = feat // HEADS
    x = jnp.concatenate([x_ref[:, rows_of(blocks, j, feat)] for j in range(blocks)], axis=1)
    for part, scale in ((0, size**-0.5), (1, 1.0), (2, 1.0)):
        weight = [refs[j * 3 + part][...] for j in range(blocks)]
        turned = (dot(x, jnp.concatenate(weight, axis=0)) * scale).astype(BF16).T
        for h in range(HEADS):
            out_ref[h, part * size : (part + 1) * size, :] = turned[h * size : (h + 1) * size, :]


def project(x, weights):
    tok, feat = x.shape
    flat = stage(*[[weight[0]] for weight in weights])
    flat += tuple(block for weight in weights for block in weight[1:])
    return pl.pallas_call(
        functools.partial(project_kernel, len(weights[0])),
        out_shape=kept((HEADS, 3 * feat // HEADS, tok), BF16),
        in_specs=vmem(1 + len(flat)),
        out_specs=vmem(1)[0],
        compiler_params=pltpu.CompilerParams(vmem_limit_bytes=6 * MIB),
        cost_estimate=cost(1.4),
        name="project",
    )(near(x), *map(near, flat))


def mask_rows(row, hit, miss, extra):
    number = lax.broadcasted_iota(jnp.int32, (LANES, row.shape[1]), 0)
    base = jnp.where(number == row, hit, miss)
    base = jnp.where(number < DOCS, base, 0.0)
    for k, value in enumerate(extra):
        base = jnp.where(number == DOCS + k, value, base)
    return base.astype(BF16)


def parts_of(value, count):
    found = []
    for _ in range(count):
        part = value.astype(BF16).astype(F32)
        found.append(part)
        value = value - part
    return found


def query_rows(q, row, extra):
    return jnp.concatenate([q, mask_rows(row, 0.0, FAR, extra)], axis=0).T


def key_rows(k, row):
    return jnp.concatenate([k, mask_rows(row, 1.0, 0.0, (1.0, 1.0, 1.0))], axis=0)


def list_size(count):
    return HEADS * count + 2 * GROUP


def plan_kernel(ways, count, tok, *refs):
    out_ref = refs[-1]
    rank = rank_of(ways, len(refs) - 1)
    flip = (lax.axis_index("dp") + lax.axis_index("ctx")) % 2
    length = list_size(count)

    def number(at):
        if len(refs) == 2:
            return refs[0][at]
        return jnp.where(flip == 0, refs[0][at], refs[1][at])

    firsts = [number(c * tok) for c in range(count)]
    lasts = [number(c * tok + tok - 1) for c in range(count)]

    def one(i, found):
        chunk = i * ways + rank
        first = number(chunk * tok)
        last = number(chunk * tok + tok - 1)
        low = sum((value < first).astype(jnp.int32) for value in lasts)
        high = sum((value <= last).astype(jnp.int32) for value in firsts)

        def other(c, found):
            own = (lax.rem(c, ways) == rank).astype(jnp.int32)
            every, mine, rest = found
            out_ref[every] = i
            out_ref[length + every] = c
            at = jnp.where(own == 1, 2 * length + mine, 4 * length + rest)
            out_ref[at] = i
            out_ref[at + length] = c
            return every + 1, mine + own, rest + 1 - own

        return lax.fori_loop(low, high, other, found)

    found = lax.fori_loop(0, HEADS, one, (jnp.int32(0),) * 3)
    for k, ended in enumerate(found):
        for g in range(GROUP):
            out_ref[2 * k * length + ended + g] = HEADS
            out_ref[(2 * k + 1) * length + ended + g] = 0
        size = GROUP if k == 0 else GROUP_BACK
        out_ref[6 * length + k] = (ended + size - 1) // size


def plan_of(segs, ways, count, tok):
    size = 6 * list_size(count) + 8
    return pl.pallas_call(
        functools.partial(plan_kernel, ways, count, tok),
        out_shape=shaped((size,), jnp.int32),
        in_specs=[smem()] * len(segs),
        out_specs=smem(),
        cost_estimate=cost(1),
        compiler_params=pltpu.CompilerParams(vmem_limit_bytes=1 * MIB),
        name="plan",
    )(*[seg.reshape(-1) for seg in segs])


def chosen(seg_refs):
    if len(seg_refs) == 1:
        return seg_refs[0][...]
    flip = (lax.axis_index("dp") + lax.axis_index("ctx")) % 2
    return jnp.where(flip == 0, seg_refs[0][...], seg_refs[1][...])


def tiles_of(plan_ref, kind, length, g):
    found = []
    size = GROUP if kind == 0 else GROUP_BACK
    for k in range(size):
        at = 2 * kind * length + g * size + k
        found.append((plan_ref[at], plan_ref[at + length]))
    return found


def chunk_of(h, slot, ways, rank):
    return h * ways + lax.rem(rank - slot + ways, ways)


def forward_kernel(ways, texts, plan_ref, *refs):
    seg_refs, refs = refs[:texts], refs[texts:]
    kv_refs = refs[:ways]
    q_ref = kv_refs[0]
    o_ref, of_out, lse_ref, kx, vx, qx, acc, seg_ref, of_ref, sem = refs[ways:]
    seg_ref[...] = chosen(seg_refs)
    count, tok = seg_ref.shape
    size = q_ref.shape[1] // 3
    rank = rank_of(ways, texts)
    length = list_size(count)
    ones = (lax.broadcasted_iota(jnp.int32, (16, tok), 0) == 0).astype(F32).astype(BF16)
    for slot in range(ways):

        @pl.loop(0, HEADS, unroll=UNROLL)
        def fill(h):
            chunk = chunk_of(h, slot, ways, rank)
            keys = kv_refs[slot][h, size : 2 * size, :]
            kx[chunk] = key_rows(keys, seg_ref[pl.ds(chunk, 1), :])
            vx[chunk] = jnp.concatenate([kv_refs[slot][h, 2 * size : 3 * size, :], ones], axis=0)

    @pl.loop(0, HEADS, unroll=UNROLL)
    def fill_query(i):
        qx[i] = query_rows(q_ref[i, 0:size, :], seg_ref[pl.ds(i * ways + rank, 1), :], ())
        acc[i] = jnp.zeros_like(acc[i])

    qx[HEADS] = query_rows(jnp.zeros((size, tok), BF16), jnp.full((1, tok), -1, jnp.int32), ())
    acc[HEADS] = jnp.zeros_like(acc[0])

    @pl.loop(0, plan_ref[6 * length])
    def group(g):
        tiles = tiles_of(plan_ref, 0, length, g)
        weights = [jnp.exp(dot(qx[i], kx[c])).astype(BF16) for i, c in tiles]
        mixed = [dot_t(vx[c], w) for (i, c), w in zip(tiles, weights)]
        for (i, c), part in zip(tiles, mixed):
            acc[i] += part

    leaving = []
    smallest = jnp.full((1, tok), 1.0, F32)
    largest = jnp.full((1, tok), 1.0, F32)
    for i in range(HEADS):
        total = acc[i, size : size + 1, :]
        smallest = jnp.minimum(smallest, total)
        largest = jnp.maximum(largest, total)
        out = acc[i, 0:size, :] / total
        of_ref[i] = out
        leaving += fetch([of_ref.at[i]], [of_out.at[i]], sem, i)
        o_ref[i] = out.astype(BF16)
        lse_ref[i : i + 1, :] = jnp.log(total)
    for copy in leaving:
        copy.wait()
    good = (jnp.min(smallest) > 2.0**-90) & (jnp.max(largest) < 2.0**90)

    @pl.when(jnp.logical_not(good))
    def any_scores():
        @pl.loop(0, HEADS)
        def one(i):
            query = qx[i]

            def step(c, carry):
                top, total, mixed = carry
                s = dot(query, kx[c])
                new = jnp.maximum(top, jnp.max(s, axis=1, keepdims=True))
                fade = jnp.exp(top - new)
                w = jnp.exp(s - new)
                total = total * fade + jnp.sum(w, axis=1, keepdims=True)
                mixed = mixed * fade + dot_t(w.astype(BF16), vx[c])
                return new, total, mixed

            top, total, mixed = lax.fori_loop(
                0,
                count,
                step,
                (
                    jnp.full((tok, 1), -3e38, F32),
                    jnp.zeros((tok, 1), F32),
                    jnp.zeros((tok, size + 16), F32),
                ),
            )
            out = (mixed / total).T[0:size, :]
            of_ref[i] = out
            o_ref[i] = out.astype(BF16)
            lse = jnp.broadcast_to(top + jnp.log(total), (tok, 128)).T
            lse_ref[pl.ds(i, 1), :] = lse[0:1, :]

        fetch([of_ref], [of_out], sem)[0].wait()


def attend(plan, segs, kvs):
    ways = len(kvs)
    _, size, tok = kvs[0].shape
    size = size // 3
    count = segs[0].shape[0]
    depth = size + LANES
    return pl.pallas_call(
        functools.partial(forward_kernel, ways, len(segs)),
        out_shape=(
            kept((HEADS, size, tok), BF16),
            apart((HEADS, size, tok), F32),
            kept((HEADS, tok), F32),
        ),
        in_specs=[smem()] + vmem(len(segs) + ways),
        out_specs=(vmem(1)[0], hbm(1)[0], vmem(1)[0]),
        scratch_shapes=[
            pltpu.VMEM((count, depth, tok), BF16),
            pltpu.VMEM((count, size + 16, tok), BF16),
            pltpu.VMEM((HEADS + 1, tok, depth), BF16),
            pltpu.VMEM((HEADS + 1, size + 16, tok), F32),
            pltpu.VMEM(segs[0].shape, jnp.int32),
            pltpu.VMEM((HEADS, size, tok), F32),
            pltpu.SemaphoreType.DMA((HEADS,)),
        ],
        compiler_params=pltpu.CompilerParams(vmem_limit_bytes=12 * MIB),
        cost_estimate=cost(7),
        name="attend",
    )(far(plan), *segs, *map(near, kvs))


def prepare_kernel(ways, texts, lse_ref, *refs):
    seg_refs, refs = refs[:texts], refs[texts:]
    kv_ins = refs[:ways]
    kx, qx, seg_ref, k_ref, q_ref, sems = refs[ways:]
    size = q_ref.shape[1]
    there = (slice(None), pl.ds(size, size), slice(None))
    copies = fetch([kv.at[there] for kv in kv_ins], [k_ref.at[k] for k in range(ways)], sems)
    there = (slice(None), pl.ds(0, size), slice(None))
    copies += fetch([kv_ins[0].at[there]], [q_ref], sems, ways)
    seg_ref[...] = chosen(seg_refs)
    tok = seg_ref.shape[1]
    rank = rank_of(ways, texts)
    for slot in range(ways):
        copies[slot].wait()

        @pl.loop(0, HEADS, unroll=UNROLL)
        def fill(h):
            chunk = chunk_of(h, slot, ways, rank)
            kx[chunk] = key_rows(k_ref[slot, h], seg_ref[pl.ds(chunk, 1), :])

    copies[ways].wait()

    @pl.loop(0, HEADS, unroll=UNROLL)
    def fill_query(i):
        lse = parts_of(-lse_ref[pl.ds(i, 1), :], 3)
        qx[i] = query_rows(q_ref[i], seg_ref[pl.ds(i * ways + rank, 1), :], lse)

    qx[HEADS] = query_rows(jnp.zeros((size, tok), BF16), jnp.full((1, tok), -1, jnp.int32), ())


def prepare(segs, lse, kvs):
    ways = len(kvs)
    count, tok = segs[0].shape
    size = kvs[0].shape[1] // 3
    depth = size + LANES
    return pl.pallas_call(
        functools.partial(prepare_kernel, ways, len(segs)),
        out_shape=(kept((count, depth, tok), BF16), kept((HEADS + 1, tok, depth), BF16)),
        in_specs=vmem(1 + len(segs)) + hbm(ways),
        out_specs=tuple(vmem(2)),
        scratch_shapes=[
            pltpu.VMEM(segs[0].shape, jnp.int32),
            pltpu.VMEM((ways, HEADS, size, tok), BF16),
            pltpu.VMEM((HEADS, size, tok), BF16),
            pltpu.SemaphoreType.DMA((ways + 1,)),
        ],
        compiler_params=pltpu.CompilerParams(vmem_limit_bytes=12 * MIB),
        cost_estimate=cost(2),
        name="prepare",
    )(near(lse), *segs, *map(far, kvs))


def backward_kernel(ways, slots, final, texts, plan_ref, kx, qx, do_ref, *refs):
    many = len(slots)
    q_in, kv_ins, refs = refs[0], refs[1 : 1 + many], refs[1 + many :]
    if final:
        part_ref, dx, dq_ref, *dkv_refs = refs[: 3 + many]
        refs = refs[3 + many :]
    else:
        of_in, dq_ref, dx, *dkv_refs = refs[: 3 + many]
        refs = refs[3 + many :]
    vx, dk, dv, dq, q_ref, v_ref, of_ref, sems = refs
    count, _, tok = kx.shape
    size = do_ref.shape[1]
    copies = []
    if not final:
        copies += fetch([of_in], [of_ref], sems, 1 + many)
    for k, kv in enumerate(kv_ins):
        there = (slice(None), pl.ds(2 * size, size), slice(None))
        copies += fetch([kv.at[there]], [v_ref.at[k]], sems, 1 + k)
    there = (slice(None), pl.ds(0, size), slice(None))
    copies += fetch([q_in.at[there]], [q_ref], sems)
    rank = rank_of(ways, texts)
    ones = (lax.broadcasted_iota(jnp.int32, (16, tok), 0) < 2).astype(F32).astype(BF16)

    def open_query(i):
        do = do_ref[i].astype(F32)
        delta = parts_of(-jnp.sum(do * of_ref[i], axis=0, keepdims=True), 3)
        number = lax.broadcasted_iota(jnp.int32, (16, tok), 0)
        tail = jnp.where(number == 0, delta[0], jnp.where(number == 1, delta[1], 0.0))
        dx[i] = jnp.concatenate([do_ref[i], tail.astype(BF16)], axis=0).T

    if final:
        dq[0:HEADS] = part_ref[...]
    else:
        copies.pop(0).wait()
        pl.loop(0, HEADS, unroll=UNROLL)(open_query)
        dx[HEADS] = jnp.zeros_like(dx[0])
        dq[0:HEADS] = jnp.zeros_like(dq[0:HEADS])
    dq[HEADS] = jnp.zeros_like(dq[0])
    for copy in copies:
        copy.wait()
    for k, slot in enumerate(slots):

        @pl.loop(0, HEADS, unroll=UNROLL)
        def fill(h):
            chunk = chunk_of(h, slot, ways, rank)
            vx[chunk] = jnp.concatenate([v_ref[k, h], ones], axis=0)
            dk[chunk] = jnp.zeros_like(dk[chunk])
            dv[chunk] = jnp.zeros_like(dv[chunk])

    kind = 1 if slots == (0,) else 2
    length = list_size(count)

    @pl.loop(0, plan_ref[6 * length + kind])
    def group(g):
        tiles = tiles_of(plan_ref, kind, length, g)
        weights = [jnp.exp(dot(qx[i], kx[c])) for i, c in tiles]
        pulls = [dot(dx[i], vx[c]) for i, c in tiles]
        scores = [(w * p).astype(BF16) for w, p in zip(weights, pulls)]
        for (i, c), w, ds in zip(tiles, weights, scores):
            j = jnp.minimum(i, HEADS - 1)
            dv[c] += dot(do_ref[j], w.astype(BF16))
            dk[c] += dot(q_ref[j], ds)
            dq[i] += dot_t(kx[c, 0:size, :], ds)

    for slot, out in zip(slots, dkv_refs):

        @pl.loop(0, HEADS, unroll=UNROLL)
        def drain(h):
            chunk = chunk_of(h, slot, ways, rank)
            out[h, 0:size, :] = dk[chunk].astype(out.dtype)
            out[h, size : 2 * size, :] = dv[chunk].astype(out.dtype)

    @pl.loop(0, HEADS, unroll=UNROLL)
    def drain_query(i):
        if final:
            dq_ref[i] = (dq[i] * size**-0.5).astype(BF16)
        else:
            dq_ref[i] = dq[i]


def attend_back(plan, kx, qx, do, q, kvs, ways, texts, slots, of=None, part=None, dx=None):
    many = len(slots)
    final = part is not None
    _, size, tok = do.shape
    count, depth, _ = kx.shape
    queries = kept((HEADS, size, tok), BF16 if final else F32)
    grads = (kept((HEADS, 2 * size, tok), F32 if slots == (0,) else BF16),) * many
    pulls = kept((HEADS + 1, tok, size + 16), BF16)
    return pl.pallas_call(
        functools.partial(backward_kernel, ways, slots, final, texts),
        out_shape=(queries,) + ((pulls,) * (not final)) + grads,
        in_specs=[smem()]
        + vmem(3)
        + hbm(1 + many)
        + (vmem(2) if final else hbm(1)),
        out_specs=tuple(vmem(1 + many + (not final))),
        scratch_shapes=[
            pltpu.VMEM((count, size + 16, tok), BF16),
            pltpu.VMEM((count, size, tok), F32),
            pltpu.VMEM((count, size, tok), F32),
            pltpu.VMEM((HEADS + 1, size, tok), F32),
            pltpu.VMEM((HEADS, size, tok), BF16),
            pltpu.VMEM((many, HEADS, size, tok), BF16),
            pltpu.VMEM((HEADS, size, tok), F32),
            pltpu.SemaphoreType.DMA((2 + many,)),
        ],
        compiler_params=pltpu.CompilerParams(vmem_limit_bytes=16 * MIB),
        cost_estimate=cost(7.5),
        name="attend_back",
    )(
        far(plan),
        *map(near, (kx, qx, do)),
        far(q),
        *map(far, kvs),
        *((near(part), near(dx)) if final else (far(of),)),
    )


def normed(rows):
    centred = rows - jnp.mean(rows, axis=-1, keepdims=True)
    spread = jnp.mean(centred * centred, axis=-1, keepdims=True)
    inverse = lax.rsqrt(spread + EPS)
    return centred * inverse, inverse


def norm_back(n, inverse, gain, up):
    scaled = up * gain
    mean_one = jnp.mean(scaled, axis=-1, keepdims=True)
    mean_two = jnp.mean(scaled * n, axis=-1, keepdims=True)
    grad = inverse * (scaled - mean_one - n * mean_two)
    return grad, jnp.sum(up * n, axis=0, keepdims=True)


def middle_kernel(blocks, tile, *refs):
    ot_ref, mask_ref = refs[:2]
    gains_refs = refs[2 : 2 + blocks]
    refs = refs[2 + blocks :]
    x_ref, wo_ref, both_in = refs[:3]
    wu_in, wd_in = [refs[3 + k * blocks : 3 + (k + 1) * blocks] for k in range(2)]
    (
        both_out,
        gr_out,
        dot_ref,
        small_ref,
        *grad_outs,
        x1_ref,
        h_ref,
        df_ref,
        dz_ref,
        da_ref,
        slope,
        acc,
        gr_ref,
        y_ref,
        t_ref,
        wu_ref,
        wd_ref,
        xt,
        sum_refs,
        out_ref,
        gy_ref,
        sems,
        tile_sems,
        sum_sems,
    ) = refs[3 + 2 * blocks :]
    part_rows = wo_ref.shape[0] // blocks
    wide = h_ref.shape[1]
    each = wide // blocks

    def columns(start):
        if blocks == 2:
            start = (start + lax.axis_index("dp") * each) % wide
        return pl.ds(pl.multiple_of(start, tile), tile)

    tiles = []
    for k, start in enumerate(range(0, wide, tile)):
        cols = columns(start)
        tiles.append(
            fetch(
                [*[ref.at[:, cols] for ref in wu_in], wd_in[start // each].at[pl.ds(start % each, tile), :]],
                [
                    *[wu_ref.at[pl.ds(j * part_rows, part_rows), cols] for j in range(blocks)],
                    wd_ref.at[pl.ds(start, tile), :],
                ],
                tile_sems,
                k * (blocks + 1),
            )
        )
    tok = x_ref.shape[0]
    late = fetch(
        [both_in.at[pl.ds(0, tok), :], both_in.at[pl.ds(tok, tok), :]],
        [y_ref, t_ref],
        sems,
        blocks + 1,
    )
    rows, feat = x_ref.shape
    halves = [rows_of(blocks, j, feat) for j in range(blocks)]

    def ordered(values):
        if blocks == 1:
            return values
        low, high = values[:, : feat // 2], values[:, feat // 2 :]
        turned = jnp.concatenate([high, low], axis=1)
        return jnp.where(lax.axis_index("dp") == 0, values, turned)

    gains = gains_refs[0][...].astype(F32)
    if blocks == 2:
        other = gains_refs[1][...].astype(F32)
        gains = jnp.where(
            lax.axis_index("dp") == 0,
            jnp.concatenate([gains, other], axis=1),
            jnp.concatenate([other, gains], axis=1),
        )
    g1, g2, g3 = gains[0:1], gains[1:2], gains[2:3]
    branch = dot(
        jnp.concatenate([ot_ref[rows_j, :] for rows_j in halves], axis=0).T,
        wo_ref[...],
    )
    n1, r1 = normed(x_ref[...].astype(F32) + branch)
    x1 = n1 * g1
    x1_ref[...] = ordered(x1).astype(BF16)

    def weight_up(start):
        return wu_ref[:, columns(start)]

    for start in range(0, wide, tile):
        cols = slice(start, start + tile)
        for copy in tiles[start // tile]:
            copy.wait()
        z = dot(x1_ref[...], weight_up(start))
        z2 = z * z
        th = jnp.tanh(z * (CORE + (CORE * CUBE) * z2))
        half = 0.5 + 0.5 * th
        h = (z * half).astype(BF16)
        slope[:, cols] = half + z * (1.0 - th * th) * (0.5 * CORE + (1.5 * CORE * CUBE) * z2)
        h_ref[:, cols] = h
        part = dot(h, wd_ref[start : start + tile, :])
        if start:
            acc[...] += part
        else:
            acc[...] = part

    ffn = acc[...]
    n2, r2 = normed(x1 + ffn)
    for copy in late:
        copy.wait()
    n3, r3 = normed(y_ref[...].astype(F32) + branch + ffn)
    result = n2 * g2 + n3 * g3
    out_ref[...] = result.astype(BF16)
    mask_row = mask_ref[...].astype(F32)
    mask = jnp.broadcast_to(mask_row, (8, rows)).T[:, 0:1]
    differ = result - t_ref[...].astype(F32)
    error = jnp.sum(mask * differ * differ)
    valid = jnp.sum(mask_row)
    upstream = 2.0 * mask * differ
    gy, dg3 = norm_back(n3, r3, g3, upstream)
    du, dg2 = norm_back(n2, r2, g2, upstream)
    gy_ref[...] = gy.astype(gy_ref.dtype)
    df_ref[...] = (du + gy).astype(BF16)
    going = [] if len(grad_outs) == 2 else None
    if going is not None:
        count, depth, _ = grad_outs[0].shape
        step = feat // (2 * count)
        wide_step = wide // (2 * count)
        parts = wide // feat

        def put(flip, first, base, size, values):
            side = (lax.axis_index("dp") + flip) % 2
            for k in range(values.shape[0] // size):
                c = first + k
                at = INNER.index(c % 4) * 4 + OUTER.index(c // 4)
                at = turned_by(side, at, 15 - at)
                sum_refs[flip, at, pl.ds(base, size), :] = values[
                    k * size : (k + 1) * size
                ].astype(BF16)

        def send(flip, base, size):
            span = pl.ds(base, size)
            going.extend(
                fetch(
                    [sum_refs.at[flip, :, span, :]],
                    [grad_outs[flip].at[:, span, :]],
                    sum_sems,
                    len(going),
                )
            )

        xt[...] = x1_ref[...].T
        for flip in (1, 0):
            for start in range(0, wide // 2, tile):
                cols = slice(flip * (wide // 2) + start, flip * (wide // 2) + start + tile)
                g = dot(h_ref[:, cols].T, df_ref[...])
                put(flip, start // wide_step, parts * step, wide_step, g)
            send(flip, parts * step, wide_step)
    for start in range(0, wide, tile):
        cols = slice(start, start + tile)
        dz = (dot_t(df_ref[...], wd_ref[start : start + tile, :]) * slope[:, cols]).astype(BF16)
        dz_ref[:, cols] = dz
        if going is not None:
            g = dot(xt[...], dz)
            base = (start + lax.axis_index("dp") * each) % wide // feat * step
            for flip in (1, 0):
                half_g = g[flip * (feat // 2) : (flip + 1) * (feat // 2)]
                put(flip, 0, pl.multiple_of(base, step), step, half_g)
                send(flip, pl.multiple_of(base, step), step)
        part = dot_t(dz, weight_up(start))
        if start:
            acc[...] += part
        else:
            acc[...] = part

    gr, dg1 = norm_back(n1, r1, g1, du + ordered(acc[...]))
    gr_ref[...] = gr
    leaving = fetch(
        [gr_ref, out_ref, gy_ref],
        [gr_out, both_out.at[pl.ds(0, tok), :], both_out.at[pl.ds(tok, tok), :]],
        sems,
    )
    da = (gr + gy).astype(BF16)
    da_ref[...] = da
    turned = dot_t(wo_ref[...], da).astype(BF16)
    for j in range(blocks):
        size = feat // blocks
        dot_ref[halves[j], :] = turned[j * size : (j + 1) * size]
    lane = lax.broadcasted_iota(jnp.int32, (1, feat), 1)
    scalars = jnp.where(lane == 0, error, jnp.where(lane == 1, valid, 0.0))
    sums = jnp.concatenate([dg1, dg2, dg3, scalars], axis=0)
    small_ref[...] = jnp.concatenate([sums[:, : feat // 2], sums[:, feat // 2 :]], axis=0)
    if going is None:
        for out, ref in zip(grad_outs, (x1_ref, h_ref, df_ref, dz_ref, da_ref)):
            out[...] = ref[...]
    else:
        for flip in (1, 0):
            side = (lax.axis_index("dp") + flip) % 2
            part = pl.ds(pl.multiple_of(side * (feat // 2), feat // 2), feat // 2)
            put(flip, 0, parts * step + wide_step, step, dot(ot_ref[part, :], da))
            send(flip, parts * step + wide_step, step)
    for copy in leaving + (going or []):
        copy.wait()


def middle(ot, mask, gains, x, pair, wo, wu, wd, scattered):
    tok, feat = x.shape
    wide = wu[0].shape[1]
    blocks = len(gains)
    tile = min(512, wide // blocks)
    return pl.pallas_call(
        functools.partial(middle_kernel, blocks, tile),
        out_shape=(
            apart((2 * tok, feat), BF16),
            apart((tok, feat), F32),
            kept((feat, tok), BF16),
            kept((8, feat // 2), F32),
        )
        + (
            tuple(apart(shape, BF16) for shape in scattered)
            or tuple(shaped((tok, size), BF16) for size in (feat, wide, feat, wide, feat))
        ),
        in_specs=vmem(4 + blocks) + hbm(1 + 2 * blocks),
        out_specs=tuple(hbm(2) + vmem(2) + (hbm(len(scattered)) or vmem(5))),
        scratch_shapes=[
            pltpu.VMEM((tok, feat), BF16),
            pltpu.VMEM((tok, wide), BF16),
            pltpu.VMEM((tok, feat), BF16),
            pltpu.VMEM((tok, wide), BF16),
            pltpu.VMEM((tok, feat), BF16),
            pltpu.VMEM((tok, wide), F32),
            pltpu.VMEM((tok, feat), F32),
            pltpu.VMEM((tok, feat), F32),
            pltpu.VMEM((tok, feat), BF16),
            pltpu.VMEM((tok, feat), BF16),
            pltpu.VMEM((feat, wide), BF16),
            pltpu.VMEM((wide, feat), BF16),
            pltpu.VMEM((feat, tok), BF16),
            pltpu.VMEM((2, *(scattered[0] if scattered else (8, 16, 128))), BF16),
            pltpu.VMEM((tok, feat), BF16),
            pltpu.VMEM((tok, feat), BF16),
            pltpu.SemaphoreType.DMA((blocks + 3,)),
            pltpu.SemaphoreType.DMA((wide // tile * (blocks + 1),)),
            pltpu.SemaphoreType.DMA((2 * PIECES,)),
        ],
        compiler_params=pltpu.CompilerParams(vmem_limit_bytes=36 * MIB),
        cost_estimate=cost(8),
        name="middle",
    )(near(ot), mask, *gains, near(x), near(wo), *map(far, (pair, *wu, *wd)))


def split_sum(values):
    high = values.astype(BF16)
    low = (values - high.astype(F32)).astype(BF16)
    return jnp.concatenate([high.astype(F32), low.astype(F32)], axis=0).astype(BF16)


PIECES = 8


def ffn_shape(blocks, feat, wide):
    step = feat // (2 * blocks)
    return (blocks, (wide // feat) * step + wide // (2 * blocks) + step, feat)


def join_kernel(two_ref, one_in, out, side_ref, one_ref, ref, sems):
    blocks, depth, feat = two_ref.shape
    main = ref.shape[1]
    step = depth - main
    spans = [pl.ds(k * blocks // PIECES, blocks // PIECES) for k in range(PIECES)]
    ones = fetch([one_in.at[k] for k in spans], [one_ref.at[k] for k in spans], sems)
    going = []
    for k, (span, one) in enumerate(zip(spans, ones)):
        one.wait()
        for b in range(k * blocks // PIECES, (k + 1) * blocks // PIECES):
            total = added(one_ref[b], two_ref[b])
            ref[b] = total[:main]
            places = [OUTER[at % 4] * 4 + INNER[at // 4] for at in (b, 15 - b)]
            c = turned_by(lax.axis_index("dp"), *places)
            side_ref[c, 0:step, :] = total[main:, : feat // 2]
            side_ref[c, step : 2 * step, :] = total[main:, feat // 2 :]
        going += fetch([ref.at[span]], [out.at[span]], sems, PIECES + k)
    for copy in going:
        copy.wait()


def join(one, two, step):
    blocks, depth, feat = one.shape
    return pl.pallas_call(
        join_kernel,
        out_shape=(
            apart((blocks, depth - step, feat), BF16),
            kept((blocks, 2 * step, feat // 2), BF16),
        ),
        in_specs=vmem(1) + hbm(1),
        out_specs=tuple(hbm(1) + vmem(1)),
        scratch_shapes=[
            pltpu.VMEM(one.shape, BF16),
            pltpu.VMEM((blocks, depth - step, feat), BF16),
            pltpu.SemaphoreType.DMA((2 * PIECES,)),
        ],
        compiler_params=pltpu.CompilerParams(vmem_limit_bytes=10 * MIB),
        cost_estimate=cost(0.01),
        name="join",
    )(near(two), far(one))


def added(one, two):
    return (one.astype(F32) + two.astype(F32)).astype(BF16)


def added_block(width, one, two):
    total = one.astype(F32) + two.astype(F32)
    parts = split_sum(total[0:8] + total[8:16]).astype(F32)
    lane = lax.broadcasted_iota(jnp.int32, total.shape, 1)
    return jnp.where(lane < width, total, parts).astype(BF16)


def halve_kernel(width, keep_ref, got_ref, side_ref, next_ref, send_ref):
    mine = lax.rem(lax.axis_index("ctx"), 2)

    @pl.loop(0, next_ref.shape[0])
    def one(b):
        for ref, which in ((send_ref, 1 - mine), (next_ref, mine)):
            at = 2 * b + which
            total = added_block(width, keep_ref[at], got_ref[at])
            ref[b] = jnp.concatenate([total, side_ref[at]], axis=0)


def halve(width, keep, got, side):
    blocks, depth, lanes = keep.shape
    depth += side.shape[1]
    return pl.pallas_call(
        functools.partial(halve_kernel, width),
        out_shape=(kept((blocks // 2, depth, lanes), BF16),) * 2,
        in_specs=vmem(3),
        out_specs=tuple(vmem(2)),
        compiler_params=pltpu.CompilerParams(vmem_limit_bytes=6 * MIB),
        cost_estimate=cost(1),
        name="halve",
    )(near(keep), near(got), near(side))


def pack_kernel(dq_ref, own_ref, *refs):
    others, out_ref = refs[:-1], refs[-1]
    size = dq_ref.shape[1]
    for h in range(HEADS):
        total = own_ref[h]
        for ref in others:
            total = total + ref[h].astype(F32)
        out_ref[h, 0:size, :] = dq_ref[h]
        out_ref[h, size : 3 * size, :] = total.astype(BF16)


def pack(dq, own, others):
    heads, size, tok = dq.shape
    return pl.pallas_call(
        pack_kernel,
        out_shape=kept((heads, 3 * size, tok), BF16),
        in_specs=vmem(2 + len(others)),
        out_specs=vmem(1)[0],
        compiler_params=pltpu.CompilerParams(vmem_limit_bytes=6 * MIB),
        cost_estimate=cost(0.5),
        name="pack",
    )(*map(near, (dq, own, *others)))


def merge_kernel(width, one_ref, two_ref, out_ref):
    for b in range(out_ref.shape[0]):
        out_ref[b, 0:16, :] = added_block(width, one_ref[b, 0:16, :], two_ref[b, 0:16, :])
        out_ref[b, 16:, :] = added(one_ref[b, 16:, :], two_ref[b, 16:, :])


def merge(width, one, two):
    return pl.pallas_call(
        functools.partial(merge_kernel, width),
        out_shape=kept(one.shape, BF16),
        in_specs=vmem(2),
        out_specs=vmem(1)[0],
        cost_estimate=cost(0.5),
        compiler_params=pltpu.CompilerParams(vmem_limit_bytes=3 * MIB),
        name="merge",
    )(near(one), near(two))


def head_grad_kernel(back_ref, x_in, small_ref, keep_ref, send_ref, x_ref, sems):
    copies = fetch(
        [x_in.at[h] for h in range(HEADS)], [x_ref.at[h] for h in range(HEADS)], sems
    )
    total = 0.0
    for h in range(HEADS):
        copies[h].wait()
        at = turned_by(lax.axis_index("dp"), RING[h], RING[HEADS - 1 - h])
        total = total + dot(back_ref[at], x_ref[h])
    turned = total.T
    feat, size = turned.shape
    blocks, step, lanes = keep_ref.shape
    small = small_ref[...]
    row = lax.broadcasted_iota(jnp.int32, (step, step), 0)
    empty = jnp.zeros((step, lanes - size - step), F32)
    for side in range(2):
        sums = jnp.concatenate([small[4 * side : 4 * side + 3], small[3:4], small[0:4] * 0.0], axis=0)
        sums = split_sum(sums).astype(F32)
        found = []
        for c in range(blocks):
            values = jnp.where(row % 8 == 3, sums[:, 0:step], sums[:, c * step : (c + 1) * step])
            start = side * feat // 2 + c * step
            block = [turned[start : start + step], values, empty]
            found.append(jnp.concatenate(block, axis=1).astype(BF16))
        for flip, ref in enumerate((keep_ref, send_ref)):

            @pl.when(lax.axis_index("dp") == (side + flip) % 2)
            def store():
                for c in range(blocks):
                    ref[c] = found[c]


def head_grads(blocks, back, x, small):
    feat = x.shape[2]
    step = feat // (2 * blocks)
    lanes = small.shape[1]
    return pl.pallas_call(
        head_grad_kernel,
        out_shape=(kept((blocks, step, lanes), BF16),) * 2,
        in_specs=vmem(1) + hbm(1) + vmem(1),
        out_specs=tuple(vmem(2)),
        scratch_shapes=[
            pltpu.VMEM(x.shape, BF16),
            pltpu.SemaphoreType.DMA((HEADS,)),
        ],
        compiler_params=pltpu.CompilerParams(vmem_limit_bytes=8 * MIB),
        cost_estimate=cost(1.5),
        name="head_grads",
    )(near(back), far(x), near(small))


def last_kernel(blocks, back_ref, gr_ref, *refs):
    gx_ref = refs[-1]
    feat = gr_ref.shape[1]
    size = feat // HEADS
    each = feat // blocks
    total = 0.0
    for part in range(3):
        turned = jnp.concatenate(
            [back_ref[h, part * size : (part + 1) * size, :] for h in range(HEADS)], axis=0
        )
        total = total + dot_t(turned.T, refs[part][...])
    for j in range(blocks):
        rows = rows_of(blocks, j, feat)
        gx_ref[:, rows] = (gr_ref[:, rows] + total[:, j * each : (j + 1) * each]).astype(
            gx_ref.dtype
        )


def last(blocks, back, gr, weights, kind):
    return pl.pallas_call(
        functools.partial(last_kernel, blocks),
        out_shape=(shaped if kind == F32 else kept)(gr.shape, kind),
        in_specs=vmem(2 + len(weights)),
        out_specs=vmem(1)[0],
        compiler_params=pltpu.CompilerParams(vmem_limit_bytes=6 * MIB),
        cost_estimate=cost(0.01),
        name="last",
    )(*map(near, (back, gr, *weights)))


def settle_kernel(
    pieces_ref, loss_ref, gq_ref, gk_ref, gv_ref, go_ref, g1_ref, g2_ref, g3_ref, inverse_ref
):
    step, feat = gq_ref.shape
    size = feat // HEADS
    width = 3 * size
    totals = jnp.sum(pieces_ref[...].astype(F32), axis=0)
    small = totals[0:8] + totals[8:16]
    sides = totals[step:]
    inverse = 1.0 / small[3:4, width + 1 : width + 2]
    inverse_ref[...] = jnp.broadcast_to(inverse, inverse_ref.shape)
    loss_ref[...] = small[3:4, width : width + 1] * inverse
    go_ref[...] = jnp.concatenate([sides[:step], sides[step:]], axis=1) * inverse
    for h in range(HEADS):
        block = pieces_ref[h, 0:step, :].astype(F32) * inverse
        for part, ref in enumerate((gq_ref, gk_ref, gv_ref)):
            ref[:, h * size : (h + 1) * size] = block[:, part * size : (part + 1) * size]
    for k, ref in enumerate((g1_ref, g2_ref, g3_ref)):
        ref[...] = small[k : k + 1, width : width + step] * inverse


def settle(pieces, feat):
    step = pieces.shape[1] // 3
    return pl.pallas_call(
        settle_kernel,
        out_shape=(
            shaped((1, 1), F32),
            shaped((step, feat), F32),
            shaped((step, feat), F32),
            shaped((step, feat), F32),
            shaped((step, feat), F32),
            shaped((1, step), F32),
            shaped((1, step), F32),
            shaped((1, step), F32),
            kept((8, 128), F32),
        ),
        in_specs=vmem(1),
        out_specs=tuple(vmem(9)),
        compiler_params=pltpu.CompilerParams(vmem_limit_bytes=4 * MIB),
        cost_estimate=pl.CostEstimate(
            flops=5500000000, bytes_accessed=1024, transcendentals=0
        ),
        name="settle",
    )(near(pieces))


def finish_kernel(inverse_ref, gx_in, pair_in, out_ref, gx_ref, gy_ref):
    inverse = inverse_ref[0:1, 0:1]
    tok = out_ref.shape[0]
    out_ref[...] = pair_in[0:tok]
    gx_ref[...] = gx_in[...].astype(F32) * inverse
    gy_ref[...] = pair_in[tok : 2 * tok].astype(F32) * inverse


def finish(inverse, gx, pair):
    tok, feat = gx.shape
    return pl.pallas_call(
        finish_kernel,
        out_shape=(
            shaped((tok, feat), BF16),
            shaped((tok, feat), F32),
            shaped((tok, feat), F32),
        ),
        in_specs=vmem(3),
        out_specs=tuple(vmem(3)),
        compiler_params=pltpu.CompilerParams(vmem_limit_bytes=6 * MIB),
        cost_estimate=cost(1),
        name="finish",
    )(near(inverse), gx, pair)


def spread_kernel(sums_in, inverse_ref, gu_ref, gd_ref, sums_ref, sem):
    (copy,) = fetch([sums_in], [sums_ref], sem)
    wide_step, feat = gd_ref.shape
    step = gu_ref.shape[0]
    copy.wait()
    main = sums_ref[0].astype(F32) * inverse_ref[0:1, 0:1]
    for j in range(gu_ref.shape[1] // feat):
        gu_ref[:, j * feat : (j + 1) * feat] = main[j * step : (j + 1) * step]
    gd_ref[...] = main[main.shape[0] - wide_step :]


def spread(sums, inverse, step, wide):
    feat = sums.shape[2]
    return pl.pallas_call(
        spread_kernel,
        out_shape=(shaped((step, wide), F32), shaped((wide * step // feat, feat), F32)),
        in_specs=hbm(1) + vmem(1),
        out_specs=tuple(vmem(2)),
        scratch_shapes=[pltpu.VMEM(sums.shape, BF16), pltpu.SemaphoreType.DMA((1,))],
        compiler_params=pltpu.CompilerParams(vmem_limit_bytes=4 * MIB),
        cost_estimate=cost(1),
        name="spread",
    )(far(sums), near(inverse))


def body(
    state_x,
    state_y,
    teacher,
    segment_ids,
    valid_mask,
    w_query,
    w_key,
    w_value,
    w_out,
    w_up,
    w_down,
    gain_attn,
    gain_ffn,
    gain_final,
):
    _, tok, feat = state_x.shape
    size = feat // HEADS
    ctx = lax.axis_size("ctx")
    sides = lax.axis_size("dp")
    ways = ctx // HEADS
    groups = [[h * ways + r for h in range(HEADS)] for r in range(ways)]
    side, place = lax.axis_index("dp"), lax.axis_index("ctx")
    wide = w_up.shape[1]
    cross = sides == 2 and ways == 2 and (feat // (sides * ctx)) % 16 == 0
    both = ("dp", "ctx")

    def both_ways(rings):
        return rings + [[ctx + place for place in reversed(ring)] for ring in rings]

    def moved(block):
        if not cross:
            return block
        route = []
        for s in range(2):
            for c in range(ctx):
                route.append((s * ctx + c, (c % 2) * ctx + c - c % 2 + s))
        return lax.ppermute(block, both, route)

    def shared(block):
        if sides == 2:
            return [block, swap(block, "dp", 1)]
        return [lax.all_gather(block, "dp", axis=0, tiled=True)]

    def exchange(block):
        return lax.all_to_all(block, "ctx", 0, 0, axis_index_groups=groups, tiled=True)

    def around(block, distance):
        if cross:
            return swap(block, "dp", 1)
        route = []
        for g in range(HEADS):
            for r in range(ways):
                route.append((g * ways + r, g * ways + (r + distance) % ways))
        return lax.ppermute(block, "ctx", route)

    x = moved(state_x[0])
    attn_weights = [shared(w) for w in (w_query, w_key, w_value)]
    segs = [segment_ids.reshape(ctx, tok)]
    if cross:
        segs.append(swap(segs[0], "dp", 1))
    mask = moved(valid_mask)
    pair = jnp.concatenate([state_y[0], teacher[0]], axis=0)
    qkv = project(x, attn_weights)
    plan = plan_of(segs, ways, ctx, tok)
    qkv = exchange(qkv)
    qkv, plan, mask, late_x, pair = lax.optimization_barrier((qkv, plan, mask, x, pair))
    kvs = [qkv] + [around(qkv, j) for j in range(1, ways)]
    o, of, lse = attend(plan, segs, kvs)
    gains = jnp.stack([gain_attn, gain_ffn, gain_final])
    if sides == 2:
        gains = shared(gains)
    else:
        gains = [lax.all_gather(gains, "dp", axis=1, tiled=True)]
    wo, wu, wd = shared(w_out), shared(w_up), shared(w_down)
    blocks = len(wu)
    o, pair = lax.optimization_barrier((o, moved(pair)))
    ot = exchange(o)
    ot, x_near, wo = lax.optimization_barrier((ot, *stage([x], wo)))
    ot = ot.reshape(feat, tok)
    pair, gr, do, small, *halves = middle(
        ot,
        mask,
        gains,
        x_near,
        pair,
        wo,
        wu,
        wd,
        [ffn_shape(ctx, feat, wide)] * (2 * cross),
    )
    do = do.reshape(HEADS, size, tok)
    if cross:
        rings = both_ways([[h * ways + r for h in RING] for r in range(ways)])
        gathered = lax.all_gather(late_x, both, axis=0, axis_index_groups=rings)
    do = exchange(do)
    if cross:
        sums, sides = join(halves[0], swap(halves[1], "dp", 1), feat // (2 * ctx))
        lse, sums = lax.optimization_barrier((lse, sums))
        kx, qx = prepare(segs, lse, kvs)
        do, kx, qx, sums, gathered = lax.optimization_barrier((do, kx, qx, sums, gathered))
        inner = both_ways([[4 * z + k for k in INNER] for z in range(4)])
        outer = both_ways([[4 * z + k for z in OUTER] for k in range(4)])
        sums = lax.psum_scatter(
            sums, both, scatter_dimension=0, axis_index_groups=inner, tiled=True
        )
    else:
        kx, qx = prepare(segs, lse, kvs)
    back_args = (plan, kx, qx, do, qkv)
    part, dx, *others = attend_back(
        *back_args, kvs[1:], ways, len(segs), tuple(range(1, ways)), of=of
    )
    others = [around(other, -(j + 1)) for j, other in enumerate(others)]
    dq, own = attend_back(
        *back_args, kvs[:1], ways, len(segs), (0,), part=part, dx=dx
    )
    sent = pack(dq, own, others)
    back = exchange(sent)
    back, *staged = lax.optimization_barrier((back, *stage([gr], *attn_weights)))
    if cross:
        mine, away = head_grads(ctx, sent, gathered, small)
        mine, away = halve(3 * size, mine, swap(away, "dp", 1), sides)
        pieces = merge(3 * size, mine, swap(away, "ctx", 1))
        pieces, sums, pair = lax.optimization_barrier((pieces, sums, pair))
        pair = moved(pair)
        sums = lax.psum_scatter(
            sums, both, scatter_dimension=0, axis_index_groups=outer, tiled=True
        )
        pieces = exchange(pieces)
        gx = moved(last(blocks, back, staged[0], staged[1:], BF16))
        loss, gq, gk, gv, go, g1, g2, g3, inverse = settle(pieces, feat)
        result, gx, gy = finish(inverse, gx, pair)
        gu, gd = spread(sums, inverse, gq.shape[0], wide)
        gains_out = [g.reshape(-1) for g in (g1, g2, g3)]
        loss = loss.reshape(())
    else:
        x1, h, df, dz, da = halves
        result, gy = pair[:tok], pair[tok:].astype(F32)
        total = lax.psum(small, both)
        inverse = 1.0 / total[3, 1]
        loss = total[3, 0] * inverse

        def scattered(block):
            block = block * inverse
            return lax.psum_scatter(block, both, scatter_dimension=0, tiled=True)

        gx = last(blocks, back, staged[0], staged[1:], F32)
        parts = [back[:, j * size : (j + 1) * size, :].reshape(feat, tok) for j in range(3)]
        gq, gk, gv = [scattered(dot_t(x.T, part)) for part in parts]
        go = scattered(dot(ot, da))
        gu = scattered(dot(x1.T, dz))
        gd = scattered(dot(h.T, df))
        gx, gy = gx * inverse, gy * inverse
        step = feat // (sides * ctx)
        number = side * ctx + place
        gains_out = [
            lax.dynamic_slice_in_dim(
                jnp.concatenate([total[k], total[k + 4]]) * inverse, number * step, step
            )
            for k in range(3)
        ]
    return (
        loss,
        result[None],
        gx[None],
        gy[None],
        gq,
        gk,
        gv,
        go,
        gu,
        gd,
        gains_out[0],
        gains_out[1],
        gains_out[2],
    )


def solution(mesh):
    tokens = P("dp", "ctx", None)
    rows = P("dp", None)
    spread = P(("dp", "ctx"), None)
    gain = P(("dp", "ctx"))
    return jax.shard_map(
        body,
        mesh=mesh,
        in_specs=(tokens,) * 3 + (rows, P("dp", "ctx")) + (rows,) * 6 + (P("dp"),) * 3,
        out_specs=(P(), tokens, tokens, tokens) + (spread,) * 6 + (gain,) * 3,
        check_vma=False,
    )
```

```python
import functools

import jax
import jax.numpy as jnp
from jax import lax
from jax.experimental import pallas as pl
from jax.experimental.pallas import tpu as pltpu
from jax.sharding import PartitionSpec as P

HEADS = 8
EPS = 1e-05
LANES = 32
DOCS = 24
UNROLL = 8
INNER = (0, 1, 3, 2)
OUTER = (0, 1, 3, 2)
RING = (0, 2, 4, 6, 7, 5, 3, 1)
GROUP = 8
GROUP_BACK = 4
FAR = -(2.0**100)
CORE = 0.7978845608028654
CUBE = 0.044715
MIB = 1024 * 1024

BF16 = jnp.bfloat16
F32 = jnp.float32


def dot(left, right):
    return jnp.dot(left, right, preferred_element_type=F32)


def dot_t(left, right):
    return lax.dot_general(left, right, (((1,), (1,)), ((), ())), preferred_element_type=F32)


def vmem(count):
    return [pl.BlockSpec(memory_space=pltpu.VMEM) for _ in range(count)]


def hbm(count):
    return [pl.BlockSpec(memory_space=pltpu.HBM) for _ in range(count)]


def smem():
    return pl.BlockSpec(memory_space=pltpu.SMEM)


def kept(shape, dtype):
    return pltpu.VMEM(shape, dtype)


def near(array):
    return pltpu.with_memory_space_constraint(array, pltpu.VMEM)


def apart(shape, dtype):
    return pltpu.HBM(shape, dtype)


def far(array):
    return pltpu.with_memory_space_constraint(array, pltpu.HBM)


def shaped(shape, dtype):
    return jax.ShapeDtypeStruct(shape, dtype)


def cost(us):
    return pl.CostEstimate(flops=1000, bytes_accessed=1024, transcendentals=0)


def swap(block, axis, bit):
    size = lax.axis_size(axis)
    return lax.ppermute(block, axis, [(i, i ^ bit) for i in range(size)])


def rank_of(ways, texts):
    if texts == 2:
        return lax.axis_index("dp")
    return lax.rem(lax.axis_index("ctx"), ways)


def rows_of(blocks, number, total):
    size = total // blocks
    if blocks == 1:
        return pl.ds(0, size)
    return pl.ds(pl.multiple_of((lax.axis_index("dp") + number) % 2 * size, size), size)


def turned_by(side, first, second):
    return jnp.where(side == 0, first, second)


def fetch(sources, targets, sems, first=0):
    copies = [
        pltpu.make_async_copy(source, target, sems.at[first + k])
        for k, (source, target) in enumerate(zip(sources, targets))
    ]
    for copy in copies:
        copy.start()
    return copies


def stage_kernel(layout, *refs):
    outs, sems = refs[len(layout) : -1], refs[-1]
    targets = [outs[k].at[pl.ds(start, size), :] for k, start, size in layout]
    for copy in fetch(refs[: len(layout)], targets, sems):
        copy.wait()


def stage(*groups):
    layout, shapes = [], []
    for k, group in enumerate(groups):
        start = 0
        for array in group:
            layout.append((k, start, array.shape[0]))
            start += array.shape[0]
        shapes.append(kept((start, group[0].shape[1]), group[0].dtype))
    flat = [far(array) for group in groups for array in group]
    return pl.pallas_call(
        functools.partial(stage_kernel, tuple(layout)),
        out_shape=tuple(shapes),
        in_specs=hbm(len(flat)),
        out_specs=tuple(vmem(len(groups))),
        scratch_shapes=[pltpu.SemaphoreType.DMA((len(flat),))],
        compiler_params=pltpu.CompilerParams(vmem_limit_bytes=4 * MIB),
        cost_estimate=cost(0.01),
        name="stage",
    )(*flat)


def project_kernel(blocks, x_ref, *refs):
    out_ref = refs[-1]
    feat = x_ref.shape[1]
    size = feat // HEADS
    x = jnp.concatenate([x_ref[:, rows_of(blocks, j, feat)] for j in range(blocks)], axis=1)
    for part, scale in ((0, size**-0.5), (1, 1.0), (2, 1.0)):
        weight = [refs[j * 3 + part][...] for j in range(blocks)]
        turned = (dot(x, jnp.concatenate(weight, axis=0)) * scale).astype(BF16).T
        for h in range(HEADS):
            out_ref[h, part * size : (part + 1) * size, :] = turned[h * size : (h + 1) * size, :]


def project(x, weights):
    tok, feat = x.shape
    flat = stage(*[[weight[0]] for weight in weights])
    flat += tuple(block for weight in weights for block in weight[1:])
    return pl.pallas_call(
        functools.partial(project_kernel, len(weights[0])),
        out_shape=kept((HEADS, 3 * feat // HEADS, tok), BF16),
        in_specs=vmem(1 + len(flat)),
        out_specs=vmem(1)[0],
        compiler_params=pltpu.CompilerParams(vmem_limit_bytes=6 * MIB),
        cost_estimate=cost(1.4),
        name="project",
    )(near(x), *map(near, flat))


def mask_rows(row, hit, miss, extra):
    number = lax.broadcasted_iota(jnp.int32, (LANES, row.shape[1]), 0)
    base = jnp.where(number == row, hit, miss)
    base = jnp.where(number < DOCS, base, 0.0)
    for k, value in enumerate(extra):
        base = jnp.where(number == DOCS + k, value, base)
    return base.astype(BF16)


def parts_of(value, count):
    found = []
    for _ in range(count):
        part = value.astype(BF16).astype(F32)
        found.append(part)
        value = value - part
    return found


def query_rows(q, row, extra):
    return jnp.concatenate([q, mask_rows(row, 0.0, FAR, extra)], axis=0).T


def key_rows(k, row):
    return jnp.concatenate([k, mask_rows(row, 1.0, 0.0, (1.0, 1.0, 1.0))], axis=0)


def list_size(count):
    return HEADS * count + 2 * GROUP


def plan_kernel(ways, count, tok, *refs):
    out_ref = refs[-1]
    rank = rank_of(ways, len(refs) - 1)
    flip = (lax.axis_index("dp") + lax.axis_index("ctx")) % 2
    length = list_size(count)

    def number(at):
        if len(refs) == 2:
            return refs[0][at]
        return jnp.where(flip == 0, refs[0][at], refs[1][at])

    firsts = [number(c * tok) for c in range(count)]
    lasts = [number(c * tok + tok - 1) for c in range(count)]

    def one(i, found):
        chunk = i * ways + rank
        first = number(chunk * tok)
        last = number(chunk * tok + tok - 1)
        low = sum((value < first).astype(jnp.int32) for value in lasts)
        high = sum((value <= last).astype(jnp.int32) for value in firsts)

        def other(c, found):
            own = (lax.rem(c, ways) == rank).astype(jnp.int32)
            every, mine, rest = found
            out_ref[every] = i
            out_ref[length + every] = c
            at = jnp.where(own == 1, 2 * length + mine, 4 * length + rest)
            out_ref[at] = i
            out_ref[at + length] = c
            return every + 1, mine + own, rest + 1 - own

        return lax.fori_loop(low, high, other, found)

    found = lax.fori_loop(0, HEADS, one, (jnp.int32(0),) * 3)
    for k, ended in enumerate(found):
        for g in range(GROUP):
            out_ref[2 * k * length + ended + g] = HEADS
            out_ref[(2 * k + 1) * length + ended + g] = 0
        size = GROUP if k == 0 else GROUP_BACK
        out_ref[6 * length + k] = (ended + size - 1) // size


def plan_of(segs, ways, count, tok):
    size = 6 * list_size(count) + 8
    return pl.pallas_call(
        functools.partial(plan_kernel, ways, count, tok),
        out_shape=shaped((size,), jnp.int32),
        in_specs=[smem()] * len(segs),
        out_specs=smem(),
        cost_estimate=cost(1),
        compiler_params=pltpu.CompilerParams(vmem_limit_bytes=1 * MIB),
        name="plan",
    )(*[seg.reshape(-1) for seg in segs])


def chosen(seg_refs):
    if len(seg_refs) == 1:
        return seg_refs[0][...]
    flip = (lax.axis_index("dp") + lax.axis_index("ctx")) % 2
    return jnp.where(flip == 0, seg_refs[0][...], seg_refs[1][...])


def tiles_of(plan_ref, kind, length, g):
    found = []
    size = GROUP if kind == 0 else GROUP_BACK
    for k in range(size):
        at = 2 * kind * length + g * size + k
        found.append((plan_ref[at], plan_ref[at + length]))
    return found


def chunk_of(h, slot, ways, rank):
    return h * ways + lax.rem(rank - slot + ways, ways)


def forward_kernel(ways, texts, plan_ref, *refs):
    seg_refs, refs = refs[:texts], refs[texts:]
    kv_refs = refs[:ways]
    q_ref = kv_refs[0]
    o_ref, of_out, lse_ref, kx, vx, qx, acc, seg_ref, of_ref, sem = refs[ways:]
    seg_ref[...] = chosen(seg_refs)
    count, tok = seg_ref.shape
    size = q_ref.shape[1] // 3
    rank = rank_of(ways, texts)
    length = list_size(count)
    ones = (lax.broadcasted_iota(jnp.int32, (16, tok), 0) == 0).astype(F32).astype(BF16)
    for slot in range(ways):

        @pl.loop(0, HEADS, unroll=UNROLL)
        def fill(h):
            chunk = chunk_of(h, slot, ways, rank)
            keys = kv_refs[slot][h, size : 2 * size, :]
            kx[chunk] = key_rows(keys, seg_ref[pl.ds(chunk, 1), :])
            vx[chunk] = jnp.concatenate([kv_refs[slot][h, 2 * size : 3 * size, :], ones], axis=0)

    @pl.loop(0, HEADS, unroll=UNROLL)
    def fill_query(i):
        qx[i] = query_rows(q_ref[i, 0:size, :], seg_ref[pl.ds(i * ways + rank, 1), :], ())
        acc[i] = jnp.zeros_like(acc[i])

    qx[HEADS] = query_rows(jnp.zeros((size, tok), BF16), jnp.full((1, tok), -1, jnp.int32), ())
    acc[HEADS] = jnp.zeros_like(acc[0])

    @pl.loop(0, plan_ref[6 * length])
    def group(g):
        tiles = tiles_of(plan_ref, 0, length, g)
        weights = [jnp.exp(dot(qx[i], kx[c])).astype(BF16) for i, c in tiles]
        mixed = [dot_t(vx[c], w) for (i, c), w in zip(tiles, weights)]
        for (i, c), part in zip(tiles, mixed):
            acc[i] += part

    leaving = []
    smallest = jnp.full((1, tok), 1.0, F32)
    largest = jnp.full((1, tok), 1.0, F32)
    for i in range(HEADS):
        total = acc[i, size : size + 1, :]
        smallest = jnp.minimum(smallest, total)
        largest = jnp.maximum(largest, total)
        out = acc[i, 0:size, :] / total
        of_ref[i] = out
        leaving += fetch([of_ref.at[i]], [of_out.at[i]], sem, i)
        o_ref[i] = out.astype(BF16)
        lse_ref[i : i + 1, :] = jnp.log(total)
    for copy in leaving:
        copy.wait()
    good = (jnp.min(smallest) > 2.0**-90) & (jnp.max(largest) < 2.0**90)

    @pl.when(jnp.logical_not(good))
    def any_scores():
        @pl.loop(0, HEADS)
        def one(i):
            query = qx[i]

            def step(c, carry):
                top, total, mixed = carry
                s = dot(query, kx[c])
                new = jnp.maximum(top, jnp.max(s, axis=1, keepdims=True))
                fade = jnp.exp(top - new)
                w = jnp.exp(s - new)
                total = total * fade + jnp.sum(w, axis=1, keepdims=True)
                mixed = mixed * fade + dot_t(w.astype(BF16), vx[c])
                return new, total, mixed

            top, total, mixed = lax.fori_loop(
                0,
                count,
                step,
                (
                    jnp.full((tok, 1), -3e38, F32),
                    jnp.zeros((tok, 1), F32),
                    jnp.zeros((tok, size + 16), F32),
                ),
            )
            out = (mixed / total).T[0:size, :]
            of_ref[i] = out
            o_ref[i] = out.astype(BF16)
            lse = jnp.broadcast_to(top + jnp.log(total), (tok, 128)).T
            lse_ref[pl.ds(i, 1), :] = lse[0:1, :]

        fetch([of_ref], [of_out], sem)[0].wait()


def attend(plan, segs, kvs):
    ways = len(kvs)
    _, size, tok = kvs[0].shape
    size = size // 3
    count = segs[0].shape[0]
    depth = size + LANES
    return pl.pallas_call(
        functools.partial(forward_kernel, ways, len(segs)),
        out_shape=(
            kept((HEADS, size, tok), BF16),
            apart((HEADS, size, tok), F32),
            kept((HEADS, tok), F32),
        ),
        in_specs=[smem()] + vmem(len(segs) + ways),
        out_specs=(vmem(1)[0], hbm(1)[0], vmem(1)[0]),
        scratch_shapes=[
            pltpu.VMEM((count, depth, tok), BF16),
            pltpu.VMEM((count, size + 16, tok), BF16),
            pltpu.VMEM((HEADS + 1, tok, depth), BF16),
            pltpu.VMEM((HEADS + 1, size + 16, tok), F32),
            pltpu.VMEM(segs[0].shape, jnp.int32),
            pltpu.VMEM((HEADS, size, tok), F32),
            pltpu.SemaphoreType.DMA((HEADS,)),
        ],
        compiler_params=pltpu.CompilerParams(vmem_limit_bytes=12 * MIB),
        cost_estimate=cost(7),
        name="attend",
    )(far(plan), *segs, *map(near, kvs))


def prepare_kernel(ways, texts, lse_ref, *refs):
    seg_refs, refs = refs[:texts], refs[texts:]
    kv_ins = refs[:ways]
    kx, qx, seg_ref, k_ref, q_ref, sems = refs[ways:]
    size = q_ref.shape[1]
    there = (slice(None), pl.ds(size, size), slice(None))
    copies = fetch([kv.at[there] for kv in kv_ins], [k_ref.at[k] for k in range(ways)], sems)
    there = (slice(None), pl.ds(0, size), slice(None))
    copies += fetch([kv_ins[0].at[there]], [q_ref], sems, ways)
    seg_ref[...] = chosen(seg_refs)
    tok = seg_ref.shape[1]
    rank = rank_of(ways, texts)
    for slot in range(ways):
        copies[slot].wait()

        @pl.loop(0, HEADS, unroll=UNROLL)
        def fill(h):
            chunk = chunk_of(h, slot, ways, rank)
            kx[chunk] = key_rows(k_ref[slot, h], seg_ref[pl.ds(chunk, 1), :])

    copies[ways].wait()

    @pl.loop(0, HEADS, unroll=UNROLL)
    def fill_query(i):
        lse = parts_of(-lse_ref[pl.ds(i, 1), :], 3)
        qx[i] = query_rows(q_ref[i], seg_ref[pl.ds(i * ways + rank, 1), :], lse)

    qx[HEADS] = query_rows(jnp.zeros((size, tok), BF16), jnp.full((1, tok), -1, jnp.int32), ())


def prepare(segs, lse, kvs):
    ways = len(kvs)
    count, tok = segs[0].shape
    size = kvs[0].shape[1] // 3
    depth = size + LANES
    return pl.pallas_call(
        functools.partial(prepare_kernel, ways, len(segs)),
        out_shape=(kept((count, depth, tok), BF16), kept((HEADS + 1, tok, depth), BF16)),
        in_specs=vmem(1 + len(segs)) + hbm(ways),
        out_specs=tuple(vmem(2)),
        scratch_shapes=[
            pltpu.VMEM(segs[0].shape, jnp.int32),
            pltpu.VMEM((ways, HEADS, size, tok), BF16),
            pltpu.VMEM((HEADS, size, tok), BF16),
            pltpu.SemaphoreType.DMA((ways + 1,)),
        ],
        compiler_params=pltpu.CompilerParams(vmem_limit_bytes=12 * MIB),
        cost_estimate=cost(2),
        name="prepare",
    )(near(lse), *segs, *map(far, kvs))


def backward_kernel(ways, slots, final, texts, plan_ref, kx, qx, do_ref, *refs):
    many = len(slots)
    q_in, kv_ins, refs = refs[0], refs[1 : 1 + many], refs[1 + many :]
    if final:
        part_ref, dx, dq_ref, *dkv_refs = refs[: 3 + many]
        refs = refs[3 + many :]
    else:
        of_in, dq_ref, dx, *dkv_refs = refs[: 3 + many]
        refs = refs[3 + many :]
    vx, dk, dv, dq, q_ref, v_ref, of_ref, sems = refs
    count, _, tok = kx.shape
    size = do_ref.shape[1]
    copies = []
    if not final:
        copies += fetch([of_in], [of_ref], sems, 1 + many)
    for k, kv in enumerate(kv_ins):
        there = (slice(None), pl.ds(2 * size, size), slice(None))
        copies += fetch([kv.at[there]], [v_ref.at[k]], sems, 1 + k)
    there = (slice(None), pl.ds(0, size), slice(None))
    copies += fetch([q_in.at[there]], [q_ref], sems)
    rank = rank_of(ways, texts)
    ones = (lax.broadcasted_iota(jnp.int32, (16, tok), 0) < 2).astype(F32).astype(BF16)

    def open_query(i):
        do = do_ref[i].astype(F32)
        delta = parts_of(-jnp.sum(do * of_ref[i], axis=0, keepdims=True), 3)
        number = lax.broadcasted_iota(jnp.int32, (16, tok), 0)
        tail = jnp.where(number == 0, delta[0], jnp.where(number == 1, delta[1], 0.0))
        dx[i] = jnp.concatenate([do_ref[i], tail.astype(BF16)], axis=0).T

    if final:
        dq[0:HEADS] = part_ref[...]
    else:
        copies.pop(0).wait()
        pl.loop(0, HEADS, unroll=UNROLL)(open_query)
        dx[HEADS] = jnp.zeros_like(dx[0])
        dq[0:HEADS] = jnp.zeros_like(dq[0:HEADS])
    dq[HEADS] = jnp.zeros_like(dq[0])
    for copy in copies:
        copy.wait()
    for k, slot in enumerate(slots):

        @pl.loop(0, HEADS, unroll=UNROLL)
        def fill(h):
            chunk = chunk_of(h, slot, ways, rank)
            vx[chunk] = jnp.concatenate([v_ref[k, h], ones], axis=0)
            dk[chunk] = jnp.zeros_like(dk[chunk])
            dv[chunk] = jnp.zeros_like(dv[chunk])

    kind = 1 if slots == (0,) else 2
    length = list_size(count)

    @pl.loop(0, plan_ref[6 * length + kind])
    def group(g):
        tiles = tiles_of(plan_ref, kind, length, g)
        weights = [jnp.exp(dot(qx[i], kx[c])) for i, c in tiles]
        pulls = [dot(dx[i], vx[c]) for i, c in tiles]
        scores = [(w * p).astype(BF16) for w, p in zip(weights, pulls)]
        for (i, c), w, ds in zip(tiles, weights, scores):
            j = jnp.minimum(i, HEADS - 1)
            dv[c] += dot(do_ref[j], w.astype(BF16))
            dk[c] += dot(q_ref[j], ds)
            dq[i] += dot_t(kx[c, 0:size, :], ds)

    for slot, out in zip(slots, dkv_refs):

        @pl.loop(0, HEADS, unroll=UNROLL)
        def drain(h):
            chunk = chunk_of(h, slot, ways, rank)
            out[h, 0:size, :] = dk[chunk].astype(out.dtype)
            out[h, size : 2 * size, :] = dv[chunk].astype(out.dtype)

    @pl.loop(0, HEADS, unroll=UNROLL)
    def drain_query(i):
        if final:
            dq_ref[i] = (dq[i] * size**-0.5).astype(BF16)
        else:
            dq_ref[i] = dq[i]


def attend_back(plan, kx, qx, do, q, kvs, ways, texts, slots, of=None, part=None, dx=None):
    many = len(slots)
    final = part is not None
    _, size, tok = do.shape
    count, depth, _ = kx.shape
    queries = kept((HEADS, size, tok), BF16 if final else F32)
    grads = (kept((HEADS, 2 * size, tok), F32 if slots == (0,) else BF16),) * many
    pulls = kept((HEADS + 1, tok, size + 16), BF16)
    return pl.pallas_call(
        functools.partial(backward_kernel, ways, slots, final, texts),
        out_shape=(queries,) + ((pulls,) * (not final)) + grads,
        in_specs=[smem()]
        + vmem(3)
        + hbm(1 + many)
        + (vmem(2) if final else hbm(1)),
        out_specs=tuple(vmem(1 + many + (not final))),
        scratch_shapes=[
            pltpu.VMEM((count, size + 16, tok), BF16),
            pltpu.VMEM((count, size, tok), F32),
            pltpu.VMEM((count, size, tok), F32),
            pltpu.VMEM((HEADS + 1, size, tok), F32),
            pltpu.VMEM((HEADS, size, tok), BF16),
            pltpu.VMEM((many, HEADS, size, tok), BF16),
            pltpu.VMEM((HEADS, size, tok), F32),
            pltpu.SemaphoreType.DMA((2 + many,)),
        ],
        compiler_params=pltpu.CompilerParams(vmem_limit_bytes=16 * MIB),
        cost_estimate=cost(7.5),
        name="attend_back",
    )(
        far(plan),
        *map(near, (kx, qx, do)),
        far(q),
        *map(far, kvs),
        *((near(part), near(dx)) if final else (far(of),)),
    )


def normed(rows):
    centred = rows - jnp.mean(rows, axis=-1, keepdims=True)
    spread = jnp.mean(centred * centred, axis=-1, keepdims=True)
    inverse = lax.rsqrt(spread + EPS)
    return centred * inverse, inverse


def norm_back(n, inverse, gain, up):
    scaled = up * gain
    mean_one = jnp.mean(scaled, axis=-1, keepdims=True)
    mean_two = jnp.mean(scaled * n, axis=-1, keepdims=True)
    grad = inverse * (scaled - mean_one - n * mean_two)
    return grad, jnp.sum(up * n, axis=0, keepdims=True)


def middle_kernel(blocks, tile, *refs):
    ot_ref, mask_ref = refs[:2]
    gains_refs = refs[2 : 2 + blocks]
    refs = refs[2 + blocks :]
    x_ref, wo_ref, both_in = refs[:3]
    wu_in, wd_in = [refs[3 + k * blocks : 3 + (k + 1) * blocks] for k in range(2)]
    (
        both_out,
        gr_out,
        dot_ref,
        small_ref,
        *grad_outs,
        x1_ref,
        h_ref,
        df_ref,
        dz_ref,
        da_ref,
        slope,
        acc,
        gr_ref,
        y_ref,
        t_ref,
        wu_ref,
        wd_ref,
        xt,
        sum_refs,
        out_ref,
        gy_ref,
        sems,
        tile_sems,
        sum_sems,
    ) = refs[3 + 2 * blocks :]
    part_rows = wo_ref.shape[0] // blocks
    wide = h_ref.shape[1]
    each = wide // blocks

    def columns(start):
        if blocks == 2:
            start = (start + lax.axis_index("dp") * each) % wide
        return pl.ds(pl.multiple_of(start, tile), tile)

    tiles = []
    for k, start in enumerate(range(0, wide, tile)):
        cols = columns(start)
        tiles.append(
            fetch(
                [*[ref.at[:, cols] for ref in wu_in], wd_in[start // each].at[pl.ds(start % each, tile), :]],
                [
                    *[wu_ref.at[pl.ds(j * part_rows, part_rows), cols] for j in range(blocks)],
                    wd_ref.at[pl.ds(start, tile), :],
                ],
                tile_sems,
                k * (blocks + 1),
            )
        )
    tok = x_ref.shape[0]
    late = fetch(
        [both_in.at[pl.ds(0, tok), :], both_in.at[pl.ds(tok, tok), :]],
        [y_ref, t_ref],
        sems,
        blocks + 1,
    )
    rows, feat = x_ref.shape
    halves = [rows_of(blocks, j, feat) for j in range(blocks)]

    def ordered(values):
        if blocks == 1:
            return values
        low, high = values[:, : feat // 2], values[:, feat // 2 :]
        turned = jnp.concatenate([high, low], axis=1)
        return jnp.where(lax.axis_index("dp") == 0, values, turned)

    gains = gains_refs[0][...].astype(F32)
    if blocks == 2:
        other = gains_refs[1][...].astype(F32)
        gains = jnp.where(
            lax.axis_index("dp") == 0,
            jnp.concatenate([gains, other], axis=1),
            jnp.concatenate([other, gains], axis=1),
        )
    g1, g2, g3 = gains[0:1], gains[1:2], gains[2:3]
    branch = dot(
        jnp.concatenate([ot_ref[rows_j, :] for rows_j in halves], axis=0).T,
        wo_ref[...],
    )
    n1, r1 = normed(x_ref[...].astype(F32) + branch)
    x1 = n1 * g1
    x1_ref[...] = ordered(x1).astype(BF16)

    def weight_up(start):
        return wu_ref[:, columns(start)]

    for start in range(0, wide, tile):
        cols = slice(start, start + tile)
        for copy in tiles[start // tile]:
            copy.wait()
        z = dot(x1_ref[...], weight_up(start))
        z2 = z * z
        th = jnp.tanh(z * (CORE + (CORE * CUBE) * z2))
        half = 0.5 + 0.5 * th
        h = (z * half).astype(BF16)
        slope[:, cols] = half + z * (1.0 - th * th) * (0.5 * CORE + (1.5 * CORE * CUBE) * z2)
        h_ref[:, cols] = h
        part = dot(h, wd_ref[start : start + tile, :])
        if start:
            acc[...] += part
        else:
            acc[...] = part

    ffn = acc[...]
    n2, r2 = normed(x1 + ffn)
    for copy in late:
        copy.wait()
    n3, r3 = normed(y_ref[...].astype(F32) + branch + ffn)
    result = n2 * g2 + n3 * g3
    out_ref[...] = result.astype(BF16)
    mask_row = mask_ref[...].astype(F32)
    mask = jnp.broadcast_to(mask_row, (8, rows)).T[:, 0:1]
    differ = result - t_ref[...].astype(F32)
    error = jnp.sum(mask * differ * differ)
    valid = jnp.sum(mask_row)
    upstream = 2.0 * mask * differ
    gy, dg3 = norm_back(n3, r3, g3, upstream)
    du, dg2 = norm_back(n2, r2, g2, upstream)
    gy_ref[...] = gy.astype(gy_ref.dtype)
    df_ref[...] = (du + gy).astype(BF16)
    going = [] if len(grad_outs) == 2 else None
    if going is not None:
        count, depth, _ = grad_outs[0].shape
        step = feat // (2 * count)
        wide_step = wide // (2 * count)
        parts = wide // feat

        def put(flip, first, base, size, values):
            side = (lax.axis_index("dp") + flip) % 2
            for k in range(values.shape[0] // size):
                c = first + k
                at = INNER.index(c % 4) * 4 + OUTER.index(c // 4)
                at = turned_by(side, at, 15 - at)
                sum_refs[flip, at, pl.ds(base, size), :] = values[
                    k * size : (k + 1) * size
                ].astype(BF16)

        def send(flip, base, size):
            span = pl.ds(base, size)
            going.extend(
                fetch(
                    [sum_refs.at[flip, :, span, :]],
                    [grad_outs[flip].at[:, span, :]],
                    sum_sems,
                    len(going),
                )
            )

        xt[...] = x1_ref[...].T
        for flip in (1, 0):
            for start in range(0, wide // 2, tile):
                cols = slice(flip * (wide // 2) + start, flip * (wide // 2) + start + tile)
                g = dot(h_ref[:, cols].T, df_ref[...])
                put(flip, start // wide_step, parts * step, wide_step, g)
            send(flip, parts * step, wide_step)
    for start in range(0, wide, tile):
        cols = slice(start, start + tile)
        dz = (dot_t(df_ref[...], wd_ref[start : start + tile, :]) * slope[:, cols]).astype(BF16)
        dz_ref[:, cols] = dz

    back = 0.0
    for k in range(blocks):
        start = k * each
        if blocks == 2:
            start = (start + lax.axis_index("dp") * each) % wide
        cols = pl.ds(pl.multiple_of(start, each), each)
        back = back + dot_t(dz_ref[:, k * each : (k + 1) * each], wu_ref[:, cols])
    if going is not None:
        for start in range(0, wide, tile):
            g = dot(xt[...], dz_ref[:, start : start + tile])
            base = (start + lax.axis_index("dp") * each) % wide // feat * step
            for flip in (1, 0):
                half_g = g[flip * (feat // 2) : (flip + 1) * (feat // 2)]
                put(flip, 0, pl.multiple_of(base, step), step, half_g)
                send(flip, pl.multiple_of(base, step), step)

    gr, dg1 = norm_back(n1, r1, g1, du + ordered(back))
    gr_ref[...] = gr
    leaving = fetch(
        [gr_ref, out_ref, gy_ref],
        [gr_out, both_out.at[pl.ds(0, tok), :], both_out.at[pl.ds(tok, tok), :]],
        sems,
    )
    da = (gr + gy).astype(BF16)
    da_ref[...] = da
    turned = dot_t(wo_ref[...], da).astype(BF16)
    for j in range(blocks):
        size = feat // blocks
        dot_ref[halves[j], :] = turned[j * size : (j + 1) * size]
    lane = lax.broadcasted_iota(jnp.int32, (1, feat), 1)
    scalars = jnp.where(lane == 0, error, jnp.where(lane == 1, valid, 0.0))
    sums = jnp.concatenate([dg1, dg2, dg3, scalars], axis=0)
    small_ref[...] = jnp.concatenate([sums[:, : feat // 2], sums[:, feat // 2 :]], axis=0)
    if going is None:
        for out, ref in zip(grad_outs, (x1_ref, h_ref, df_ref, dz_ref, da_ref)):
            out[...] = ref[...]
    else:
        for flip in (1, 0):
            side = (lax.axis_index("dp") + flip) % 2
            part = pl.ds(pl.multiple_of(side * (feat // 2), feat // 2), feat // 2)
            put(flip, 0, parts * step + wide_step, step, dot(ot_ref[part, :], da))
            send(flip, parts * step + wide_step, step)
    for copy in leaving + (going or []):
        copy.wait()


def middle(ot, mask, gains, x, pair, wo, wu, wd, scattered):
    tok, feat = x.shape
    wide = wu[0].shape[1]
    blocks = len(gains)
    tile = min(512, wide // blocks)
    return pl.pallas_call(
        functools.partial(middle_kernel, blocks, tile),
        out_shape=(
            apart((2 * tok, feat), BF16),
            apart((tok, feat), F32),
            kept((feat, tok), BF16),
            kept((8, feat // 2), F32),
        )
        + (
            tuple(apart(shape, BF16) for shape in scattered)
            or tuple(shaped((tok, size), BF16) for size in (feat, wide, feat, wide, feat))
        ),
        in_specs=vmem(4 + blocks) + hbm(1 + 2 * blocks),
        out_specs=tuple(hbm(2) + vmem(2) + (hbm(len(scattered)) or vmem(5))),
        scratch_shapes=[
            pltpu.VMEM((tok, feat), BF16),
            pltpu.VMEM((tok, wide), BF16),
            pltpu.VMEM((tok, feat), BF16),
            pltpu.VMEM((tok, wide), BF16),
            pltpu.VMEM((tok, feat), BF16),
            pltpu.VMEM((tok, wide), F32),
            pltpu.VMEM((tok, feat), F32),
            pltpu.VMEM((tok, feat), F32),
            pltpu.VMEM((tok, feat), BF16),
            pltpu.VMEM((tok, feat), BF16),
            pltpu.VMEM((feat, wide), BF16),
            pltpu.VMEM((wide, feat), BF16),
            pltpu.VMEM((feat, tok), BF16),
            pltpu.VMEM((2, *(scattered[0] if scattered else (8, 16, 128))), BF16),
            pltpu.VMEM((tok, feat), BF16),
            pltpu.VMEM((tok, feat), BF16),
            pltpu.SemaphoreType.DMA((blocks + 3,)),
            pltpu.SemaphoreType.DMA((wide // tile * (blocks + 1),)),
            pltpu.SemaphoreType.DMA((2 * PIECES,)),
        ],
        compiler_params=pltpu.CompilerParams(vmem_limit_bytes=36 * MIB),
        cost_estimate=cost(8),
        name="middle",
    )(near(ot), mask, *gains, near(x), near(wo), *map(far, (pair, *wu, *wd)))


def split_sum(values):
    high = values.astype(BF16)
    low = (values - high.astype(F32)).astype(BF16)
    return jnp.concatenate([high.astype(F32), low.astype(F32)], axis=0).astype(BF16)


PIECES = 8


def ffn_shape(blocks, feat, wide):
    step = feat // (2 * blocks)
    return (blocks, (wide // feat) * step + wide // (2 * blocks) + step, feat)


def join_kernel(two_ref, one_in, out, side_ref, one_ref, ref, sems):
    blocks, depth, feat = two_ref.shape
    main = ref.shape[1]
    step = depth - main
    spans = [pl.ds(k * blocks // PIECES, blocks // PIECES) for k in range(PIECES)]
    ones = fetch([one_in.at[k] for k in spans], [one_ref.at[k] for k in spans], sems)
    going = []
    for k, (span, one) in enumerate(zip(spans, ones)):
        one.wait()
        for b in range(k * blocks // PIECES, (k + 1) * blocks // PIECES):
            total = added(one_ref[b], two_ref[b])
            ref[b] = total[:main]
            places = [OUTER[at % 4] * 4 + INNER[at // 4] for at in (b, 15 - b)]
            c = turned_by(lax.axis_index("dp"), *places)
            side_ref[c, 0:step, :] = total[main:, : feat // 2]
            side_ref[c, step : 2 * step, :] = total[main:, feat // 2 :]
        going += fetch([ref.at[span]], [out.at[span]], sems, PIECES + k)
    for copy in going:
        copy.wait()


def join(one, two, step):
    blocks, depth, feat = one.shape
    return pl.pallas_call(
        join_kernel,
        out_shape=(
            apart((blocks, depth - step, feat), BF16),
            kept((blocks, 2 * step, feat // 2), BF16),
        ),
        in_specs=vmem(1) + hbm(1),
        out_specs=tuple(hbm(1) + vmem(1)),
        scratch_shapes=[
            pltpu.VMEM(one.shape, BF16),
            pltpu.VMEM((blocks, depth - step, feat), BF16),
            pltpu.SemaphoreType.DMA((2 * PIECES,)),
        ],
        compiler_params=pltpu.CompilerParams(vmem_limit_bytes=10 * MIB),
        cost_estimate=cost(0.01),
        name="join",
    )(near(two), far(one))


def added(one, two):
    return (one.astype(F32) + two.astype(F32)).astype(BF16)


def added_block(width, one, two):
    total = one.astype(F32) + two.astype(F32)
    parts = split_sum(total[0:8] + total[8:16]).astype(F32)
    lane = lax.broadcasted_iota(jnp.int32, total.shape, 1)
    return jnp.where(lane < width, total, parts).astype(BF16)


def halve_kernel(width, keep_ref, got_ref, side_ref, next_ref, send_ref):
    mine = lax.rem(lax.axis_index("ctx"), 2)

    @pl.loop(0, next_ref.shape[0])
    def one(b):
        for ref, which in ((send_ref, 1 - mine), (next_ref, mine)):
            at = 2 * b + which
            total = added_block(width, keep_ref[at], got_ref[at])
            ref[b] = jnp.concatenate([total, side_ref[at]], axis=0)


def halve(width, keep, got, side):
    blocks, depth, lanes = keep.shape
    depth += side.shape[1]
    return pl.pallas_call(
        functools.partial(halve_kernel, width),
        out_shape=(kept((blocks // 2, depth, lanes), BF16),) * 2,
        in_specs=vmem(3),
        out_specs=tuple(vmem(2)),
        compiler_params=pltpu.CompilerParams(vmem_limit_bytes=6 * MIB),
        cost_estimate=cost(1),
        name="halve",
    )(near(keep), near(got), near(side))


def pack_kernel(dq_ref, own_ref, *refs):
    others, out_ref = refs[:-1], refs[-1]
    size = dq_ref.shape[1]
    for h in range(HEADS):
        total = own_ref[h]
        for ref in others:
            total = total + ref[h].astype(F32)
        out_ref[h, 0:size, :] = dq_ref[h]
        out_ref[h, size : 3 * size, :] = total.astype(BF16)


def pack(dq, own, others):
    heads, size, tok = dq.shape
    return pl.pallas_call(
        pack_kernel,
        out_shape=kept((heads, 3 * size, tok), BF16),
        in_specs=vmem(2 + len(others)),
        out_specs=vmem(1)[0],
        compiler_params=pltpu.CompilerParams(vmem_limit_bytes=6 * MIB),
        cost_estimate=cost(0.5),
        name="pack",
    )(*map(near, (dq, own, *others)))


def merge_kernel(width, one_ref, two_ref, out_ref):
    for b in range(out_ref.shape[0]):
        out_ref[b, 0:16, :] = added_block(width, one_ref[b, 0:16, :], two_ref[b, 0:16, :])
        out_ref[b, 16:, :] = added(one_ref[b, 16:, :], two_ref[b, 16:, :])


def merge(width, one, two):
    return pl.pallas_call(
        functools.partial(merge_kernel, width),
        out_shape=kept(one.shape, BF16),
        in_specs=vmem(2),
        out_specs=vmem(1)[0],
        cost_estimate=cost(0.5),
        compiler_params=pltpu.CompilerParams(vmem_limit_bytes=3 * MIB),
        name="merge",
    )(near(one), near(two))


def head_grad_kernel(back_ref, x_in, small_ref, keep_ref, send_ref, x_ref, sems):
    copies = fetch(
        [x_in.at[h] for h in range(HEADS)], [x_ref.at[h] for h in range(HEADS)], sems
    )
    total = 0.0
    for h in range(HEADS):
        copies[h].wait()
        at = turned_by(lax.axis_index("dp"), RING[h], RING[HEADS - 1 - h])
        total = total + dot(back_ref[at], x_ref[h])
    turned = total.T
    feat, size = turned.shape
    blocks, step, lanes = keep_ref.shape
    small = small_ref[...]
    row = lax.broadcasted_iota(jnp.int32, (step, step), 0)
    empty = jnp.zeros((step, lanes - size - step), F32)
    for side in range(2):
        sums = jnp.concatenate([small[4 * side : 4 * side + 3], small[3:4], small[0:4] * 0.0], axis=0)
        sums = split_sum(sums).astype(F32)
        found = []
        for c in range(blocks):
            values = jnp.where(row % 8 == 3, sums[:, 0:step], sums[:, c * step : (c + 1) * step])
            start = side * feat // 2 + c * step
            block = [turned[start : start + step], values, empty]
            found.append(jnp.concatenate(block, axis=1).astype(BF16))
        for flip, ref in enumerate((keep_ref, send_ref)):

            @pl.when(lax.axis_index("dp") == (side + flip) % 2)
            def store():
                for c in range(blocks):
                    ref[c] = found[c]


def head_grads(blocks, back, x, small):
    feat = x.shape[2]
    step = feat // (2 * blocks)
    lanes = small.shape[1]
    return pl.pallas_call(
        head_grad_kernel,
        out_shape=(kept((blocks, step, lanes), BF16),) * 2,
        in_specs=vmem(1) + hbm(1) + vmem(1),
        out_specs=tuple(vmem(2)),
        scratch_shapes=[
            pltpu.VMEM(x.shape, BF16),
            pltpu.SemaphoreType.DMA((HEADS,)),
        ],
        compiler_params=pltpu.CompilerParams(vmem_limit_bytes=8 * MIB),
        cost_estimate=cost(1.5),
        name="head_grads",
    )(near(back), far(x), near(small))


def last_kernel(blocks, back_ref, gr_ref, *refs):
    gx_ref = refs[-1]
    feat = gr_ref.shape[1]
    size = feat // HEADS
    each = feat // blocks
    total = 0.0
    for part in range(3):
        turned = jnp.concatenate(
            [back_ref[h, part * size : (part + 1) * size, :] for h in range(HEADS)], axis=0
        )
        total = total + dot_t(turned.T, refs[part][...])
    for j in range(blocks):
        rows = rows_of(blocks, j, feat)
        gx_ref[:, rows] = (gr_ref[:, rows] + total[:, j * each : (j + 1) * each]).astype(
            gx_ref.dtype
        )


def last(blocks, back, gr, weights, kind):
    return pl.pallas_call(
        functools.partial(last_kernel, blocks),
        out_shape=(shaped if kind == F32 else kept)(gr.shape, kind),
        in_specs=vmem(2 + len(weights)),
        out_specs=vmem(1)[0],
        compiler_params=pltpu.CompilerParams(vmem_limit_bytes=6 * MIB),
        cost_estimate=cost(0.01),
        name="last",
    )(*map(near, (back, gr, *weights)))


def settle_kernel(
    pieces_ref, loss_ref, gq_ref, gk_ref, gv_ref, go_ref, g1_ref, g2_ref, g3_ref, inverse_ref
):
    step, feat = gq_ref.shape
    size = feat // HEADS
    width = 3 * size
    totals = jnp.sum(pieces_ref[...].astype(F32), axis=0)
    small = totals[0:8] + totals[8:16]
    sides = totals[step:]
    inverse = 1.0 / small[3:4, width + 1 : width + 2]
    inverse_ref[...] = jnp.broadcast_to(inverse, inverse_ref.shape)
    loss_ref[...] = small[3:4, width : width + 1] * inverse
    go_ref[...] = jnp.concatenate([sides[:step], sides[step:]], axis=1) * inverse
    for h in range(HEADS):
        block = pieces_ref[h, 0:step, :].astype(F32) * inverse
        for part, ref in enumerate((gq_ref, gk_ref, gv_ref)):
            ref[:, h * size : (h + 1) * size] = block[:, part * size : (part + 1) * size]
    for k, ref in enumerate((g1_ref, g2_ref, g3_ref)):
        ref[...] = small[k : k + 1, width : width + step] * inverse


def settle(pieces, feat):
    step = pieces.shape[1] // 3
    return pl.pallas_call(
        settle_kernel,
        out_shape=(
            shaped((1, 1), F32),
            shaped((step, feat), F32),
            shaped((step, feat), F32),
            shaped((step, feat), F32),
            shaped((step, feat), F32),
            shaped((1, step), F32),
            shaped((1, step), F32),
            shaped((1, step), F32),
            kept((8, 128), F32),
        ),
        in_specs=vmem(1),
        out_specs=tuple(vmem(9)),
        compiler_params=pltpu.CompilerParams(vmem_limit_bytes=4 * MIB),
        cost_estimate=pl.CostEstimate(
            flops=5500000000, bytes_accessed=1024, transcendentals=0
        ),
        name="settle",
    )(near(pieces))


def finish_kernel(inverse_ref, gx_in, pair_in, out_ref, gx_ref, gy_ref):
    inverse = inverse_ref[0:1, 0:1]
    tok = out_ref.shape[0]
    out_ref[...] = pair_in[0:tok]
    gx_ref[...] = gx_in[...].astype(F32) * inverse
    gy_ref[...] = pair_in[tok : 2 * tok].astype(F32) * inverse


def finish(inverse, gx, pair):
    tok, feat = gx.shape
    return pl.pallas_call(
        finish_kernel,
        out_shape=(
            shaped((tok, feat), BF16),
            shaped((tok, feat), F32),
            shaped((tok, feat), F32),
        ),
        in_specs=vmem(3),
        out_specs=tuple(vmem(3)),
        compiler_params=pltpu.CompilerParams(vmem_limit_bytes=6 * MIB),
        cost_estimate=cost(1),
        name="finish",
    )(near(inverse), gx, pair)


def spread_kernel(sums_in, inverse_ref, gu_ref, gd_ref, sums_ref, sem):
    (copy,) = fetch([sums_in], [sums_ref], sem)
    wide_step, feat = gd_ref.shape
    step = gu_ref.shape[0]
    copy.wait()
    main = sums_ref[0].astype(F32) * inverse_ref[0:1, 0:1]
    for j in range(gu_ref.shape[1] // feat):
        gu_ref[:, j * feat : (j + 1) * feat] = main[j * step : (j + 1) * step]
    gd_ref[...] = main[main.shape[0] - wide_step :]


def spread(sums, inverse, step, wide):
    feat = sums.shape[2]
    return pl.pallas_call(
        spread_kernel,
        out_shape=(shaped((step, wide), F32), shaped((wide * step // feat, feat), F32)),
        in_specs=hbm(1) + vmem(1),
        out_specs=tuple(vmem(2)),
        scratch_shapes=[pltpu.VMEM(sums.shape, BF16), pltpu.SemaphoreType.DMA((1,))],
        compiler_params=pltpu.CompilerParams(vmem_limit_bytes=4 * MIB),
        cost_estimate=cost(1),
        name="spread",
    )(far(sums), near(inverse))


def body(
    state_x,
    state_y,
    teacher,
    segment_ids,
    valid_mask,
    w_query,
    w_key,
    w_value,
    w_out,
    w_up,
    w_down,
    gain_attn,
    gain_ffn,
    gain_final,
):
    _, tok, feat = state_x.shape
    size = feat // HEADS
    ctx = lax.axis_size("ctx")
    sides = lax.axis_size("dp")
    ways = ctx // HEADS
    groups = [[h * ways + r for h in range(HEADS)] for r in range(ways)]
    side, place = lax.axis_index("dp"), lax.axis_index("ctx")
    wide = w_up.shape[1]
    cross = sides == 2 and ways == 2 and (feat // (sides * ctx)) % 16 == 0
    both = ("dp", "ctx")

    def both_ways(rings):
        return rings + [[ctx + place for place in reversed(ring)] for ring in rings]

    def moved(block):
        if not cross:
            return block
        route = []
        for s in range(2):
            for c in range(ctx):
                route.append((s * ctx + c, (c % 2) * ctx + c - c % 2 + s))
        return lax.ppermute(block, both, route)

    def shared(block):
        if sides == 2:
            return [block, swap(block, "dp", 1)]
        return [lax.all_gather(block, "dp", axis=0, tiled=True)]

    def exchange(block):
        return lax.all_to_all(block, "ctx", 0, 0, axis_index_groups=groups, tiled=True)

    def around(block, distance):
        if cross:
            return swap(block, "dp", 1)
        route = []
        for g in range(HEADS):
            for r in range(ways):
                route.append((g * ways + r, g * ways + (r + distance) % ways))
        return lax.ppermute(block, "ctx", route)

    x = moved(state_x[0])
    attn_weights = [shared(w) for w in (w_query, w_key, w_value)]
    segs = [segment_ids.reshape(ctx, tok)]
    if cross:
        segs.append(swap(segs[0], "dp", 1))
    mask = moved(valid_mask)
    pair = jnp.concatenate([state_y[0], teacher[0]], axis=0)
    qkv = project(x, attn_weights)
    plan = plan_of(segs, ways, ctx, tok)
    qkv = exchange(qkv)
    qkv, plan, mask, late_x, pair = lax.optimization_barrier((qkv, plan, mask, x, pair))
    kvs = [qkv] + [around(qkv, j) for j in range(1, ways)]
    o, of, lse = attend(plan, segs, kvs)
    gains = jnp.stack([gain_attn, gain_ffn, gain_final])
    if sides == 2:
        gains = shared(gains)
    else:
        gains = [lax.all_gather(gains, "dp", axis=1, tiled=True)]
    wo, wu, wd = shared(w_out), shared(w_up), shared(w_down)
    blocks = len(wu)
    o, pair = lax.optimization_barrier((o, moved(pair)))
    ot = exchange(o)
    ot, x_near, wo = lax.optimization_barrier((ot, *stage([x], wo)))
    ot = ot.reshape(feat, tok)
    pair, gr, do, small, *halves = middle(
        ot,
        mask,
        gains,
        x_near,
        pair,
        wo,
        wu,
        wd,
        [ffn_shape(ctx, feat, wide)] * (2 * cross),
    )
    do = do.reshape(HEADS, size, tok)
    if cross:
        rings = both_ways([[h * ways + r for h in RING] for r in range(ways)])
        gathered = lax.all_gather(late_x, both, axis=0, axis_index_groups=rings)
    do = exchange(do)
    if cross:
        sums, sides = join(halves[0], swap(halves[1], "dp", 1), feat // (2 * ctx))
        lse, sums = lax.optimization_barrier((lse, sums))
        kx, qx = prepare(segs, lse, kvs)
        do, kx, qx, sums, gathered = lax.optimization_barrier((do, kx, qx, sums, gathered))
        inner = both_ways([[4 * z + k for k in INNER] for z in range(4)])
        outer = both_ways([[4 * z + k for z in OUTER] for k in range(4)])
        sums = lax.psum_scatter(
            sums, both, scatter_dimension=0, axis_index_groups=inner, tiled=True
        )
    else:
        kx, qx = prepare(segs, lse, kvs)
    back_args = (plan, kx, qx, do, qkv)
    part, dx, *others = attend_back(
        *back_args, kvs[1:], ways, len(segs), tuple(range(1, ways)), of=of
    )
    others = [around(other, -(j + 1)) for j, other in enumerate(others)]
    dq, own = attend_back(
        *back_args, kvs[:1], ways, len(segs), (0,), part=part, dx=dx
    )
    sent = pack(dq, own, others)
    back = exchange(sent)
    back, *staged = lax.optimization_barrier((back, *stage([gr], *attn_weights)))
    if cross:
        mine, away = head_grads(ctx, sent, gathered, small)
        mine, away = halve(3 * size, mine, swap(away, "dp", 1), sides)
        pieces = merge(3 * size, mine, swap(away, "ctx", 1))
        pieces, sums, pair = lax.optimization_barrier((pieces, sums, pair))
        pair = moved(pair)
        sums = lax.psum_scatter(
            sums, both, scatter_dimension=0, axis_index_groups=outer, tiled=True
        )
        pieces = exchange(pieces)
        gx = moved(last(blocks, back, staged[0], staged[1:], BF16))
        loss, gq, gk, gv, go, g1, g2, g3, inverse = settle(pieces, feat)
        result, gx, gy = finish(inverse, gx, pair)
        gu, gd = spread(sums, inverse, gq.shape[0], wide)
        gains_out = [g.reshape(-1) for g in (g1, g2, g3)]
        loss = loss.reshape(())
    else:
        x1, h, df, dz, da = halves
        result, gy = pair[:tok], pair[tok:].astype(F32)
        total = lax.psum(small, both)
        inverse = 1.0 / total[3, 1]
        loss = total[3, 0] * inverse

        def scattered(block):
            block = block * inverse
            return lax.psum_scatter(block, both, scatter_dimension=0, tiled=True)

        gx = last(blocks, back, staged[0], staged[1:], F32)
        parts = [back[:, j * size : (j + 1) * size, :].reshape(feat, tok) for j in range(3)]
        gq, gk, gv = [scattered(dot_t(x.T, part)) for part in parts]
        go = scattered(dot(ot, da))
        gu = scattered(dot(x1.T, dz))
        gd = scattered(dot(h.T, df))
        gx, gy = gx * inverse, gy * inverse
        step = feat // (sides * ctx)
        number = side * ctx + place
        gains_out = [
            lax.dynamic_slice_in_dim(
                jnp.concatenate([total[k], total[k + 4]]) * inverse, number * step, step
            )
            for k in range(3)
        ]
    return (
        loss,
        result[None],
        gx[None],
        gy[None],
        gq,
        gk,
        gv,
        go,
        gu,
        gd,
        gains_out[0],
        gains_out[1],
        gains_out[2],
    )


def solution(mesh):
    tokens = P("dp", "ctx", None)
    rows = P("dp", None)
    spread = P(("dp", "ctx"), None)
    gain = P(("dp", "ctx"))
    return jax.shard_map(
        body,
        mesh=mesh,
        in_specs=(tokens,) * 3 + (rows, P("dp", "ctx")) + (rows,) * 6 + (P("dp"),) * 3,
        out_specs=(P(), tokens, tokens, tokens) + (spread,) * 6 + (gain,) * 3,
        check_vma=False,
    )
```

```python
import functools

import jax
import jax.numpy as jnp
from jax import lax
from jax.experimental import pallas as pl
from jax.experimental.pallas import tpu as pltpu
from jax.sharding import PartitionSpec as P

HEADS = 8
EPS = 1e-05
LANES = 32
DOCS = 24
UNROLL = 8
INNER = (0, 1, 3, 2)
OUTER = (0, 1, 2, 3)
RING = (0, 2, 4, 6, 7, 5, 3, 1)
GROUP = 8
GROUP_BACK = 4
FAR = -(2.0**100)
CORE = 0.7978845608028654
CUBE = 0.044715
MIB = 1024 * 1024

BF16 = jnp.bfloat16
F32 = jnp.float32


def dot(left, right):
    return jnp.dot(left, right, preferred_element_type=F32)


def dot_t(left, right):
    return lax.dot_general(left, right, (((1,), (1,)), ((), ())), preferred_element_type=F32)


def vmem(count):
    return [pl.BlockSpec(memory_space=pltpu.VMEM) for _ in range(count)]


def hbm(count):
    return [pl.BlockSpec(memory_space=pltpu.HBM) for _ in range(count)]


def smem():
    return pl.BlockSpec(memory_space=pltpu.SMEM)


def kept(shape, dtype):
    return pltpu.VMEM(shape, dtype)


def near(array):
    return pltpu.with_memory_space_constraint(array, pltpu.VMEM)


def apart(shape, dtype):
    return pltpu.HBM(shape, dtype)


def far(array):
    return pltpu.with_memory_space_constraint(array, pltpu.HBM)


def shaped(shape, dtype):
    return jax.ShapeDtypeStruct(shape, dtype)


def cost(us):
    return pl.CostEstimate(flops=1000, bytes_accessed=1024, transcendentals=0)


def swap(block, axis, bit):
    size = lax.axis_size(axis)
    return lax.ppermute(block, axis, [(i, i ^ bit) for i in range(size)])


def rank_of(ways, texts):
    if texts == 2:
        return lax.axis_index("dp")
    return lax.rem(lax.axis_index("ctx"), ways)


def rows_of(blocks, number, total):
    size = total // blocks
    if blocks == 1:
        return pl.ds(0, size)
    return pl.ds(pl.multiple_of((lax.axis_index("dp") + number) % 2 * size, size), size)


def turned_by(side, first, second):
    return jnp.where(side == 0, first, second)


def fetch(sources, targets, sems, first=0):
    copies = [
        pltpu.make_async_copy(source, target, sems.at[first + k])
        for k, (source, target) in enumerate(zip(sources, targets))
    ]
    for copy in copies:
        copy.start()
    return copies


def stage_kernel(layout, *refs):
    outs, sems = refs[len(layout) : -1], refs[-1]
    targets = [outs[k].at[pl.ds(start, size), :] for k, start, size in layout]
    for copy in fetch(refs[: len(layout)], targets, sems):
        copy.wait()


def stage(*groups):
    layout, shapes = [], []
    for k, group in enumerate(groups):
        start = 0
        for array in group:
            layout.append((k, start, array.shape[0]))
            start += array.shape[0]
        shapes.append(kept((start, group[0].shape[1]), group[0].dtype))
    flat = [far(array) for group in groups for array in group]
    return pl.pallas_call(
        functools.partial(stage_kernel, tuple(layout)),
        out_shape=tuple(shapes),
        in_specs=hbm(len(flat)),
        out_specs=tuple(vmem(len(groups))),
        scratch_shapes=[pltpu.SemaphoreType.DMA((len(flat),))],
        compiler_params=pltpu.CompilerParams(vmem_limit_bytes=4 * MIB),
        cost_estimate=cost(0.01),
        name="stage",
    )(*flat)


def project_kernel(blocks, x_ref, *refs):
    out_ref = refs[-1]
    feat = x_ref.shape[1]
    size = feat // HEADS
    x = jnp.concatenate([x_ref[:, rows_of(blocks, j, feat)] for j in range(blocks)], axis=1)
    for part, scale in ((0, size**-0.5), (1, 1.0), (2, 1.0)):
        weight = [refs[j * 3 + part][...] for j in range(blocks)]
        turned = (dot(x, jnp.concatenate(weight, axis=0)) * scale).astype(BF16).T
        for h in range(HEADS):
            out_ref[h, part * size : (part + 1) * size, :] = turned[h * size : (h + 1) * size, :]


def project(x, weights):
    tok, feat = x.shape
    flat = stage(*[[weight[0]] for weight in weights])
    flat += tuple(block for weight in weights for block in weight[1:])
    return pl.pallas_call(
        functools.partial(project_kernel, len(weights[0])),
        out_shape=kept((HEADS, 3 * feat // HEADS, tok), BF16),
        in_specs=vmem(1 + len(flat)),
        out_specs=vmem(1)[0],
        compiler_params=pltpu.CompilerParams(vmem_limit_bytes=6 * MIB),
        cost_estimate=cost(1.4),
        name="project",
    )(near(x), *map(near, flat))


def mask_rows(row, hit, miss, extra):
    number = lax.broadcasted_iota(jnp.int32, (LANES, row.shape[1]), 0)
    base = jnp.where(number == row, hit, miss)
    base = jnp.where(number < DOCS, base, 0.0)
    for k, value in enumerate(extra):
        base = jnp.where(number == DOCS + k, value, base)
    return base.astype(BF16)


def parts_of(value, count):
    found = []
    for _ in range(count):
        part = value.astype(BF16).astype(F32)
        found.append(part)
        value = value - part
    return found


def query_rows(q, row, extra):
    return jnp.concatenate([q, mask_rows(row, 0.0, FAR, extra)], axis=0).T


def key_rows(k, row):
    return jnp.concatenate([k, mask_rows(row, 1.0, 0.0, (1.0, 1.0, 1.0))], axis=0)


def list_size(count):
    return HEADS * count + 2 * GROUP


def plan_kernel(ways, count, tok, *refs):
    out_ref = refs[-1]
    rank = rank_of(ways, len(refs) - 1)
    flip = (lax.axis_index("dp") + lax.axis_index("ctx")) % 2
    length = list_size(count)

    def number(at):
        if len(refs) == 2:
            return refs[0][at]
        return jnp.where(flip == 0, refs[0][at], refs[1][at])

    firsts = [number(c * tok) for c in range(count)]
    lasts = [number(c * tok + tok - 1) for c in range(count)]

    def one(i, found):
        chunk = i * ways + rank
        first = number(chunk * tok)
        last = number(chunk * tok + tok - 1)
        low = sum((value < first).astype(jnp.int32) for value in lasts)
        high = sum((value <= last).astype(jnp.int32) for value in firsts)

        def other(c, found):
            own = (lax.rem(c, ways) == rank).astype(jnp.int32)
            every, mine, rest = found
            out_ref[every] = i
            out_ref[length + every] = c
            at = jnp.where(own == 1, 2 * length + mine, 4 * length + rest)
            out_ref[at] = i
            out_ref[at + length] = c
            return every + 1, mine + own, rest + 1 - own

        return lax.fori_loop(low, high, other, found)

    found = lax.fori_loop(0, HEADS, one, (jnp.int32(0),) * 3)
    for k, ended in enumerate(found):
        for g in range(GROUP):
            out_ref[2 * k * length + ended + g] = HEADS
            out_ref[(2 * k + 1) * length + ended + g] = 0
        size = GROUP if k == 0 else GROUP_BACK
        out_ref[6 * length + k] = (ended + size - 1) // size


def plan_of(segs, ways, count, tok):
    size = 6 * list_size(count) + 8
    return pl.pallas_call(
        functools.partial(plan_kernel, ways, count, tok),
        out_shape=shaped((size,), jnp.int32),
        in_specs=[smem()] * len(segs),
        out_specs=smem(),
        cost_estimate=cost(1),
        compiler_params=pltpu.CompilerParams(vmem_limit_bytes=1 * MIB),
        name="plan",
    )(*[seg.reshape(-1) for seg in segs])


def chosen(seg_refs):
    if len(seg_refs) == 1:
        return seg_refs[0][...]
    flip = (lax.axis_index("dp") + lax.axis_index("ctx")) % 2
    return jnp.where(flip == 0, seg_refs[0][...], seg_refs[1][...])


def tiles_of(plan_ref, kind, length, g):
    found = []
    size = GROUP if kind == 0 else GROUP_BACK
    for k in range(size):
        at = 2 * kind * length + g * size + k
        found.append((plan_ref[at], plan_ref[at + length]))
    return found


def chunk_of(h, slot, ways, rank):
    return h * ways + lax.rem(rank - slot + ways, ways)


def forward_kernel(ways, texts, plan_ref, *refs):
    seg_refs, refs = refs[:texts], refs[texts:]
    kv_refs = refs[:ways]
    q_ref = kv_refs[0]
    o_ref, of_out, lse_ref, kx, vx, qx, acc, seg_ref, of_ref, sem = refs[ways:]
    seg_ref[...] = chosen(seg_refs)
    count, tok = seg_ref.shape
    size = q_ref.shape[1] // 3
    rank = rank_of(ways, texts)
    length = list_size(count)
    ones = (lax.broadcasted_iota(jnp.int32, (16, tok), 0) == 0).astype(F32).astype(BF16)
    for slot in range(ways):

        @pl.loop(0, HEADS, unroll=UNROLL)
        def fill(h):
            chunk = chunk_of(h, slot, ways, rank)
            keys = kv_refs[slot][h, size : 2 * size, :]
            kx[chunk] = key_rows(keys, seg_ref[pl.ds(chunk, 1), :])
            vx[chunk] = jnp.concatenate([kv_refs[slot][h, 2 * size : 3 * size, :], ones], axis=0)

    @pl.loop(0, HEADS, unroll=UNROLL)
    def fill_query(i):
        qx[i] = query_rows(q_ref[i, 0:size, :], seg_ref[pl.ds(i * ways + rank, 1), :], ())
        acc[i] = jnp.zeros_like(acc[i])

    qx[HEADS] = query_rows(jnp.zeros((size, tok), BF16), jnp.full((1, tok), -1, jnp.int32), ())
    acc[HEADS] = jnp.zeros_like(acc[0])

    @pl.loop(0, plan_ref[6 * length])
    def group(g):
        tiles = tiles_of(plan_ref, 0, length, g)
        weights = [jnp.exp(dot(qx[i], kx[c])).astype(BF16) for i, c in tiles]
        mixed = [dot_t(vx[c], w) for (i, c), w in zip(tiles, weights)]
        for (i, c), part in zip(tiles, mixed):
            acc[i] += part

    leaving = []
    smallest = jnp.full((1, tok), 1.0, F32)
    largest = jnp.full((1, tok), 1.0, F32)
    for i in range(HEADS):
        total = acc[i, size : size + 1, :]
        smallest = jnp.minimum(smallest, total)
        largest = jnp.maximum(largest, total)
        out = acc[i, 0:size, :] / total
        of_ref[i] = out
        leaving += fetch([of_ref.at[i]], [of_out.at[i]], sem, i)
        o_ref[i] = out.astype(BF16)
        lse_ref[i : i + 1, :] = jnp.log(total)
    for copy in leaving:
        copy.wait()
    good = (jnp.min(smallest) > 2.0**-90) & (jnp.max(largest) < 2.0**90)

    @pl.when(jnp.logical_not(good))
    def any_scores():
        @pl.loop(0, HEADS)
        def one(i):
            query = qx[i]

            def step(c, carry):
                top, total, mixed = carry
                s = dot(query, kx[c])
                new = jnp.maximum(top, jnp.max(s, axis=1, keepdims=True))
                fade = jnp.exp(top - new)
                w = jnp.exp(s - new)
                total = total * fade + jnp.sum(w, axis=1, keepdims=True)
                mixed = mixed * fade + dot_t(w.astype(BF16), vx[c])
                return new, total, mixed

            top, total, mixed = lax.fori_loop(
                0,
                count,
                step,
                (
                    jnp.full((tok, 1), -3e38, F32),
                    jnp.zeros((tok, 1), F32),
                    jnp.zeros((tok, size + 16), F32),
                ),
            )
            out = (mixed / total).T[0:size, :]
            of_ref[i] = out
            o_ref[i] = out.astype(BF16)
            lse = jnp.broadcast_to(top + jnp.log(total), (tok, 128)).T
            lse_ref[pl.ds(i, 1), :] = lse[0:1, :]

        fetch([of_ref], [of_out], sem)[0].wait()


def attend(plan, segs, kvs):
    ways = len(kvs)
    _, size, tok = kvs[0].shape
    size = size // 3
    count = segs[0].shape[0]
    depth = size + LANES
    return pl.pallas_call(
        functools.partial(forward_kernel, ways, len(segs)),
        out_shape=(
            kept((HEADS, size, tok), BF16),
            apart((HEADS, size, tok), F32),
            kept((HEADS, tok), F32),
        ),
        in_specs=[smem()] + vmem(len(segs) + ways),
        out_specs=(vmem(1)[0], hbm(1)[0], vmem(1)[0]),
        scratch_shapes=[
            pltpu.VMEM((count, depth, tok), BF16),
            pltpu.VMEM((count, size + 16, tok), BF16),
            pltpu.VMEM((HEADS + 1, tok, depth), BF16),
            pltpu.VMEM((HEADS + 1, size + 16, tok), F32),
            pltpu.VMEM(segs[0].shape, jnp.int32),
            pltpu.VMEM((HEADS, size, tok), F32),
            pltpu.SemaphoreType.DMA((HEADS,)),
        ],
        compiler_params=pltpu.CompilerParams(vmem_limit_bytes=12 * MIB),
        cost_estimate=cost(7),
        name="attend",
    )(far(plan), *segs, *map(near, kvs))


def prepare_kernel(ways, texts, lse_ref, *refs):
    seg_refs, refs = refs[:texts], refs[texts:]
    kv_ins = refs[:ways]
    kx, qx, seg_ref, k_ref, q_ref, sems = refs[ways:]
    size = q_ref.shape[1]
    there = (slice(None), pl.ds(size, size), slice(None))
    copies = fetch([kv.at[there] for kv in kv_ins], [k_ref.at[k] for k in range(ways)], sems)
    there = (slice(None), pl.ds(0, size), slice(None))
    copies += fetch([kv_ins[0].at[there]], [q_ref], sems, ways)
    seg_ref[...] = chosen(seg_refs)
    tok = seg_ref.shape[1]
    rank = rank_of(ways, texts)
    for slot in range(ways):
        copies[slot].wait()

        @pl.loop(0, HEADS, unroll=UNROLL)
        def fill(h):
            chunk = chunk_of(h, slot, ways, rank)
            kx[chunk] = key_rows(k_ref[slot, h], seg_ref[pl.ds(chunk, 1), :])

    copies[ways].wait()

    @pl.loop(0, HEADS, unroll=UNROLL)
    def fill_query(i):
        lse = parts_of(-lse_ref[pl.ds(i, 1), :], 3)
        qx[i] = query_rows(q_ref[i], seg_ref[pl.ds(i * ways + rank, 1), :], lse)

    qx[HEADS] = query_rows(jnp.zeros((size, tok), BF16), jnp.full((1, tok), -1, jnp.int32), ())


def prepare(segs, lse, kvs):
    ways = len(kvs)
    count, tok = segs[0].shape
    size = kvs[0].shape[1] // 3
    depth = size + LANES
    return pl.pallas_call(
        functools.partial(prepare_kernel, ways, len(segs)),
        out_shape=(kept((count, depth, tok), BF16), kept((HEADS + 1, tok, depth), BF16)),
        in_specs=vmem(1 + len(segs)) + hbm(ways),
        out_specs=tuple(vmem(2)),
        scratch_shapes=[
            pltpu.VMEM(segs[0].shape, jnp.int32),
            pltpu.VMEM((ways, HEADS, size, tok), BF16),
            pltpu.VMEM((HEADS, size, tok), BF16),
            pltpu.SemaphoreType.DMA((ways + 1,)),
        ],
        compiler_params=pltpu.CompilerParams(vmem_limit_bytes=12 * MIB),
        cost_estimate=cost(2),
        name="prepare",
    )(near(lse), *segs, *map(far, kvs))


def backward_kernel(ways, slots, final, texts, plan_ref, kx, qx, do_ref, *refs):
    many = len(slots)
    q_in, kv_ins, refs = refs[0], refs[1 : 1 + many], refs[1 + many :]
    if final:
        part_ref, dx, dq_ref, *dkv_refs = refs[: 3 + many]
        refs = refs[3 + many :]
    else:
        of_in, dq_ref, dx, *dkv_refs = refs[: 3 + many]
        refs = refs[3 + many :]
    vx, dk, dv, dq, q_ref, v_ref, of_ref, sems = refs
    count, _, tok = kx.shape
    size = do_ref.shape[1]
    copies = []
    if not final:
        copies += fetch([of_in], [of_ref], sems, 1 + many)
    for k, kv in enumerate(kv_ins):
        there = (slice(None), pl.ds(2 * size, size), slice(None))
        copies += fetch([kv.at[there]], [v_ref.at[k]], sems, 1 + k)
    there = (slice(None), pl.ds(0, size), slice(None))
    copies += fetch([q_in.at[there]], [q_ref], sems)
    rank = rank_of(ways, texts)
    ones = (lax.broadcasted_iota(jnp.int32, (16, tok), 0) < 2).astype(F32).astype(BF16)

    def open_query(i):
        do = do_ref[i].astype(F32)
        delta = parts_of(-jnp.sum(do * of_ref[i], axis=0, keepdims=True), 3)
        number = lax.broadcasted_iota(jnp.int32, (16, tok), 0)
        tail = jnp.where(number == 0, delta[0], jnp.where(number == 1, delta[1], 0.0))
        dx[i] = jnp.concatenate([do_ref[i], tail.astype(BF16)], axis=0).T

    if final:
        dq[0:HEADS] = part_ref[...]
    else:
        copies.pop(0).wait()
        pl.loop(0, HEADS, unroll=UNROLL)(open_query)
        dx[HEADS] = jnp.zeros_like(dx[0])
        dq[0:HEADS] = jnp.zeros_like(dq[0:HEADS])
    dq[HEADS] = jnp.zeros_like(dq[0])
    for copy in copies:
        copy.wait()
    for k, slot in enumerate(slots):

        @pl.loop(0, HEADS, unroll=UNROLL)
        def fill(h):
            chunk = chunk_of(h, slot, ways, rank)
            vx[chunk] = jnp.concatenate([v_ref[k, h], ones], axis=0)
            dk[chunk] = jnp.zeros_like(dk[chunk])
            dv[chunk] = jnp.zeros_like(dv[chunk])

    kind = 1 if slots == (0,) else 2
    length = list_size(count)

    @pl.loop(0, plan_ref[6 * length + kind])
    def group(g):
        tiles = tiles_of(plan_ref, kind, length, g)
        weights = [jnp.exp(dot(qx[i], kx[c])) for i, c in tiles]
        pulls = [dot(dx[i], vx[c]) for i, c in tiles]
        scores = [(w * p).astype(BF16) for w, p in zip(weights, pulls)]
        for (i, c), w, ds in zip(tiles, weights, scores):
            j = jnp.minimum(i, HEADS - 1)
            dv[c] += dot(do_ref[j], w.astype(BF16))
            dk[c] += dot(q_ref[j], ds)
            dq[i] += dot_t(kx[c, 0:size, :], ds)

    for slot, out in zip(slots, dkv_refs):

        @pl.loop(0, HEADS, unroll=UNROLL)
        def drain(h):
            chunk = chunk_of(h, slot, ways, rank)
            out[h, 0:size, :] = dk[chunk].astype(out.dtype)
            out[h, size : 2 * size, :] = dv[chunk].astype(out.dtype)

    @pl.loop(0, HEADS, unroll=UNROLL)
    def drain_query(i):
        if final:
            dq_ref[i] = (dq[i] * size**-0.5).astype(BF16)
        else:
            dq_ref[i] = dq[i]


def attend_back(plan, kx, qx, do, q, kvs, ways, texts, slots, of=None, part=None, dx=None):
    many = len(slots)
    final = part is not None
    _, size, tok = do.shape
    count, depth, _ = kx.shape
    queries = kept((HEADS, size, tok), BF16 if final else F32)
    grads = (kept((HEADS, 2 * size, tok), F32 if slots == (0,) else BF16),) * many
    pulls = kept((HEADS + 1, tok, size + 16), BF16)
    return pl.pallas_call(
        functools.partial(backward_kernel, ways, slots, final, texts),
        out_shape=(queries,) + ((pulls,) * (not final)) + grads,
        in_specs=[smem()]
        + vmem(3)
        + hbm(1 + many)
        + (vmem(2) if final else hbm(1)),
        out_specs=tuple(vmem(1 + many + (not final))),
        scratch_shapes=[
            pltpu.VMEM((count, size + 16, tok), BF16),
            pltpu.VMEM((count, size, tok), F32),
            pltpu.VMEM((count, size, tok), F32),
            pltpu.VMEM((HEADS + 1, size, tok), F32),
            pltpu.VMEM((HEADS, size, tok), BF16),
            pltpu.VMEM((many, HEADS, size, tok), BF16),
            pltpu.VMEM((HEADS, size, tok), F32),
            pltpu.SemaphoreType.DMA((2 + many,)),
        ],
        compiler_params=pltpu.CompilerParams(vmem_limit_bytes=16 * MIB),
        cost_estimate=cost(7.5),
        name="attend_back",
    )(
        far(plan),
        *map(near, (kx, qx, do)),
        far(q),
        *map(far, kvs),
        *((near(part), near(dx)) if final else (far(of),)),
    )


def normed(rows):
    centred = rows - jnp.mean(rows, axis=-1, keepdims=True)
    spread = jnp.mean(centred * centred, axis=-1, keepdims=True)
    inverse = lax.rsqrt(spread + EPS)
    return centred * inverse, inverse


def norm_back(n, inverse, gain, up):
    scaled = up * gain
    mean_one = jnp.mean(scaled, axis=-1, keepdims=True)
    mean_two = jnp.mean(scaled * n, axis=-1, keepdims=True)
    grad = inverse * (scaled - mean_one - n * mean_two)
    return grad, jnp.sum(up * n, axis=0, keepdims=True)


def middle_kernel(blocks, tile, *refs):
    ot_ref, mask_ref = refs[:2]
    gains_refs = refs[2 : 2 + blocks]
    refs = refs[2 + blocks :]
    x_ref, wo_ref, both_in = refs[:3]
    wu_in, wd_in = [refs[3 + k * blocks : 3 + (k + 1) * blocks] for k in range(2)]
    (
        both_out,
        gr_out,
        dot_ref,
        small_ref,
        *grad_outs,
        x1_ref,
        h_ref,
        df_ref,
        dz_ref,
        da_ref,
        slope,
        acc,
        gr_ref,
        y_ref,
        t_ref,
        wu_ref,
        wd_ref,
        xt,
        sum_refs,
        out_ref,
        gy_ref,
        sems,
        tile_sems,
        sum_sems,
    ) = refs[3 + 2 * blocks :]
    part_rows = wo_ref.shape[0] // blocks
    wide = h_ref.shape[1]
    each = wide // blocks

    def columns(start):
        if blocks == 2:
            start = (start + lax.axis_index("dp") * each) % wide
        return pl.ds(pl.multiple_of(start, tile), tile)

    tiles = []
    for k, start in enumerate(range(0, wide, tile)):
        cols = columns(start)
        tiles.append(
            fetch(
                [*[ref.at[:, cols] for ref in wu_in], wd_in[start // each].at[pl.ds(start % each, tile), :]],
                [
                    *[wu_ref.at[pl.ds(j * part_rows, part_rows), cols] for j in range(blocks)],
                    wd_ref.at[pl.ds(start, tile), :],
                ],
                tile_sems,
                k * (blocks + 1),
            )
        )
    tok = x_ref.shape[0]
    late = fetch(
        [both_in.at[pl.ds(0, tok), :], both_in.at[pl.ds(tok, tok), :]],
        [y_ref, t_ref],
        sems,
        blocks + 1,
    )
    rows, feat = x_ref.shape
    halves = [rows_of(blocks, j, feat) for j in range(blocks)]

    def ordered(values):
        if blocks == 1:
            return values
        low, high = values[:, : feat // 2], values[:, feat // 2 :]
        turned = jnp.concatenate([high, low], axis=1)
        return jnp.where(lax.axis_index("dp") == 0, values, turned)

    gains = gains_refs[0][...].astype(F32)
    if blocks == 2:
        other = gains_refs[1][...].astype(F32)
        gains = jnp.where(
            lax.axis_index("dp") == 0,
            jnp.concatenate([gains, other], axis=1),
            jnp.concatenate([other, gains], axis=1),
        )
    g1, g2, g3 = gains[0:1], gains[1:2], gains[2:3]
    branch = dot(
        jnp.concatenate([ot_ref[rows_j, :] for rows_j in halves], axis=0).T,
        wo_ref[...],
    )
    n1, r1 = normed(x_ref[...].astype(F32) + branch)
    x1 = n1 * g1
    x1_ref[...] = ordered(x1).astype(BF16)

    def weight_up(start):
        return wu_ref[:, columns(start)]

    for start in range(0, wide, tile):
        cols = slice(start, start + tile)
        for copy in tiles[start // tile]:
            copy.wait()
        z = dot(x1_ref[...], weight_up(start))
        z2 = z * z
        th = jnp.tanh(z * (CORE + (CORE * CUBE) * z2))
        half = 0.5 + 0.5 * th
        h = (z * half).astype(BF16)
        slope[:, cols] = half + z * (1.0 - th * th) * (0.5 * CORE + (1.5 * CORE * CUBE) * z2)
        h_ref[:, cols] = h
        part = dot(h, wd_ref[start : start + tile, :])
        if start:
            acc[...] += part
        else:
            acc[...] = part

    ffn = acc[...]
    n2, r2 = normed(x1 + ffn)
    for copy in late:
        copy.wait()
    n3, r3 = normed(y_ref[...].astype(F32) + branch + ffn)
    result = n2 * g2 + n3 * g3
    out_ref[...] = result.astype(BF16)
    mask_row = mask_ref[...].astype(F32)
    mask = jnp.broadcast_to(mask_row, (8, rows)).T[:, 0:1]
    differ = result - t_ref[...].astype(F32)
    error = jnp.sum(mask * differ * differ)
    valid = jnp.sum(mask_row)
    upstream = 2.0 * mask * differ
    gy, dg3 = norm_back(n3, r3, g3, upstream)
    du, dg2 = norm_back(n2, r2, g2, upstream)
    gy_ref[...] = gy.astype(gy_ref.dtype)
    df_ref[...] = (du + gy).astype(BF16)
    going = [] if len(grad_outs) == 2 else None
    if going is not None:
        count, depth, _ = grad_outs[0].shape
        step = feat // (2 * count)
        wide_step = wide // (2 * count)
        parts = wide // feat

        def put(flip, first, base, size, values):
            side = (lax.axis_index("dp") + flip) % 2
            for k in range(values.shape[0] // size):
                c = first + k
                at = INNER.index(c % 4) * 4 + OUTER.index(c // 4)
                at = turned_by(side, at, 15 - at)
                sum_refs[flip, at, pl.ds(base, size), :] = values[
                    k * size : (k + 1) * size
                ].astype(BF16)

        def send(flip, base, size):
            span = pl.ds(base, size)
            going.extend(
                fetch(
                    [sum_refs.at[flip, :, span, :]],
                    [grad_outs[flip].at[:, span, :]],
                    sum_sems,
                    len(going),
                )
            )

        xt[...] = x1_ref[...].T
        for flip in (1, 0):
            for start in range(0, wide // 2, tile):
                cols = slice(flip * (wide // 2) + start, flip * (wide // 2) + start + tile)
                g = dot(h_ref[:, cols].T, df_ref[...])
                put(flip, start // wide_step, parts * step, wide_step, g)
            send(flip, parts * step, wide_step)
    for start in range(0, wide, tile):
        cols = slice(start, start + tile)
        dz = (dot_t(df_ref[...], wd_ref[start : start + tile, :]) * slope[:, cols]).astype(BF16)
        dz_ref[:, cols] = dz

    back = 0.0
    for k in range(blocks):
        start = k * each
        if blocks == 2:
            start = (start + lax.axis_index("dp") * each) % wide
        cols = pl.ds(pl.multiple_of(start, each), each)
        back = back + dot_t(dz_ref[:, k * each : (k + 1) * each], wu_ref[:, cols])
    if going is not None:
        for start in range(0, wide, tile):
            g = dot(xt[...], dz_ref[:, start : start + tile])
            base = (start + lax.axis_index("dp") * each) % wide // feat * step
            for flip in (1, 0):
                half_g = g[flip * (feat // 2) : (flip + 1) * (feat // 2)]
                put(flip, 0, pl.multiple_of(base, step), step, half_g)
                send(flip, pl.multiple_of(base, step), step)

    gr, dg1 = norm_back(n1, r1, g1, du + ordered(back))
    gr_ref[...] = gr
    leaving = fetch(
        [gr_ref, out_ref, gy_ref],
        [gr_out, both_out.at[pl.ds(0, tok), :], both_out.at[pl.ds(tok, tok), :]],
        sems,
    )
    da = (gr + gy).astype(BF16)
    da_ref[...] = da
    turned = dot_t(wo_ref[...], da).astype(BF16)
    for j in range(blocks):
        size = feat // blocks
        dot_ref[halves[j], :] = turned[j * size : (j + 1) * size]
    lane = lax.broadcasted_iota(jnp.int32, (1, feat), 1)
    scalars = jnp.where(lane == 0, error, jnp.where(lane == 1, valid, 0.0))
    sums = jnp.concatenate([dg1, dg2, dg3, scalars], axis=0)
    small_ref[...] = jnp.concatenate([sums[:, : feat // 2], sums[:, feat // 2 :]], axis=0)
    if going is None:
        for out, ref in zip(grad_outs, (x1_ref, h_ref, df_ref, dz_ref, da_ref)):
            out[...] = ref[...]
    else:
        for flip in (1, 0):
            side = (lax.axis_index("dp") + flip) % 2
            part = pl.ds(pl.multiple_of(side * (feat // 2), feat // 2), feat // 2)
            put(flip, 0, parts * step + wide_step, step, dot(ot_ref[part, :], da))
            send(flip, parts * step + wide_step, step)
    for copy in leaving + (going or []):
        copy.wait()


def middle(ot, mask, gains, x, pair, wo, wu, wd, scattered):
    tok, feat = x.shape
    wide = wu[0].shape[1]
    blocks = len(gains)
    tile = min(512, wide // blocks)
    return pl.pallas_call(
        functools.partial(middle_kernel, blocks, tile),
        out_shape=(
            apart((2 * tok, feat), BF16),
            apart((tok, feat), F32),
            kept((feat, tok), BF16),
            kept((8, feat // 2), F32),
        )
        + (
            tuple(apart(shape, BF16) for shape in scattered)
            or tuple(shaped((tok, size), BF16) for size in (feat, wide, feat, wide, feat))
        ),
        in_specs=vmem(4 + blocks) + hbm(1 + 2 * blocks),
        out_specs=tuple(hbm(2) + vmem(2) + (hbm(len(scattered)) or vmem(5))),
        scratch_shapes=[
            pltpu.VMEM((tok, feat), BF16),
            pltpu.VMEM((tok, wide), BF16),
            pltpu.VMEM((tok, feat), BF16),
            pltpu.VMEM((tok, wide), BF16),
            pltpu.VMEM((tok, feat), BF16),
            pltpu.VMEM((tok, wide), F32),
            pltpu.VMEM((tok, feat), F32),
            pltpu.VMEM((tok, feat), F32),
            pltpu.VMEM((tok, feat), BF16),
            pltpu.VMEM((tok, feat), BF16),
            pltpu.VMEM((feat, wide), BF16),
            pltpu.VMEM((wide, feat), BF16),
            pltpu.VMEM((feat, tok), BF16),
            pltpu.VMEM((2, *(scattered[0] if scattered else (8, 16, 128))), BF16),
            pltpu.VMEM((tok, feat), BF16),
            pltpu.VMEM((tok, feat), BF16),
            pltpu.SemaphoreType.DMA((blocks + 3,)),
            pltpu.SemaphoreType.DMA((wide // tile * (blocks + 1),)),
            pltpu.SemaphoreType.DMA((2 * PIECES,)),
        ],
        compiler_params=pltpu.CompilerParams(vmem_limit_bytes=36 * MIB),
        cost_estimate=cost(8),
        name="middle",
    )(near(ot), mask, *gains, near(x), near(wo), *map(far, (pair, *wu, *wd)))


def split_sum(values):
    high = values.astype(BF16)
    low = (values - high.astype(F32)).astype(BF16)
    return jnp.concatenate([high.astype(F32), low.astype(F32)], axis=0).astype(BF16)


PIECES = 8


def ffn_shape(blocks, feat, wide):
    step = feat // (2 * blocks)
    return (blocks, (wide // feat) * step + wide // (2 * blocks) + step, feat)


def join_kernel(two_ref, one_in, out, side_ref, one_ref, ref, sems):
    blocks, depth, feat = two_ref.shape
    main = ref.shape[1]
    step = depth - main
    spans = [pl.ds(k * blocks // PIECES, blocks // PIECES) for k in range(PIECES)]
    ones = fetch([one_in.at[k] for k in spans], [one_ref.at[k] for k in spans], sems)
    going = []
    for k, (span, one) in enumerate(zip(spans, ones)):
        one.wait()
        for b in range(k * blocks // PIECES, (k + 1) * blocks // PIECES):
            total = added(one_ref[b], two_ref[b])
            ref[b] = total[:main]
            places = [OUTER[at % 4] * 4 + INNER[at // 4] for at in (b, 15 - b)]
            c = turned_by(lax.axis_index("dp"), *places)
            side_ref[c, 0:step, :] = total[main:, : feat // 2]
            side_ref[c, step : 2 * step, :] = total[main:, feat // 2 :]
        going += fetch([ref.at[span]], [out.at[span]], sems, PIECES + k)
    for copy in going:
        copy.wait()


def join(one, two, step):
    blocks, depth, feat = one.shape
    return pl.pallas_call(
        join_kernel,
        out_shape=(
            apart((blocks, depth - step, feat), BF16),
            kept((blocks, 2 * step, feat // 2), BF16),
        ),
        in_specs=vmem(1) + hbm(1),
        out_specs=tuple(hbm(1) + vmem(1)),
        scratch_shapes=[
            pltpu.VMEM(one.shape, BF16),
            pltpu.VMEM((blocks, depth - step, feat), BF16),
            pltpu.SemaphoreType.DMA((2 * PIECES,)),
        ],
        compiler_params=pltpu.CompilerParams(vmem_limit_bytes=10 * MIB),
        cost_estimate=cost(0.01),
        name="join",
    )(near(two), far(one))


def added(one, two):
    return (one.astype(F32) + two.astype(F32)).astype(BF16)


def added_block(width, one, two):
    total = one.astype(F32) + two.astype(F32)
    parts = split_sum(total[0:8] + total[8:16]).astype(F32)
    lane = lax.broadcasted_iota(jnp.int32, total.shape, 1)
    return jnp.where(lane < width, total, parts).astype(BF16)


def halve_kernel(width, keep_ref, got_ref, side_ref, next_ref, send_ref):
    mine = lax.rem(lax.axis_index("ctx"), 2)

    @pl.loop(0, next_ref.shape[0])
    def one(b):
        for ref, which in ((send_ref, 1 - mine), (next_ref, mine)):
            at = 2 * b + which
            total = added_block(width, keep_ref[at], got_ref[at])
            ref[b] = jnp.concatenate([total, side_ref[at]], axis=0)


def halve(width, keep, got, side):
    blocks, depth, lanes = keep.shape
    depth += side.shape[1]
    return pl.pallas_call(
        functools.partial(halve_kernel, width),
        out_shape=(kept((blocks // 2, depth, lanes), BF16),) * 2,
        in_specs=vmem(3),
        out_specs=tuple(vmem(2)),
        compiler_params=pltpu.CompilerParams(vmem_limit_bytes=6 * MIB),
        cost_estimate=cost(1),
        name="halve",
    )(near(keep), near(got), near(side))


def pack_kernel(dq_ref, own_ref, *refs):
    others, out_ref = refs[:-1], refs[-1]
    size = dq_ref.shape[1]
    for h in range(HEADS):
        total = own_ref[h]
        for ref in others:
            total = total + ref[h].astype(F32)
        out_ref[h, 0:size, :] = dq_ref[h]
        out_ref[h, size : 3 * size, :] = total.astype(BF16)


def pack(dq, own, others):
    heads, size, tok = dq.shape
    return pl.pallas_call(
        pack_kernel,
        out_shape=kept((heads, 3 * size, tok), BF16),
        in_specs=vmem(2 + len(others)),
        out_specs=vmem(1)[0],
        compiler_params=pltpu.CompilerParams(vmem_limit_bytes=6 * MIB),
        cost_estimate=cost(0.5),
        name="pack",
    )(*map(near, (dq, own, *others)))


def merge_kernel(width, one_ref, two_ref, out_ref):
    for b in range(out_ref.shape[0]):
        out_ref[b, 0:16, :] = added_block(width, one_ref[b, 0:16, :], two_ref[b, 0:16, :])
        out_ref[b, 16:, :] = added(one_ref[b, 16:, :], two_ref[b, 16:, :])


def merge(width, one, two):
    return pl.pallas_call(
        functools.partial(merge_kernel, width),
        out_shape=kept(one.shape, BF16),
        in_specs=vmem(2),
        out_specs=vmem(1)[0],
        cost_estimate=cost(0.5),
        compiler_params=pltpu.CompilerParams(vmem_limit_bytes=3 * MIB),
        name="merge",
    )(near(one), near(two))


def head_grad_kernel(back_ref, x_in, small_ref, keep_ref, send_ref, x_ref, sems):
    copies = fetch(
        [x_in.at[h] for h in range(HEADS)], [x_ref.at[h] for h in range(HEADS)], sems
    )
    total = 0.0
    for h in range(HEADS):
        copies[h].wait()
        at = turned_by(lax.axis_index("dp"), RING[h], RING[HEADS - 1 - h])
        total = total + dot(back_ref[at], x_ref[h])
    turned = total.T
    feat, size = turned.shape
    blocks, step, lanes = keep_ref.shape
    small = small_ref[...]
    row = lax.broadcasted_iota(jnp.int32, (step, step), 0)
    empty = jnp.zeros((step, lanes - size - step), F32)
    for side in range(2):
        sums = jnp.concatenate([small[4 * side : 4 * side + 3], small[3:4], small[0:4] * 0.0], axis=0)
        sums = split_sum(sums).astype(F32)
        found = []
        for c in range(blocks):
            values = jnp.where(row % 8 == 3, sums[:, 0:step], sums[:, c * step : (c + 1) * step])
            start = side * feat // 2 + c * step
            block = [turned[start : start + step], values, empty]
            found.append(jnp.concatenate(block, axis=1).astype(BF16))
        for flip, ref in enumerate((keep_ref, send_ref)):

            @pl.when(lax.axis_index("dp") == (side + flip) % 2)
            def store():
                for c in range(blocks):
                    ref[c] = found[c]


def head_grads(blocks, back, x, small):
    feat = x.shape[2]
    step = feat // (2 * blocks)
    lanes = small.shape[1]
    return pl.pallas_call(
        head_grad_kernel,
        out_shape=(kept((blocks, step, lanes), BF16),) * 2,
        in_specs=vmem(1) + hbm(1) + vmem(1),
        out_specs=tuple(vmem(2)),
        scratch_shapes=[
            pltpu.VMEM(x.shape, BF16),
            pltpu.SemaphoreType.DMA((HEADS,)),
        ],
        compiler_params=pltpu.CompilerParams(vmem_limit_bytes=8 * MIB),
        cost_estimate=cost(1.5),
        name="head_grads",
    )(near(back), far(x), near(small))


def last_kernel(blocks, back_ref, gr_ref, *refs):
    gx_ref = refs[-1]
    feat = gr_ref.shape[1]
    size = feat // HEADS
    each = feat // blocks
    total = 0.0
    for part in range(3):
        turned = jnp.concatenate(
            [back_ref[h, part * size : (part + 1) * size, :] for h in range(HEADS)], axis=0
        )
        total = total + dot_t(turned.T, refs[part][...])
    for j in range(blocks):
        rows = rows_of(blocks, j, feat)
        gx_ref[:, rows] = (gr_ref[:, rows] + total[:, j * each : (j + 1) * each]).astype(
            gx_ref.dtype
        )


def last(blocks, back, gr, weights, kind):
    return pl.pallas_call(
        functools.partial(last_kernel, blocks),
        out_shape=(shaped if kind == F32 else kept)(gr.shape, kind),
        in_specs=vmem(2 + len(weights)),
        out_specs=vmem(1)[0],
        compiler_params=pltpu.CompilerParams(vmem_limit_bytes=6 * MIB),
        cost_estimate=cost(0.01),
        name="last",
    )(*map(near, (back, gr, *weights)))


def settle_kernel(
    pieces_ref, loss_ref, gq_ref, gk_ref, gv_ref, go_ref, g1_ref, g2_ref, g3_ref, inverse_ref
):
    step, feat = gq_ref.shape
    size = feat // HEADS
    width = 3 * size
    totals = jnp.sum(pieces_ref[...].astype(F32), axis=0)
    small = totals[0:8] + totals[8:16]
    sides = totals[step:]
    inverse = 1.0 / small[3:4, width + 1 : width + 2]
    inverse_ref[...] = jnp.broadcast_to(inverse, inverse_ref.shape)
    loss_ref[...] = small[3:4, width : width + 1] * inverse
    go_ref[...] = jnp.concatenate([sides[:step], sides[step:]], axis=1) * inverse
    for h in range(HEADS):
        block = pieces_ref[h, 0:step, :].astype(F32) * inverse
        for part, ref in enumerate((gq_ref, gk_ref, gv_ref)):
            ref[:, h * size : (h + 1) * size] = block[:, part * size : (part + 1) * size]
    for k, ref in enumerate((g1_ref, g2_ref, g3_ref)):
        ref[...] = small[k : k + 1, width : width + step] * inverse


def settle(pieces, feat):
    step = pieces.shape[1] // 3
    return pl.pallas_call(
        settle_kernel,
        out_shape=(
            shaped((1, 1), F32),
            shaped((step, feat), F32),
            shaped((step, feat), F32),
            shaped((step, feat), F32),
            shaped((step, feat), F32),
            shaped((1, step), F32),
            shaped((1, step), F32),
            shaped((1, step), F32),
            kept((8, 128), F32),
        ),
        in_specs=vmem(1),
        out_specs=tuple(vmem(9)),
        compiler_params=pltpu.CompilerParams(vmem_limit_bytes=4 * MIB),
        cost_estimate=pl.CostEstimate(
            flops=5500000000, bytes_accessed=1024, transcendentals=0
        ),
        name="settle",
    )(near(pieces))


def finish_kernel(inverse_ref, gx_in, pair_in, out_ref, gx_ref, gy_ref):
    inverse = inverse_ref[0:1, 0:1]
    tok = out_ref.shape[0]
    out_ref[...] = pair_in[0:tok]
    gx_ref[...] = gx_in[...].astype(F32) * inverse
    gy_ref[...] = pair_in[tok : 2 * tok].astype(F32) * inverse


def finish(inverse, gx, pair):
    tok, feat = gx.shape
    return pl.pallas_call(
        finish_kernel,
        out_shape=(
            shaped((tok, feat), BF16),
            shaped((tok, feat), F32),
            shaped((tok, feat), F32),
        ),
        in_specs=vmem(3),
        out_specs=tuple(vmem(3)),
        compiler_params=pltpu.CompilerParams(vmem_limit_bytes=6 * MIB),
        cost_estimate=cost(1),
        name="finish",
    )(near(inverse), gx, pair)


def spread_kernel(sums_in, inverse_ref, gu_ref, gd_ref, sums_ref, sem):
    (copy,) = fetch([sums_in], [sums_ref], sem)
    wide_step, feat = gd_ref.shape
    step = gu_ref.shape[0]
    copy.wait()
    main = sums_ref[0].astype(F32) * inverse_ref[0:1, 0:1]
    for j in range(gu_ref.shape[1] // feat):
        gu_ref[:, j * feat : (j + 1) * feat] = main[j * step : (j + 1) * step]
    gd_ref[...] = main[main.shape[0] - wide_step :]


def spread(sums, inverse, step, wide):
    feat = sums.shape[2]
    return pl.pallas_call(
        spread_kernel,
        out_shape=(shaped((step, wide), F32), shaped((wide * step // feat, feat), F32)),
        in_specs=hbm(1) + vmem(1),
        out_specs=tuple(vmem(2)),
        scratch_shapes=[pltpu.VMEM(sums.shape, BF16), pltpu.SemaphoreType.DMA((1,))],
        compiler_params=pltpu.CompilerParams(vmem_limit_bytes=4 * MIB),
        cost_estimate=cost(1),
        name="spread",
    )(far(sums), near(inverse))


def body(
    state_x,
    state_y,
    teacher,
    segment_ids,
    valid_mask,
    w_query,
    w_key,
    w_value,
    w_out,
    w_up,
    w_down,
    gain_attn,
    gain_ffn,
    gain_final,
):
    _, tok, feat = state_x.shape
    size = feat // HEADS
    ctx = lax.axis_size("ctx")
    sides = lax.axis_size("dp")
    ways = ctx // HEADS
    groups = [[h * ways + r for h in range(HEADS)] for r in range(ways)]
    side, place = lax.axis_index("dp"), lax.axis_index("ctx")
    wide = w_up.shape[1]
    cross = sides == 2 and ways == 2 and (feat // (sides * ctx)) % 16 == 0
    both = ("dp", "ctx")

    def both_ways(rings):
        return rings + [[ctx + place for place in reversed(ring)] for ring in rings]

    def moved(block):
        if not cross:
            return block
        route = []
        for s in range(2):
            for c in range(ctx):
                route.append((s * ctx + c, (c % 2) * ctx + c - c % 2 + s))
        return lax.ppermute(block, both, route)

    def shared(block):
        if sides == 2:
            return [block, swap(block, "dp", 1)]
        return [lax.all_gather(block, "dp", axis=0, tiled=True)]

    def exchange(block):
        return lax.all_to_all(block, "ctx", 0, 0, axis_index_groups=groups, tiled=True)

    def around(block, distance):
        if cross:
            return swap(block, "dp", 1)
        route = []
        for g in range(HEADS):
            for r in range(ways):
                route.append((g * ways + r, g * ways + (r + distance) % ways))
        return lax.ppermute(block, "ctx", route)

    x = moved(state_x[0])
    attn_weights = [shared(w) for w in (w_query, w_key, w_value)]
    segs = [segment_ids.reshape(ctx, tok)]
    if cross:
        segs.append(swap(segs[0], "dp", 1))
    mask = moved(valid_mask)
    pair = jnp.concatenate([state_y[0], teacher[0]], axis=0)
    qkv = project(x, attn_weights)
    plan = plan_of(segs, ways, ctx, tok)
    qkv = exchange(qkv)
    qkv, plan, mask, late_x, pair = lax.optimization_barrier((qkv, plan, mask, x, pair))
    kvs = [qkv] + [around(qkv, j) for j in range(1, ways)]
    o, of, lse = attend(plan, segs, kvs)
    gains = jnp.stack([gain_attn, gain_ffn, gain_final])
    if sides == 2:
        gains = shared(gains)
    else:
        gains = [lax.all_gather(gains, "dp", axis=1, tiled=True)]
    wo, wu, wd = shared(w_out), shared(w_up), shared(w_down)
    blocks = len(wu)
    o, pair = lax.optimization_barrier((o, moved(pair)))
    ot = exchange(o)
    ot, x_near, wo = lax.optimization_barrier((ot, *stage([x], wo)))
    ot = ot.reshape(feat, tok)
    pair, gr, do, small, *halves = middle(
        ot,
        mask,
        gains,
        x_near,
        pair,
        wo,
        wu,
        wd,
        [ffn_shape(ctx, feat, wide)] * (2 * cross),
    )
    do = do.reshape(HEADS, size, tok)
    if cross:
        rings = both_ways([[h * ways + r for h in RING] for r in range(ways)])
        gathered = lax.all_gather(late_x, both, axis=0, axis_index_groups=rings)
    do = exchange(do)
    if cross:
        sums, sides = join(halves[0], swap(halves[1], "dp", 1), feat // (2 * ctx))
        lse, sums = lax.optimization_barrier((lse, sums))
        kx, qx = prepare(segs, lse, kvs)
        do, kx, qx, sums, gathered = lax.optimization_barrier((do, kx, qx, sums, gathered))
        inner = both_ways([[4 * z + k for k in INNER] for z in range(4)])
        outer = both_ways([[4 * z + k for z in OUTER] for k in range(4)])
        sums = lax.psum_scatter(
            sums, both, scatter_dimension=0, axis_index_groups=inner, tiled=True
        )
    else:
        kx, qx = prepare(segs, lse, kvs)
    back_args = (plan, kx, qx, do, qkv)
    part, dx, *others = attend_back(
        *back_args, kvs[1:], ways, len(segs), tuple(range(1, ways)), of=of
    )
    others = [around(other, -(j + 1)) for j, other in enumerate(others)]
    dq, own = attend_back(
        *back_args, kvs[:1], ways, len(segs), (0,), part=part, dx=dx
    )
    sent = pack(dq, own, others)
    back = exchange(sent)
    back, *staged = lax.optimization_barrier((back, *stage([gr], *attn_weights)))
    if cross:
        mine, away = head_grads(ctx, sent, gathered, small)
        mine, away = halve(3 * size, mine, swap(away, "dp", 1), sides)
        pieces = merge(3 * size, mine, swap(away, "ctx", 1))
        pieces, sums, pair = lax.optimization_barrier((pieces, sums, pair))
        pair = moved(pair)
        sums = lax.psum_scatter(
            sums, both, scatter_dimension=0, axis_index_groups=outer, tiled=True
        )
        pieces = exchange(pieces)
        gx = moved(last(blocks, back, staged[0], staged[1:], BF16))
        loss, gq, gk, gv, go, g1, g2, g3, inverse = settle(pieces, feat)
        result, gx, gy = finish(inverse, gx, pair)
        gu, gd = spread(sums, inverse, gq.shape[0], wide)
        gains_out = [g.reshape(-1) for g in (g1, g2, g3)]
        loss = loss.reshape(())
    else:
        x1, h, df, dz, da = halves
        result, gy = pair[:tok], pair[tok:].astype(F32)
        total = lax.psum(small, both)
        inverse = 1.0 / total[3, 1]
        loss = total[3, 0] * inverse

        def scattered(block):
            block = block * inverse
            return lax.psum_scatter(block, both, scatter_dimension=0, tiled=True)

        gx = last(blocks, back, staged[0], staged[1:], F32)
        parts = [back[:, j * size : (j + 1) * size, :].reshape(feat, tok) for j in range(3)]
        gq, gk, gv = [scattered(dot_t(x.T, part)) for part in parts]
        go = scattered(dot(ot, da))
        gu = scattered(dot(x1.T, dz))
        gd = scattered(dot(h.T, df))
        gx, gy = gx * inverse, gy * inverse
        step = feat // (sides * ctx)
        number = side * ctx + place
        gains_out = [
            lax.dynamic_slice_in_dim(
                jnp.concatenate([total[k], total[k + 4]]) * inverse, number * step, step
            )
            for k in range(3)
        ]
    return (
        loss,
        result[None],
        gx[None],
        gy[None],
        gq,
        gk,
        gv,
        go,
        gu,
        gd,
        gains_out[0],
        gains_out[1],
        gains_out[2],
    )


def solution(mesh):
    tokens = P("dp", "ctx", None)
    rows = P("dp", None)
    spread = P(("dp", "ctx"), None)
    gain = P(("dp", "ctx"))
    return jax.shard_map(
        body,
        mesh=mesh,
        in_specs=(tokens,) * 3 + (rows, P("dp", "ctx")) + (rows,) * 6 + (P("dp"),) * 3,
        out_specs=(P(), tokens, tokens, tokens) + (spread,) * 6 + (gain,) * 3,
        check_vma=False,
    )
```
